512 devices in a mesh: dp: 4 (over x), row: 32 (over z_lo, y), col: 4 (over z_hi, core).
Axes of the slice: x: 4, y: 4, z: 16 (z_hi: 2, z_lo: 8; z = z_hi * 8 + z_lo), core: 2. Of those that a mesh axis runs over, the one named last changes fastest.
Arguments:
- hidden_in: bfloat16 [4, 256, 128, 256], P('dp', 'row', 'col'), may hold values from -6 to 6
- token_ids: int32 [4, 256, 128], P('dp', 'row', 'col'), may hold values from 0 to 3
- embed: bfloat16 [4, 256], replicated, may hold values from -4 to 4
- norm1_gain: float32 [256], replicated, may hold values from 0.1 to 1.9
- norm2_gain: float32 [256], replicated, may hold values from 0.1 to 1.9
- w_qkv: bfloat16 [256, 768], replicated, may hold values from -0.375 to 0.375
- rel_bias: float32 [8, 225], replicated, may hold values from -3 to 3
- w_proj: bfloat16 [256, 256], replicated, may hold values from -0.375 to 0.375
- w_up: bfloat16 [256, 1024], replicated, may hold values from -0.375 to 0.375
- w_down: bfloat16 [1024, 256], replicated, may hold values from -0.1875 to 0.1875
- out_grad: bfloat16 [4, 256, 128, 256], P('dp', 'row', 'col'), may hold values from -6 to 6
Outputs:
- in_grad: bfloat16 [4, 256, 128, 256], P('dp', 'row', 'col')
- attention_grads: float32 [2048, 128], P(('dp', 'row', 'col'))
- mlp_grads: float32 [4096, 128], P(('dp', 'row', 'col'))
The draws below stay inside these ranges and needn't reach their ends.
All inputs are finite; a program needn't handle non-finite values.
Results may differ from the reference program's by a relative error of at most 0.0079.
Values may be sent and summed in bfloat16 or wider, within the bound.
A program may use at most 64 MiB of HBM per device.

```python
import jax
import jax.numpy as jnp
from jax import lax

D = 256
FF = 1024
HEADS = 8
VOCAB = 4
WIN = 8
HEAD_DIM = 32
SHIFT = 4
PAIRS = 225
SHOTS = 4
ROWS = 256
COLS = 128


def plant(drawn, own_key, least, high):
    longest = drawn.shape.index(max(drawn.shape))
    spots = []
    for shift in (0, 1):
        where = [jax.random.randint(jax.random.fold_in(own_key, axis), (), 0, length) for axis, length in enumerate(drawn.shape)]
        where[longest] = (where[longest] + shift) % drawn.shape[longest]
        spots.append(tuple(where))
    return drawn.at[spots[0]].set(least).at[spots[1]].set(high)


def block_scale(rng, dims, cuts, smallest, high):
    gain, own = 1.0, jax.random.fold_in(rng, 6)
    for position, blocks in cuts:
        steps = jnp.exp(jax.random.uniform(jax.random.fold_in(own, position), (blocks,), jnp.float32, smallest / len(cuts), high / len(cuts)))
        gain = gain * jnp.repeat(steps, dims[position] // blocks).reshape([-1 if axis == position else 1 for axis in range(len(dims))])
    return gain


def normal_values(stream_key, shape, scale, bound, split=(), kind=jnp.bfloat16):
    factor_of = block_scale(stream_key, shape, split, -0.22, 0.18) if split else 1.0
    entries = jax.random.normal(stream_key, shape, jnp.float32) * scale * factor_of
    return jnp.minimum(jnp.maximum(entries, -bound), bound).astype(kind)


def setup_inputs(seed: int = 0) -> dict:
    key_list = jax.random.split(jax.random.key(seed), 12)
    hidden_in = normal_values(key_list[0], (SHOTS, ROWS, COLS, D), 1.0, 6.0, ((0, 4), (1, 32), (2, 4)))
    token_ids = plant(jax.random.randint(key_list[1], (SHOTS, ROWS, COLS), 0, VOCAB), jax.random.fold_in(key_list[1], 1), 0, VOCAB - 1).astype(jnp.int32)
    embed = normal_values(key_list[2], (VOCAB, D), 1.0, 4.0)
    norm1_gain = jnp.clip(1.0 + 0.18 * jax.random.normal(key_list[3], (D,), jnp.float32), 0.1, 1.9)
    norm2_gain = jnp.clip(1.0 + 0.18 * jax.random.normal(key_list[4], (D,), jnp.float32), 0.1, 1.9)
    w_qkv = normal_values(key_list[5], (D, 3 * D), D ** -0.5, 0.375)
    rel_bias = normal_values(key_list[6], (HEADS, PAIRS), 1.0, 3.0, (), jnp.float32)
    w_proj = normal_values(key_list[7], (D, D), D ** -0.5, 0.375)
    w_up = normal_values(key_list[8], (D, FF), D ** -0.5, 0.375)
    w_down = normal_values(key_list[9], (FF, D), FF ** -0.5, 0.1875)
    out_grad = normal_values(key_list[10], (SHOTS, ROWS, COLS, D), 1.0, 6.0, ((0, 4), (1, 32), (2, 4)))
    return dict(hidden_in=hidden_in, token_ids=token_ids, embed=embed, norm1_gain=norm1_gain, norm2_gain=norm2_gain, w_qkv=w_qkv, rel_bias=rel_bias, w_proj=w_proj, w_up=w_up, w_down=w_down, out_grad=out_grad)


NORM_EPS = 1e-05
GELU_SCALE = 0.7978845608028654
GELU_CUBIC = 0.044715

def layer_norm(values, gain_vec):
    center = values - lax.optimization_barrier(jnp.mean(values, axis=-1, keepdims=True))
    inv_std = lax.rsqrt(lax.optimization_barrier(jnp.mean(center * center, axis=-1, keepdims=True)) + NORM_EPS)
    normed = center * inv_std
    return (normed, inv_std, normed * gain_vec)

def norm_back(upstream, normed, inv_std, gain_vec):
    scaled = upstream * gain_vec
    return inv_std * (scaled - lax.optimization_barrier(jnp.mean(scaled, axis=-1, keepdims=True)) - normed * lax.optimization_barrier(jnp.mean(scaled * normed, axis=-1, keepdims=True)))

def gelu_value(pre_act):
    inner_arg = GELU_SCALE * (pre_act + GELU_CUBIC * pre_act * pre_act * pre_act)
    return 0.5 * pre_act * (1.0 + jnp.tanh(inner_arg))

def gelu_slope(pre_act):
    tanh_part = jnp.tanh(GELU_SCALE * (pre_act + GELU_CUBIC * pre_act * pre_act * pre_act))
    return 0.5 * (1.0 + tanh_part) + 0.5 * pre_act * (1.0 - tanh_part * tanh_part) * GELU_SCALE * (1.0 + 3.0 * GELU_CUBIC * pre_act * pre_act)

def to_windows(grid_map):
    shot_count, height, breadth, channels = grid_map.shape
    blocks = grid_map.reshape(shot_count, height // WIN, WIN, breadth // WIN, WIN, channels)
    return blocks.transpose(0, 1, 3, 2, 4, 5).reshape(-1, WIN * WIN, channels)

def from_windows(window_rows, shot_count, height, breadth):
    channels = window_rows.shape[-1]
    blocks = window_rows.reshape(shot_count, height // WIN, breadth // WIN, WIN, WIN, channels)
    return blocks.transpose(0, 1, 3, 2, 4, 5).reshape(shot_count, height, breadth, channels)

def split_heads(window_rows, first_col):
    window_count = window_rows.shape[0]
    return window_rows[:, :, first_col:first_col + D].reshape(window_count, WIN * WIN, HEADS, HEAD_DIM).astype(jnp.float32)

def position_bias(rel_bias):
    cell_ids = jnp.arange(WIN * WIN)
    cell_row = cell_ids // WIN
    cell_col = cell_ids % WIN
    offset = (cell_row[:, None] - cell_row[None, :] + WIN - 1) * (2 * WIN - 1) + (cell_col[:, None] - cell_col[None, :] + WIN - 1)
    return rel_bias[:, offset.astype(jnp.int32)]

def attend(tile_grid, w_qkv, bias_full):
    shot_count, height, breadth, channels = tile_grid.shape
    mixed_rows = jnp.dot(tile_grid.reshape(-1, channels), w_qkv, preferred_element_type=jnp.float32).astype(jnp.bfloat16)
    window_rows = to_windows(mixed_rows.reshape(shot_count, height, breadth, 3 * channels))
    queries = split_heads(window_rows, 0)
    key_rows = split_heads(window_rows, D)
    value_rows = split_heads(window_rows, 2 * D)
    scale_factor = HEAD_DIM ** (-0.5)
    scores = jnp.einsum('wihd,wjhd->whij', queries, key_rows) * scale_factor + bias_full[None]
    raised = jnp.exp(scores)
    soft_probs = raised / lax.optimization_barrier(jnp.sum(raised, axis=-1, keepdims=True))
    probs_low = soft_probs.astype(jnp.bfloat16)
    context = jnp.einsum('whij,wjhd->wihd', probs_low.astype(jnp.float32), value_rows)
    context = context.reshape(-1, WIN * WIN, D).astype(jnp.bfloat16)
    return (from_windows(context, shot_count, height, breadth), (queries, key_rows, value_rows, soft_probs, probs_low))

def attend_back(grad_grid, saved_state):
    shot_count, height, breadth, channels = grad_grid.shape
    queries, key_rows, value_rows, soft_probs, probs_low = saved_state
    grad_heads = to_windows(grad_grid).reshape(-1, WIN * WIN, HEADS, HEAD_DIM).astype(jnp.float32)
    grad_dots = jnp.einsum('wihd,wjhd->whij', grad_heads, value_rows)
    grad_values = jnp.einsum('whij,wihd->wjhd', probs_low.astype(jnp.float32), grad_heads)
    grad_scores = soft_probs * (grad_dots - lax.optimization_barrier(jnp.sum(soft_probs * grad_dots, axis=-1, keepdims=True)))
    scores_low = grad_scores.astype(jnp.bfloat16).astype(jnp.float32)
    scale_factor = HEAD_DIM ** (-0.5)
    grad_queries = jnp.einsum('whij,wjhd->wihd', scores_low, key_rows) * scale_factor
    grad_keys = jnp.einsum('whij,wihd->wjhd', scores_low, queries) * scale_factor
    window_count = grad_heads.shape[0]
    joined = jnp.concatenate([grad_queries.reshape(window_count, WIN * WIN, D), grad_keys.reshape(window_count, WIN * WIN, D), grad_values.reshape(window_count, WIN * WIN, D)], axis=-1).astype(jnp.bfloat16)
    return from_windows(joined, shot_count, height, breadth)

def reference(hidden_in, token_ids, embed, norm1_gain, norm2_gain, w_qkv, rel_bias, w_proj, w_up, w_down, out_grad):
    bias_full = position_bias(rel_bias)
    cell_count = ROWS * COLS

    def one_shot(totals, shot_inputs):
        hidden_shot, ids_shot, grad_shot = shot_inputs
        resid_in = hidden_shot.reshape(cell_count, D).astype(jnp.float32) + embed.astype(jnp.float32)[ids_shot.reshape(-1)]
        normed_one, inv_one, scaled_one = layer_norm(resid_in, norm1_gain)
        normal_low = scaled_one.astype(jnp.bfloat16)
        grid_low = normal_low.reshape(1, ROWS, COLS, D)
        shifted = jnp.roll(grid_low, (-SHIFT, -SHIFT), axis=(1, 2))
        context_tile, saved_state = attend(shifted, w_qkv, bias_full)
        context = jnp.roll(context_tile, (SHIFT, SHIFT), axis=(1, 2)).reshape(cell_count, D)
        resid_mid = resid_in + jnp.dot(context, w_proj, preferred_element_type=jnp.float32)
        normed_two, inv_two, scaled_two = layer_norm(resid_mid, norm2_gain)
        mlp_in = scaled_two.astype(jnp.bfloat16)
        pre_act = jnp.dot(mlp_in, w_up, preferred_element_type=jnp.float32)
        activation = gelu_value(pre_act).astype(jnp.bfloat16)
        grad_flat = grad_shot.reshape(cell_count, D)
        grad_act = jnp.dot(grad_flat, w_down.T, preferred_element_type=jnp.float32)
        grad_pre = (grad_act * gelu_slope(pre_act)).astype(jnp.bfloat16)
        up_grad = jnp.dot(mlp_in.T, grad_pre, preferred_element_type=jnp.float32)
        down_grad = jnp.dot(activation.T, grad_flat, preferred_element_type=jnp.float32)
        grad_mid = jnp.dot(grad_pre, w_up.T, preferred_element_type=jnp.float32)
        grad_res = grad_flat.astype(jnp.float32) + norm_back(grad_mid, normed_two, inv_two, norm2_gain)
        grad_res_low = grad_res.astype(jnp.bfloat16)
        proj_grad = jnp.dot(context.T, grad_res_low, preferred_element_type=jnp.float32)
        grad_context = jnp.dot(grad_res_low, w_proj.T, preferred_element_type=jnp.float32).astype(jnp.bfloat16)
        grad_grid = jnp.roll(grad_context.reshape(1, ROWS, COLS, D), (-SHIFT, -SHIFT), axis=(1, 2))
        grad_mixed = jnp.roll(attend_back(grad_grid, saved_state), (SHIFT, SHIFT), axis=(1, 2)).reshape(cell_count, 3 * D)
        qkv_grad = jnp.dot(normal_low.T, grad_mixed, preferred_element_type=jnp.float32)
        grad_norm_in = jnp.dot(grad_mixed, w_qkv.T, preferred_element_type=jnp.float32)
        grad_in = grad_res + norm_back(grad_norm_in, normed_one, inv_one, norm1_gain)
        new_totals = (totals[0] + qkv_grad, totals[1] + proj_grad, totals[2] + up_grad, totals[3] + down_grad)
        return (new_totals, grad_in.astype(jnp.bfloat16).reshape(ROWS, COLS, D))
    start_totals = (jnp.zeros((D, 3 * D), jnp.float32), jnp.zeros((D, D), jnp.float32), jnp.zeros((D, FF), jnp.float32), jnp.zeros((FF, D), jnp.float32))
    totals, in_grad = lax.scan(one_shot, start_totals, (hidden_in, token_ids, out_grad))
    attention_grads = jnp.concatenate([totals[0].reshape(-1), totals[1].reshape(-1)]).reshape(-1, 128)
    mlp_grads = jnp.concatenate([totals[2].reshape(-1), totals[3].reshape(-1)]).reshape(-1, 128)
    return (in_grad, attention_grads, mlp_grads)
```

```python
import jax
import jax.numpy as jnp
from jax import lax
from jax.experimental import pallas as pl
from jax.experimental.pallas import tpu as pltpu
from jax.sharding import PartitionSpec as P

D = 256
FF = 1024
HEADS = 8
HEAD_DIM = 32
WIN = 8
PAIRS = 225
CELLS = 256
NORM_EPS = 1e-05
GELU_SCALE = 0.7978845608028654
GELU_CUBIC = 0.044715
SCALE = HEAD_DIM ** (-0.5)

NX, NY, NZ_LO, NZ_HI = 4, 4, 8, 2
NZ = NZ_LO * NZ_HI
ROW_DEVICES, COL_DEVICES = NZ_LO * NY, NZ_HI * 2
MLP_UNIT, ATT_UNIT = 16, 8

MESH = pl.DeviceIdType.MESH
BF = jnp.bfloat16
F32 = jnp.float32


def iota(shape, dim):
    return lax.broadcasted_iota(jnp.int32, shape, dim)


def one_hot(condition):
    return jnp.where(condition, 1.0, 0.0).astype(BF)


def dot(left, right):
    return jnp.dot(left, right, preferred_element_type=F32)


def dot_nt(left, right):
    return lax.dot_general(left, right, (((1,), (1,)), ((), ())), preferred_element_type=F32)


def dot_tn(left, right):
    return lax.dot_general(left, right, (((0,), (0,)), ((), ())), preferred_element_type=F32)


def mean_of(values):
    return jnp.mean(values, axis=-1, keepdims=True)


def layer_norm(values):
    center = values - mean_of(values)
    inv_std = lax.rsqrt(mean_of(center * center) + NORM_EPS)
    return center * inv_std, inv_std


def norm_back(upstream, normed, inv_std, gain):
    scaled = upstream * gain
    return inv_std * (scaled - mean_of(scaled) - normed * mean_of(scaled * normed))


def window_cell(token):
    return token & 7, ((token >> 6) << 3) + ((token >> 3) & 7)


def block_sum(values, ones_pair):
    high = values.astype(BF)
    low = (values - high.astype(F32)).astype(BF)
    parts = []
    for j in range(4):
        lanes = slice(128 * j, 128 * (j + 1))
        parts.append(dot(jnp.concatenate([high[:, lanes], low[:, lanes]], axis=1), ones_pair))
    return jnp.concatenate(parts, axis=1)


def kernel(
    hid_ref, tok_ref, emb_ref, g1_ref, g2_ref, wqkv_ref, rb_ref, wproj_ref, wup_ref, wdown_ref, og_ref,
    out_ref, att_ref, mlp_ref,
    stage, halo_hid, halo_og, halo_rd, halo_tok,
    bias_s, probs_s, ke_s, ve_s, qkv_s, ctx_s, g_s, df_s, dqkv_s, back_main, back_rd, got_up, got_rd,
    mlp_f32, mlp_send, mlp_recv, mlp_x, mlp_y, mlp_rx, mlp_ry, mlp_x3, mlp_y3, mlp_rx3, mlp_ry3,
    mlp_z, mlp_rz, mlp_c, mlp_rc,
    att_f32, att_send, att_recv, att_x, att_y, att_rx, att_ry, att_x3, att_y3, att_rx3, att_ry3,
    att_z, att_rz, att_c, att_rc,
    halo_ss, halo_rs, back_ss, back_rs, mlp_ss, mlp_rs, att_ss, att_rs, mlp_zs, mlp_zr, att_zs, att_zr,
):
    x_at, row, col = lax.axis_index("dp"), lax.axis_index("row"), lax.axis_index("col")
    z_lo, y_at = row // NY, row % NY
    z_hi, core = col // 2, col % 2
    z_at = z_hi * NZ_LO + z_lo
    mate = 1 - core

    above = (row + ROW_DEVICES - 1) % ROW_DEVICES
    below = (row + 1) % ROW_DEVICES
    left = (col + COL_DEVICES - 1) % COL_DEVICES
    right = (col + 1) % COL_DEVICES

    def at_mate():
        return (x_at, row, z_hi * 2 + mate)

    def at_x(other):
        return (other, row, col)

    def at_y(other):
        return (x_at, z_lo * NY + other, col)

    def at_z(other):
        return (x_at, (other % NZ_LO) * NY + y_at, (other // NZ_LO) * 2 + core)

    partners = [at_mate()]
    partners += [at_x((x_at + d) % NX) for d in range(1, NX)]
    partners += [at_y((y_at + d) % NY) for d in range(1, NY)]
    partners += [at_z((z_at + d) % NZ) for d in range(1, NZ)]
    partners += [(x_at, above, col), (x_at, below, col), (x_at, row, left), (x_at, row, right)]
    partners += [(x_at, above, left), (x_at, below, right)]
    barrier = pltpu.get_barrier_semaphore()
    for partner in partners:
        pl.semaphore_signal(barrier, inc=1, device_id=partner, device_id_type=MESH)

    def send(src, dst, send_sem, recv_sem, device):
        copy = pltpu.make_async_remote_copy(
            src_ref=src, dst_ref=dst, send_sem=send_sem, recv_sem=recv_sem,
            device_id=device, device_id_type=MESH,
        )
        copy.start()
        return copy

    r32, s256 = iota((32, CELLS), 0), iota((32, CELLS), 1)
    stage_row = jnp.where(r32 < 16, 4, 0) + ((r32 & 15) >> 2)
    pick = one_hot(s256 == stage_row * 32 + (r32 & 3))
    stage[:, :D] = dot(pick, hid_ref[...]).astype(BF)
    stage[:, D:] = dot(pick, og_ref[...]).astype(BF)

    pl.semaphore_wait(barrier, len(partners))

    to_above, to_left, to_corner = (x_at, above, col), (x_at, row, left), (x_at, above, left)
    halo = []
    for n, (src, dst, device) in enumerate([
        (tok_ref, halo_tok.at[0], to_above),
        (tok_ref, halo_tok.at[1], to_left),
        (tok_ref, halo_tok.at[2], to_corner),
        (stage.at[pl.ds(0, 16)], halo_rd.at[pl.ds(0, 16)], to_left),
        (stage.at[pl.ds(16, 16)], halo_rd.at[pl.ds(16, 16)], to_corner),
        (hid_ref.at[pl.ds(0, 128)], halo_hid, to_above),
        (og_ref.at[pl.ds(0, 128)], halo_og, to_above),
    ]):
        halo.append(send(src, dst, halo_ss.at[n], halo_rs.at[n], device))

    wide_row, wide_lane = iota((128, 512), 0), iota((128, 512), 1)
    pair_sum = jnp.where(
        (wide_row >> 4) == (wide_lane >> 6), (wide_row & 15) + ((wide_lane >> 3) & 7), -1
    )
    rb = rb_ref[...]
    rb_high = rb.astype(BF)
    rb_rest = rb - rb_high.astype(F32)
    rb_mid = rb_rest.astype(BF)
    rb_low = (rb_rest - rb_mid.astype(F32)).astype(BF)
    rb_parts = jnp.concatenate([rb_high, rb_mid, rb_low], axis=0)
    key_row = iota((8, 512), 1) & 7
    for qj in range(8):
        tall = dot(rb_parts, one_hot(pair_sum == qj + 7))
        tall = tall[0:16] + tall[16:32] + tall[32:48]
        rows = jnp.zeros((8, 512), F32)
        for ki in range(8):
            rows = jnp.where(key_row == ki, tall[7 - ki : 15 - ki], rows)
        bias_s[8 * qj : 8 * qj + 8, :] = rows

    t_row, t_col = window_cell(iota((CELLS, CELLS), 0))
    s_lane = iota((CELLS, CELLS), 1)
    pick_main = one_hot((t_col < 28) & (s_lane == 32 * t_row + t_col + 4))
    e_row, e_col = window_cell(iota((CELLS, 32), 0))
    pick_edge = one_hot((e_col >= 28) & (iota((CELLS, 32), 1) == 4 * e_row + e_col - 28))

    for n in range(6):
        halo[n].wait_recv()
    tok = tok_ref[...]
    tok_below, tok_right, tok_corner = halo_tok[0], halo_tok[1], halo_tok[2]
    tok_main = jnp.concatenate(
        [tok[4 + i : 5 + i, :] for i in range(4)] + [tok_below[i : i + 1, :] for i in range(4)], axis=1
    )
    tok_edge = jnp.concatenate(
        [tok_right[4 + i : 5 + i, 0:4] for i in range(4)] + [tok_corner[i : i + 1, 0:4] for i in range(4)],
        axis=1,
    )
    tok_main = jnp.broadcast_to(tok_main.astype(F32), (128, CELLS)).astype(BF)
    tok_edge = jnp.broadcast_to(tok_edge.astype(F32), (128, 32)).astype(BF)
    ids = dot_nt(pick_main, tok_main) + dot_nt(pick_edge, tok_edge)
    ids = jnp.concatenate([ids, ids], axis=1)
    emb = emb_ref[...].astype(F32)
    token_part = jnp.where(
        ids < 1.5,
        jnp.where(ids < 0.5, emb[0:1], emb[1:2]),
        jnp.where(ids < 2.5, emb[2:3], emb[3:4]),
    )
    main_hid = jnp.concatenate([hid_ref[128:256, :], halo_hid[...]], axis=0)
    resid_in = dot(pick_main, main_hid) + dot(pick_edge, halo_rd[:, :D]) + token_part
    normed_one, inv_one = layer_norm(resid_in)
    gain_one = g1_ref[...]
    normal_low = (normed_one * gain_one).astype(BF)

    qkv_s[...] = dot(normal_low, wqkv_ref[...]).astype(BF)

    head_mask = one_hot((iota((512, D), 0) >> 6) == (iota((512, D), 1) >> 5))
    ones_pair = one_hot(((iota((256, 128), 0) & 127) >> 6) == (iota((256, 128), 1) >> 6))
    for w in range(4):
        cells = slice(64 * w, 64 * w + 64)
        keys = jnp.concatenate([qkv_s[cells, D : 2 * D]] * HEADS, axis=0) * head_mask
        ke_s[w] = keys
        ve_s[w] = jnp.concatenate([qkv_s[cells, 2 * D :]] * HEADS, axis=0) * head_mask
        probs_s[cells, :] = jnp.exp(dot_nt(qkv_s[cells, :D], keys) * SCALE + bias_s[...])
    raised = probs_s[...]
    probs = raised / block_sum(raised, ones_pair)
    probs_s[...] = probs
    probs_low = probs.astype(BF)
    for w in range(4):
        cells = slice(64 * w, 64 * w + 64)
        ctx_s[cells, :] = dot(probs_low[cells], ve_s[w]).astype(BF)

    context = ctx_s[...]
    resid_mid = resid_in + dot(context, wproj_ref[...])
    normed_two, inv_two = layer_norm(resid_mid)
    gain_two = g2_ref[...]
    mlp_in = (normed_two * gain_two).astype(BF)

    halo[6].wait_recv()
    main_og = jnp.concatenate([og_ref[128:256, :], halo_og[...]], axis=0)
    grad_f32 = dot(pick_main, main_og) + dot(pick_edge, halo_rd[:, D:])
    grad = grad_f32.astype(BF)

    grad_mid = jnp.zeros((CELLS, D), F32)
    for n in range(4):
        units = slice(256 * n, 256 * n + 256)
        pre = dot(mlp_in, wup_ref[:, units])
        grad_act = dot_nt(grad, wdown_ref[units, :])
        square = pre * pre
        tanh_part = jnp.tanh(GELU_SCALE * pre * (1.0 + GELU_CUBIC * square))
        half_plus = 0.5 * (1.0 + tanh_part)
        slope = half_plus + 0.5 * pre * (1.0 - tanh_part * tanh_part) * (
            GELU_SCALE * (1.0 + 3.0 * GELU_CUBIC * square)
        )
        act = (pre * half_plus).astype(BF)
        grad_pre = (grad_act * slope).astype(BF)
        grad_mid = grad_mid + dot_nt(grad_pre, wup_ref[:, units])
        up_grad = dot_tn(mlp_in, grad_pre)
        half, lane_tile = n // 2, 2 * (n % 2)
        mlp_f32[half, pl.ds(lane_tile, 256, stride=4), :] = up_grad[:, :128]
        mlp_f32[half, pl.ds(lane_tile + 1, 256, stride=4), :] = up_grad[:, 128:]
        down_grad = dot_tn(act, grad)
        mlp_f32[0, 1024 + 256 * n : 1280 + 256 * n, :] = down_grad[:, :128]
        mlp_f32[1, 1024 + 256 * n : 1280 + 256 * n, :] = down_grad[:, 128:]

    mlp = dict(
        unit=MLP_UNIT, f32=mlp_f32, send=mlp_send, recv=mlp_recv, x=mlp_x, y=mlp_y, rx=mlp_rx, ry=mlp_ry,
        x3=mlp_x3, y3=mlp_y3, rx3=mlp_rx3, ry3=mlp_ry3, z=mlp_z, rz=mlp_rz, c=mlp_c, rc=mlp_rc,
        ss=mlp_ss, rs=mlp_rs, zs=mlp_zs, zr=mlp_zr,
    )
    att = dict(
        unit=ATT_UNIT, f32=att_f32, send=att_send, recv=att_recv, x=att_x, y=att_y, rx=att_rx, ry=att_ry,
        x3=att_x3, y3=att_y3, rx3=att_rx3, ry3=att_ry3, z=att_z, rz=att_rz, c=att_c, rc=att_rc,
        ss=att_ss, rs=att_rs, zs=att_zs, zr=att_zr,
    )
    sends = []

    def start_mate(b):
        b["send"][...] = b["f32"][mate].astype(BF)
        b["p1"] = [send(b["send"], b["recv"], b["ss"].at[0], b["rs"].at[0], at_mate())]
        sends.extend(b["p1"])

    def start_xy(b):
        b["p1"][0].wait_recv()
        unit = b["unit"]
        part = NZ_LO // 2 * NY * unit
        for x in range(NX):
            first, second = slice(2 * part * x, 2 * part * x + part), slice(2 * part * x + part, 2 * part * (x + 1))
            total = b["f32"][core, first, :] + b["recv"][first, :].astype(F32)
            b["x"][x] = total.astype(BF)
            total = b["f32"][core, second, :] + b["recv"][second, :].astype(F32)
            total = total.reshape(NZ_LO // 2, NY, unit, 128)
            quarter = part // NY
            for y in range(NY):
                b["y"][y, quarter * x : quarter * (x + 1), :] = total[:, y].reshape(quarter, 128).astype(BF)
        b["p2"] = []
        for d in range(1, NX):
            other = (x_at + d) % NX
            b["p2"].append(
                send(b["x"].at[other], b["rx"].at[d - 1], b["ss"].at[d], b["rs"].at[d], at_x(other))
            )
            other = (y_at + d) % NY
            b["p2"].append(
                send(b["y"].at[other], b["ry"].at[d - 1], b["ss"].at[3 + d], b["rs"].at[3 + d], at_y(other))
            )
        sends.extend(b["p2"])

    def start_yx(b):
        for copy in b["p2"]:
            copy.wait_recv()
        unit = b["unit"]
        quarter = NZ_LO // 2 * unit
        total = b["x"][x_at].astype(F32)
        for d in range(NX - 1):
            total = total + b["rx"][d].astype(F32)
        total = total.reshape(NZ_LO // 2, NY, unit, 128)
        for y in range(NY):
            b["x3"][y] = total[:, y].reshape(quarter, 128).astype(BF)
        total = b["y"][y_at].astype(F32)
        for d in range(NY - 1):
            total = total + b["ry"][d].astype(F32)
        for x in range(NX):
            b["y3"][x] = total[quarter * x : quarter * (x + 1)].astype(BF)
        b["p3"] = []
        for d in range(1, NX):
            other = (y_at + d) % NY
            b["p3"].append(
                send(b["x3"].at[other], b["rx3"].at[d - 1], b["ss"].at[6 + d], b["rs"].at[6 + d], at_y(other))
            )
            other = (x_at + d) % NX
            b["p3"].append(
                send(b["y3"].at[other], b["ry3"].at[d - 1], b["ss"].at[9 + d], b["rs"].at[9 + d], at_x(other))
            )
        sends.extend(b["p3"])

    def start_z(b):
        for copy in b["p3"]:
            copy.wait_recv()
        unit = b["unit"]
        for part, own, own_at, got in ((0, b["x3"], y_at, b["rx3"]), (1, b["y3"], x_at, b["ry3"])):
            total = own[own_at].astype(F32)
            for d in range(NX - 1):
                total = total + got[d].astype(F32)
            piece = unit // 2
            for lo in range(NZ_LO // 2):
                for hi in range(NZ_HI):
                    start = lo * unit + hi * piece
                    b["z"][part * (NZ_LO // 2) + lo, hi] = total[start : start + piece]
        b["p4"] = []
        for d in range(1, NZ):
            other = (z_at + d) % NZ
            b["p4"].append(
                send(
                    b["z"].at[other % NZ_LO, other // NZ_LO], b["rz"].at[d - 1],
                    b["zs"].at[d - 1], b["zr"].at[d - 1], at_z(other),
                )
            )
        sends.extend(b["p4"])

    def start_last(b):
        for copy in b["p4"]:
            copy.wait_recv()
        total = b["z"][z_lo, z_hi]
        for d in range(NZ - 1):
            total = total + b["rz"][d]
        rows = b["unit"] // 4
        b["c"][0] = total[:rows]
        b["c"][1] = total[rows:]
        b["p5"] = [send(b["c"].at[mate], b["rc"], b["ss"].at[13], b["rs"].at[13], at_mate())]
        sends.extend(b["p5"])

    def finish(b):
        b["p5"][0].wait_recv()
        own, got = b["c"][core], b["rc"][...]
        return jnp.where(core == 0, own, got), jnp.where(core == 0, got, own)

    start_mate(mlp)

    grad_res = grad_f32 + norm_back(grad_mid, normed_two, inv_two, gain_two)
    grad_res_low = grad_res.astype(BF)
    proj_grad = dot_tn(context, grad_res_low)
    att_f32[0, 768:, :] = proj_grad[:, :128]
    att_f32[1, 768:, :] = proj_grad[:, 128:]
    grad_context = dot_nt(grad_res_low, wproj_ref[...]).astype(BF)

    start_xy(mlp)

    grad_probs = jnp.concatenate(
        [dot_nt(grad_context[64 * w : 64 * w + 64], ve_s[w]) for w in range(4)], axis=0
    )
    probs = probs_s[...]
    grad_scores = probs * (grad_probs - block_sum(probs * grad_probs, ones_pair))
    scores_low = grad_scores.astype(BF)
    probs_low = probs.astype(BF)

    start_yx(mlp)

    head_of_lane = iota((64, D), 1) >> 5

    def own_heads(stacked):
        result = jnp.zeros((64, D), F32)
        for h in range(HEADS):
            result = jnp.where(head_of_lane == h, stacked[64 * h : 64 * h + 64], result)
        return result

    for w in range(4):
        cells = slice(64 * w, 64 * w + 64)
        dqkv_s[cells, :D] = (dot(scores_low[cells], ke_s[w]) * SCALE).astype(BF)
        dqkv_s[cells, D : 2 * D] = (own_heads(dot_tn(scores_low[cells], qkv_s[cells, :D])) * SCALE).astype(BF)
        dqkv_s[cells, 2 * D :] = own_heads(dot_tn(probs_low[cells], grad_context[cells])).astype(BF)

    start_z(mlp)

    for m in range(3):
        part_grad = dot_tn(normal_low, dqkv_s[:, D * m : D * (m + 1)])
        att_f32[0, pl.ds(m, 256, stride=3), :] = part_grad[:, :128]
        att_f32[1, pl.ds(m, 256, stride=3), :] = part_grad[:, 128:]
    start_mate(att)

    grad_norm_in = dot_nt(dqkv_s[...], wqkv_ref[...])
    grad_in = (grad_res + norm_back(grad_norm_in, normed_one, inv_one, gain_one)).astype(BF)
    u_row, u_col = window_cell(iota((CELLS, CELLS), 1))
    place_main = one_hot((u_col < 28) & (iota((CELLS, CELLS), 0) == 32 * u_row + u_col + 4))
    v_row, v_col = window_cell(iota((32, CELLS), 1))
    place_edge = one_hot((v_col >= 28) & (iota((32, CELLS), 0) == 4 * v_row + v_col - 28))
    back_main[...] = dot(place_main, grad_in).astype(BF)
    back_rd[...] = dot(place_edge, grad_in).astype(BF)
    to_below, to_right, to_last = (x_at, below, col), (x_at, row, right), (x_at, below, right)
    back = []
    for n, (src, dst, device) in enumerate([
        (back_rd.at[pl.ds(0, 16)], got_rd.at[pl.ds(0, 16)], to_right),
        (back_rd.at[pl.ds(16, 16)], got_rd.at[pl.ds(16, 16)], to_last),
        (back_main.at[pl.ds(128, 128)], got_up, to_below),
    ]):
        back.append(send(src, dst, back_ss.at[n], back_rs.at[n], device))

    start_xy(att)
    start_last(mlp)

    for copy in back:
        copy.wait_recv()
    spread = one_hot(iota((128, 16), 0) == 32 * (iota((128, 16), 1) >> 2) + (iota((128, 16), 1) & 3))
    out_ref[0:128, :] = (got_up[...].astype(F32) + dot(spread, got_rd[16:32, :])).astype(BF)
    out_ref[128:256, :] = (back_main[0:128, :].astype(F32) + dot(spread, got_rd[0:16, :])).astype(BF)

    start_yx(att)
    start_z(att)
    first, second = finish(mlp)
    apart = jnp.concatenate([first, second], axis=0)
    mixed = jnp.concatenate([part[i : i + 1] for i in range(4) for part in (first, second)], axis=0)
    mlp_ref[...] = jnp.where(x_at < 2, apart, mixed)

    start_last(att)
    first, second = finish(att)
    att_ref[...] = jnp.concatenate([first[0:1], second[0:1], first[1:2], second[1:2]], axis=0)

    for copy in halo + back + sends:
        copy.wait_send()


def reduce_scratch(unit):
    chip_rows = NZ_LO * NY * unit
    half, quarter = chip_rows // 2, chip_rows // 8
    return [
        pltpu.VMEM((2, NX * chip_rows, 128), F32),
        pltpu.VMEM((NX * chip_rows, 128), BF),
        pltpu.VMEM((NX * chip_rows, 128), BF),
        pltpu.VMEM((NX, half, 128), BF),
        pltpu.VMEM((NY, half, 128), BF),
        pltpu.VMEM((NX - 1, half, 128), BF),
        pltpu.VMEM((NY - 1, half, 128), BF),
        pltpu.VMEM((NY, quarter, 128), BF),
        pltpu.VMEM((NX, quarter, 128), BF),
        pltpu.VMEM((NY - 1, quarter, 128), BF),
        pltpu.VMEM((NX - 1, quarter, 128), BF),
        pltpu.VMEM((NZ_LO, NZ_HI, unit // 2, 128), F32),
        pltpu.VMEM((NZ - 1, unit // 2, 128), F32),
        pltpu.VMEM((2, unit // 4, 128), F32),
        pltpu.VMEM((unit // 4, 128), F32),
    ]


def on_device(
    hidden_in, token_ids, embed, norm1_gain, norm2_gain, w_qkv, rel_bias, w_proj, w_up, w_down, out_grad
):
    table = rel_bias.reshape(HEADS, 15, 15).transpose(1, 0, 2)
    table = jnp.pad(table, ((0, 1), (0, 0), (0, 1))).reshape(16, 128)
    dma = pltpu.SemaphoreType.DMA
    grad_out, attention_grads, mlp_grads = pl.pallas_call(
        kernel,
        out_shape=(
            jax.ShapeDtypeStruct((CELLS, D), BF),
            jax.ShapeDtypeStruct((4, 128), F32),
            jax.ShapeDtypeStruct((8, 128), F32),
        ),
        in_specs=[pl.BlockSpec(memory_space=pltpu.VMEM)] * 11,
        out_specs=[pl.BlockSpec(memory_space=pltpu.VMEM)] * 3,
        scratch_shapes=[
            pltpu.VMEM((32, 2 * D), BF),
            pltpu.VMEM((128, D), BF),
            pltpu.VMEM((128, D), BF),
            pltpu.VMEM((32, 2 * D), BF),
            pltpu.VMEM((3, 8, 32), jnp.int32),
            pltpu.VMEM((64, 512), F32),
            pltpu.VMEM((CELLS, 512), F32),
            pltpu.VMEM((4, 512, D), BF),
            pltpu.VMEM((4, 512, D), BF),
            pltpu.VMEM((CELLS, 3 * D), BF),
            pltpu.VMEM((CELLS, D), BF),
            pltpu.VMEM((CELLS, FF), BF),
            pltpu.VMEM((CELLS, FF), BF),
            pltpu.VMEM((CELLS, 3 * D), BF),
            pltpu.VMEM((CELLS, D), BF),
            pltpu.VMEM((32, D), BF),
            pltpu.VMEM((128, D), BF),
            pltpu.VMEM((32, D), BF),
        ]
        + reduce_scratch(MLP_UNIT)
        + reduce_scratch(ATT_UNIT)
        + [dma((7,)), dma((7,)), dma((3,)), dma((3,)), dma((14,)), dma((14,)), dma((14,)), dma((14,))]
        + [dma((NZ - 1,))] * 4,
        compiler_params=pltpu.CompilerParams(
            collective_id=0, has_side_effects=True, vmem_limit_bytes=48 * 1024 * 1024
        ),
        name="decoder_block_backward",
    )(
        hidden_in.reshape(CELLS, D),
        token_ids.reshape(8, 32),
        embed,
        norm1_gain.reshape(1, D),
        norm2_gain.reshape(1, D),
        w_qkv,
        table,
        w_proj,
        w_up,
        w_down,
        out_grad.reshape(CELLS, D),
    )
    return grad_out.reshape(1, 8, 32, D), attention_grads, mlp_grads


def solution(mesh):
    placed = (
        P("dp", "row", "col", None),
        P("dp", "row", "col"),
        P(),
        P(),
        P(),
        P(),
        P(),
        P(),
        P(),
        P(),
        P("dp", "row", "col", None),
    )
    return jax.shard_map(
        on_device,
        mesh=mesh,
        in_specs=placed,
        out_specs=(
            P("dp", "row", "col", None),
            P(("dp", "row", "col"), None),
            P(("dp", "row", "col"), None),
        ),
        check_vma=False,
    )
```

```python
import jax
import jax.numpy as jnp
from jax import lax
from jax.experimental import pallas as pl
from jax.experimental.pallas import tpu as pltpu
from jax.sharding import PartitionSpec as P

D = 256
FF = 1024
HEADS = 8
HEAD_DIM = 32
WIN = 8
PAIRS = 225
CELLS = 256
NORM_EPS = 1e-05
GELU_SCALE = 0.7978845608028654
GELU_CUBIC = 0.044715
SCALE = HEAD_DIM ** (-0.5)

NX, NY, NZ_LO, NZ_HI = 4, 4, 8, 2
NZ = NZ_LO * NZ_HI
ROW_DEVICES, COL_DEVICES = NZ_LO * NY, NZ_HI * 2
MLP_UNIT, ATT_UNIT = 16, 8

MESH = pl.DeviceIdType.MESH
BF = jnp.bfloat16
F32 = jnp.float32


def iota(shape, dim):
    return lax.broadcasted_iota(jnp.int32, shape, dim)


def one_hot(condition):
    return jnp.where(condition, 1.0, 0.0).astype(BF)


def dot(left, right):
    return jnp.dot(left, right, preferred_element_type=F32)


def dot_nt(left, right):
    return lax.dot_general(left, right, (((1,), (1,)), ((), ())), preferred_element_type=F32)


def dot_tn(left, right):
    return lax.dot_general(left, right, (((0,), (0,)), ((), ())), preferred_element_type=F32)


def mean_of(values):
    return jnp.mean(values, axis=-1, keepdims=True)


def layer_norm(values):
    center = values - mean_of(values)
    inv_std = lax.rsqrt(mean_of(center * center) + NORM_EPS)
    return center * inv_std, inv_std


def norm_back(upstream, normed, inv_std, gain):
    scaled = upstream * gain
    return inv_std * (scaled - mean_of(scaled) - normed * mean_of(scaled * normed))


def window_cell(token):
    return token & 7, ((token >> 6) << 3) + ((token >> 3) & 7)


def block_sum(values, ones_pair):
    high = values.astype(BF)
    low = (values - high.astype(F32)).astype(BF)
    parts = []
    for j in range(4):
        lanes = slice(128 * j, 128 * (j + 1))
        parts.append(dot(jnp.concatenate([high[:, lanes], low[:, lanes]], axis=1), ones_pair))
    return jnp.concatenate(parts, axis=1)


def load_rel_bias(rb):
    rb_high = rb.astype(BF)
    rb_rest = rb - rb_high.astype(F32)
    rb_mid = rb_rest.astype(BF)
    rb_low = (rb_rest - rb_mid.astype(F32)).astype(BF)
    parts = jnp.concatenate([rb_high, rb_mid, rb_low], axis=0)
    pair, lane = iota((PAIRS, 2048), 0), iota((PAIRS, 2048), 1)
    offset = lane & 15
    spread = dot(parts, one_hot((offset < 15) & (pair == 15 * (lane >> 7) + offset)))
    spread = spread[0:8] + spread[8:16] + spread[16:24]
    own = iota((8, 2048), 0) == ((iota((8, 2048), 1) >> 4) & 7)
    line = jnp.sum(jnp.where(own, spread, 0.0), axis=0, keepdims=True)
    return jnp.concatenate([line[:, 128 * u : 128 * u + 128] for u in range(16)], axis=0)


def kernel(
    hid_in, tok_in, emb_in, g1_in, g2_in, wqkv_in, rb_in, wproj_in, wup_in, wdown_in, og_in,
    out_ref, att_ref, mlp_ref,
    hid_ref, tok_ref, emb_ref, g1_ref, g2_ref, wqkv_ref, rb_ref, wproj_ref, wup_ref, wdown_ref, og_ref,
    stage_hid, stage_og, halo_hid, halo_og, edge_hid, edge_og, halo_tok,
    bias_s, probs_s, ke_s, ve_s, qkv_s, ctx_s, dqkv_s, back_main, back_rd, got_up, got_rd,
    mlp_f32, mlp_send, mlp_recv, mlp_x, mlp_y, mlp_rx, mlp_ry,
    att_f32, att_send, att_recv, att_x, att_y, att_rx, att_ry,
    x3, y3, rx3, ry3, z_send, z_recv, c_send, c_recv,
    in_sem, halo_ss, halo_rs, back_ss, back_rs, mlp_ss, mlp_rs, att_ss, att_rs, late_ss, late_rs, z_ss, z_rs,
):
    loads = [
        pltpu.make_async_copy(src, dst, in_sem.at[n])
        for n, (src, dst) in enumerate([
            (hid_in, hid_ref), (og_in, og_ref), (tok_in, tok_ref), (rb_in, rb_ref), (emb_in, emb_ref),
            (g1_in, g1_ref), (g2_in, g2_ref), (wqkv_in, wqkv_ref), (wproj_in, wproj_ref),
            (wup_in, wup_ref), (wdown_in, wdown_ref),
        ])
    ]
    for load in loads:
        load.start()

    x_at, row, col = lax.axis_index("dp"), lax.axis_index("row"), lax.axis_index("col")
    z_lo, y_at = row // NY, row % NY
    z_hi, core = col // 2, col % 2
    z_at = z_hi * NZ_LO + z_lo
    mate = 1 - core

    above = (row + ROW_DEVICES - 1) % ROW_DEVICES
    below = (row + 1) % ROW_DEVICES
    left = (col + COL_DEVICES - 1) % COL_DEVICES
    right = (col + 1) % COL_DEVICES

    def at_mate():
        return (x_at, row, z_hi * 2 + mate)

    def at_x(other):
        return (other, row, col)

    def at_y(other):
        return (x_at, z_lo * NY + other, col)

    def at_z(other):
        return (x_at, (other % NZ_LO) * NY + y_at, (other // NZ_LO) * 2 + core)

    partners = [(x_at, above, left), (x_at, below, right), (x_at, above, col), (x_at, below, col)]
    partners += [(x_at, row, left), (x_at, row, right), at_mate()]
    partners += [at_x((x_at + d) % NX) for d in range(1, NX)]
    partners += [at_y((y_at + d) % NY) for d in range(1, NY)]
    partners += [at_z((z_at + d) % NZ) for d in range(1, NZ)]
    barrier = pltpu.get_barrier_semaphore()
    for partner in partners:
        pl.semaphore_signal(barrier, inc=1, device_id=partner, device_id_type=MESH)

    def send(src, dst, send_sem, recv_sem, device):
        copy = pltpu.make_async_remote_copy(
            src_ref=src, dst_ref=dst, send_sem=send_sem, recv_sem=recv_sem,
            device_id=device, device_id_type=MESH,
        )
        copy.start()
        return copy

    r32, s256 = iota((32, CELLS), 0), iota((32, CELLS), 1)
    stage_row = jnp.where(r32 < 16, 4, 0) + ((r32 & 15) >> 2)
    pick = one_hot(s256 == stage_row * 32 + (r32 & 3))
    for n in range(3):
        loads[n].wait()
    stage_hid[...] = dot(pick, hid_ref[...]).astype(BF)
    stage_og[...] = dot(pick, og_ref[...]).astype(BF)

    pl.semaphore_wait(barrier, len(partners))

    to_above, to_left, to_corner = (x_at, above, col), (x_at, row, left), (x_at, above, left)
    halo = []
    for n, (src, dst, device) in enumerate([
        (stage_hid.at[pl.ds(16, 16)], edge_hid.at[pl.ds(16, 16)], to_corner),
        (tok_ref, halo_tok.at[2], to_corner),
        (stage_hid.at[pl.ds(0, 16)], edge_hid.at[pl.ds(0, 16)], to_left),
        (tok_ref, halo_tok.at[1], to_left),
        (hid_ref.at[pl.ds(0, 128)], halo_hid, to_above),
        (tok_ref, halo_tok.at[0], to_above),
        (stage_og.at[pl.ds(16, 16)], edge_og.at[pl.ds(16, 16)], to_corner),
        (stage_og.at[pl.ds(0, 16)], edge_og.at[pl.ds(0, 16)], to_left),
        (og_ref.at[pl.ds(0, 128)], halo_og, to_above),
    ]):
        halo.append(send(src, dst, halo_ss.at[n], halo_rs.at[n], device))

    loads[3].wait()
    rb = load_rel_bias(rb_ref[...])
    wide_row, wide_lane = iota((128, 512), 0), iota((128, 512), 1)
    pair_sum = jnp.where(
        (wide_row >> 4) == (wide_lane >> 6), (wide_row & 15) + ((wide_lane >> 3) & 7), -1
    )
    rb_high = rb.astype(BF)
    rb_rest = rb - rb_high.astype(F32)
    rb_mid = rb_rest.astype(BF)
    rb_low = (rb_rest - rb_mid.astype(F32)).astype(BF)
    rb_parts = jnp.concatenate([rb_high, rb_mid, rb_low], axis=0)
    key_row = iota((8, 512), 1) & 7
    for qj in range(8):
        tall = dot(rb_parts, one_hot(pair_sum == qj + 7))
        tall = tall[0:16] + tall[16:32] + tall[32:48]
        rows = jnp.zeros((8, 512), F32)
        for ki in range(8):
            rows = jnp.where(key_row == ki, tall[7 - ki : 15 - ki], rows)
        bias_s[8 * qj : 8 * qj + 8, :] = rows

    t_row, t_col = window_cell(iota((CELLS, CELLS), 0))
    s_lane = iota((CELLS, CELLS), 1)
    pick_main = one_hot((t_col < 28) & (s_lane == 32 * t_row + t_col + 4))
    e_row, e_col = window_cell(iota((CELLS, 32), 0))
    pick_edge = one_hot((e_col >= 28) & (iota((CELLS, 32), 1) == 4 * e_row + e_col - 28))
    for load in loads[4:]:
        load.wait()

    for copy in halo[:6]:
        copy.wait_recv()
    tok = tok_ref[...]
    tok_below, tok_right, tok_corner = halo_tok[0], halo_tok[1], halo_tok[2]
    tok_main = jnp.concatenate(
        [tok[4 + i : 5 + i, :] for i in range(4)] + [tok_below[i : i + 1, :] for i in range(4)], axis=1
    )
    tok_edge = jnp.concatenate(
        [tok_right[4 + i : 5 + i, 0:4] for i in range(4)] + [tok_corner[i : i + 1, 0:4] for i in range(4)],
        axis=1,
    )
    tok_main = jnp.broadcast_to(tok_main.astype(F32), (128, CELLS)).astype(BF)
    tok_edge = jnp.broadcast_to(tok_edge.astype(F32), (128, 32)).astype(BF)
    ids = dot_nt(pick_main, tok_main) + dot_nt(pick_edge, tok_edge)
    ids = jnp.concatenate([ids, ids], axis=1)
    emb = emb_ref[...].astype(F32)
    token_part = jnp.where(
        ids < 1.5,
        jnp.where(ids < 0.5, emb[0:1], emb[1:2]),
        jnp.where(ids < 2.5, emb[2:3], emb[3:4]),
    )
    main_hid = jnp.concatenate([hid_ref[128:256, :], halo_hid[...]], axis=0)
    resid_in = dot(pick_main, main_hid) + dot(pick_edge, edge_hid[...]) + token_part
    normed_one, inv_one = layer_norm(resid_in)
    gain_one = g1_ref[...]
    normal_low = (normed_one * gain_one).astype(BF)

    qkv_s[...] = dot(normal_low, wqkv_ref[...]).astype(BF)

    head_mask = one_hot((iota((512, D), 0) >> 6) == (iota((512, D), 1) >> 5))
    ones_pair = one_hot(((iota((256, 128), 0) & 127) >> 6) == (iota((256, 128), 1) >> 6))
    for w in range(4):
        cells = slice(64 * w, 64 * w + 64)
        keys = jnp.concatenate([qkv_s[cells, D : 2 * D]] * HEADS, axis=0) * head_mask
        ke_s[w] = keys
        ve_s[w] = jnp.concatenate([qkv_s[cells, 2 * D :]] * HEADS, axis=0) * head_mask
        probs_s[cells, :] = jnp.exp(dot_nt(qkv_s[cells, :D], keys) * SCALE + bias_s[...])
    raised = probs_s[...]
    probs = raised / block_sum(raised, ones_pair)
    probs_s[...] = probs
    probs_low = probs.astype(BF)
    for w in range(4):
        cells = slice(64 * w, 64 * w + 64)
        ctx_s[cells, :] = dot(probs_low[cells], ve_s[w]).astype(BF)

    context = ctx_s[...]
    resid_mid = resid_in + dot(context, wproj_ref[...])
    normed_two, inv_two = layer_norm(resid_mid)
    gain_two = g2_ref[...]
    mlp_in = (normed_two * gain_two).astype(BF)

    for copy in halo[6:]:
        copy.wait_recv()
    main_og = jnp.concatenate([og_ref[128:256, :], halo_og[...]], axis=0)
    grad_f32 = dot(pick_main, main_og) + dot(pick_edge, edge_og[...])
    grad = grad_f32.astype(BF)

    grad_mid = jnp.zeros((CELLS, D), F32)
    for n in range(4):
        units = slice(256 * n, 256 * n + 256)
        pre = dot(mlp_in, wup_ref[:, units])
        grad_act = dot_nt(grad, wdown_ref[units, :])
        square = pre * pre
        tanh_part = jnp.tanh(GELU_SCALE * pre * (1.0 + GELU_CUBIC * square))
        half_plus = 0.5 * (1.0 + tanh_part)
        slope = half_plus + 0.5 * pre * (1.0 - tanh_part * tanh_part) * (
            GELU_SCALE * (1.0 + 3.0 * GELU_CUBIC * square)
        )
        act = (pre * half_plus).astype(BF)
        grad_pre = (grad_act * slope).astype(BF)
        grad_mid = grad_mid + dot_nt(grad_pre, wup_ref[:, units])
        up_grad = dot_tn(mlp_in, grad_pre)
        half, lane_tile = n // 2, 2 * (n % 2)
        mlp_f32[half, pl.ds(lane_tile, 256, stride=4), :] = up_grad[:, :128]
        mlp_f32[half, pl.ds(lane_tile + 1, 256, stride=4), :] = up_grad[:, 128:]
        down_grad = dot_tn(act, grad)
        mlp_f32[0, 1024 + 256 * n : 1280 + 256 * n, :] = down_grad[:, :128]
        mlp_f32[1, 1024 + 256 * n : 1280 + 256 * n, :] = down_grad[:, 128:]

    mlp = dict(
        unit=MLP_UNIT, f32=mlp_f32, send=mlp_send, recv=mlp_recv, x=mlp_x, y=mlp_y, rx=mlp_rx, ry=mlp_ry,
        ss=mlp_ss, rs=mlp_rs,
    )
    att = dict(
        unit=ATT_UNIT, f32=att_f32, send=att_send, recv=att_recv, x=att_x, y=att_y, rx=att_rx, ry=att_ry,
        ss=att_ss, rs=att_rs,
    )
    sends = []

    def start_mate(b):
        b["send"][...] = b["f32"][mate].astype(BF)
        b["p1"] = [send(b["send"], b["recv"], b["ss"].at[0], b["rs"].at[0], at_mate())]
        sends.extend(b["p1"])

    def start_xy(b):
        b["p1"][0].wait_recv()
        unit = b["unit"]
        part = NZ_LO // 2 * NY * unit
        quarter = part // NY
        for x in range(NX):
            first, second = slice(2 * part * x, 2 * part * x + part), slice(2 * part * x + part, 2 * part * (x + 1))
            total = b["f32"][core, first, :] + b["recv"][first, :].astype(F32)
            b["x"][x] = total.astype(BF)
            total = b["f32"][core, second, :] + b["recv"][second, :].astype(F32)
            total = total.reshape(NZ_LO // 2, NY, unit, 128)
            for y in range(NY):
                b["y"][y, quarter * x : quarter * (x + 1), :] = total[:, y].reshape(quarter, 128).astype(BF)
        b["p2"] = []
        for d in (2, 1, 3):
            other = (x_at + d) % NX
            b["p2"].append(
                send(b["x"].at[other], b["rx"].at[d - 1], b["ss"].at[d], b["rs"].at[d], at_x(other))
            )
            other = (y_at + d) % NY
            b["p2"].append(
                send(b["y"].at[other], b["ry"].at[d - 1], b["ss"].at[3 + d], b["rs"].at[3 + d], at_y(other))
            )
        sends.extend(b["p2"])

    start_mate(mlp)

    grad_res = grad_f32 + norm_back(grad_mid, normed_two, inv_two, gain_two)
    grad_res_low = grad_res.astype(BF)
    proj_grad = dot_tn(context, grad_res_low)
    att_f32[0, 768:, :] = proj_grad[:, :128]
    att_f32[1, 768:, :] = proj_grad[:, 128:]
    grad_context = dot_nt(grad_res_low, wproj_ref[...]).astype(BF)

    grad_probs = jnp.concatenate(
        [dot_nt(grad_context[64 * w : 64 * w + 64], ve_s[w]) for w in range(4)], axis=0
    )
    probs = probs_s[...]
    grad_scores = probs * (grad_probs - block_sum(probs * grad_probs, ones_pair))
    scores_low = grad_scores.astype(BF)
    probs_low = probs.astype(BF)

    head_of_lane = iota((64, D), 1) >> 5

    def own_heads(stacked):
        result = jnp.zeros((64, D), F32)
        for h in range(HEADS):
            result = jnp.where(head_of_lane == h, stacked[64 * h : 64 * h + 64], result)
        return result

    for w in range(4):
        cells = slice(64 * w, 64 * w + 64)
        dqkv_s[cells, :D] = (dot(scores_low[cells], ke_s[w]) * SCALE).astype(BF)
        dqkv_s[cells, D : 2 * D] = (own_heads(dot_tn(scores_low[cells], qkv_s[cells, :D])) * SCALE).astype(BF)
        dqkv_s[cells, 2 * D :] = own_heads(dot_tn(probs_low[cells], grad_context[cells])).astype(BF)

    for m in range(3):
        part_grad = dot_tn(normal_low, dqkv_s[:, D * m : D * (m + 1)])
        att_f32[0, pl.ds(m, 256, stride=3), :] = part_grad[:, :128]
        att_f32[1, pl.ds(m, 256, stride=3), :] = part_grad[:, 128:]

    start_mate(att)
    start_xy(mlp)

    grad_norm_in = dot_nt(dqkv_s[...], wqkv_ref[...])
    grad_in = (grad_res + norm_back(grad_norm_in, normed_one, inv_one, gain_one)).astype(BF)
    u_row, u_col = window_cell(iota((CELLS, CELLS), 1))
    place_main = one_hot((u_col < 28) & (iota((CELLS, CELLS), 0) == 32 * u_row + u_col + 4))
    v_row, v_col = window_cell(iota((32, CELLS), 1))
    place_edge = one_hot((v_col >= 28) & (iota((32, CELLS), 0) == 4 * v_row + v_col - 28))
    back_main[...] = dot(place_main, grad_in).astype(BF)
    back_rd[...] = dot(place_edge, grad_in).astype(BF)

    start_xy(att)

    to_below, to_right, to_last = (x_at, below, col), (x_at, row, right), (x_at, below, right)
    back = []
    for n, (src, dst, device) in enumerate([
        (back_rd.at[pl.ds(16, 16)], got_rd.at[pl.ds(16, 16)], to_last),
        (back_rd.at[pl.ds(0, 16)], got_rd.at[pl.ds(0, 16)], to_right),
        (back_main.at[pl.ds(128, 128)], got_up, to_below),
    ]):
        back.append(send(src, dst, back_ss.at[n], back_rs.at[n], device))

    first_parts, second_parts = [], []
    for b in (mlp, att):
        for copy in b["p2"]:
            copy.wait_recv()
        total = b["x"][x_at].astype(F32)
        for d in range(NX - 1):
            total = total + b["rx"][d].astype(F32)
        first_parts.append(total.reshape(NZ_LO // 2, NY, b["unit"], 128))
        total = b["y"][y_at].astype(F32)
        for d in range(NY - 1):
            total = total + b["ry"][d].astype(F32)
        second_parts.append(total.reshape(NX, NZ_LO // 2 * b["unit"], 128))
    for y in range(NY):
        x3[y, 0:64, :] = first_parts[0][:, y].reshape(64, 128).astype(BF)
        x3[y, 64:96, :] = first_parts[1][:, y].reshape(32, 128).astype(BF)
    for x in range(NX):
        y3[x, 0:64, :] = second_parts[0][x].astype(BF)
        y3[x, 64:96, :] = second_parts[1][x].astype(BF)
    swaps = []
    for d in (2, 1, 3):
        other = (y_at + d) % NY
        swaps.append(send(x3.at[other], rx3.at[d - 1], late_ss.at[d - 1], late_rs.at[d - 1], at_y(other)))
        other = (x_at + d) % NX
        swaps.append(send(y3.at[other], ry3.at[d - 1], late_ss.at[2 + d], late_rs.at[2 + d], at_x(other)))

    for copy in swaps:
        copy.wait_recv()
    for part, own, own_at, got in ((0, x3, y_at, rx3), (1, y3, x_at, ry3)):
        total = own[own_at].astype(F32)
        for d in range(NX - 1):
            total = total + got[d].astype(F32)
        for lo in range(NZ_LO // 2):
            for hi in range(NZ_HI):
                at_mlp, at_att = 16 * lo + 8 * hi, 64 + 8 * lo + 4 * hi
                piece = jnp.concatenate(
                    [total[at_mlp : at_mlp + 8], total[at_att : at_att + 4], jnp.zeros((4, 128), F32)], axis=0
                )
                z_send[part * (NZ_LO // 2) + lo, hi] = piece.astype(BF)
    ring = []
    for d in (8, 7, 9, 6, 10, 5, 11, 4, 12, 3, 13, 2, 14, 1, 15):
        other = (z_at + d) % NZ
        ring.append(
            send(
                z_send.at[other % NZ_LO, other // NZ_LO], z_recv.at[d - 1],
                z_ss.at[d - 1], z_rs.at[d - 1], at_z(other),
            )
        )

    for copy in back:
        copy.wait_recv()
    spread = one_hot(iota((128, 16), 0) == 32 * (iota((128, 16), 1) >> 2) + (iota((128, 16), 1) & 3))
    out_ref[0:128, :] = (got_up[...].astype(F32) + dot(spread, got_rd[16:32, :])).astype(BF)
    out_ref[128:256, :] = (back_main[0:128, :].astype(F32) + dot(spread, got_rd[0:16, :])).astype(BF)

    for copy in ring:
        copy.wait_recv()
    total = z_send[z_lo, z_hi].astype(F32)
    for d in range(NZ - 1):
        total = total + z_recv[d].astype(F32)
    for k in range(2):
        c_send[k] = jnp.concatenate(
            [total[4 * k : 4 * k + 4], total[8 + 2 * k : 10 + 2 * k], total[12:14]], axis=0
        )
    last = send(c_send.at[mate], c_recv, late_ss.at[6], late_rs.at[6], at_mate())
    last.wait_recv()
    own, got = c_send[core], c_recv[...]
    first, second = jnp.where(core == 0, own, got), jnp.where(core == 0, got, own)
    apart = jnp.concatenate([first[0:4], second[0:4]], axis=0)
    mixed = jnp.concatenate([part[i : i + 1] for i in range(4) for part in (first, second)], axis=0)
    mlp_ref[...] = jnp.where(x_at < 2, apart, mixed)
    att_ref[...] = jnp.concatenate([first[4:5], second[4:5], first[5:6], second[5:6]], axis=0)

    for copy in halo + back + sends + swaps + ring + [last]:
        copy.wait_send()


def reduce_scratch(unit):
    chip_rows = NZ_LO * NY * unit
    half = chip_rows // 2
    return [
        pltpu.VMEM((2, NX * chip_rows, 128), F32),
        pltpu.VMEM((NX * chip_rows, 128), BF),
        pltpu.VMEM((NX * chip_rows, 128), BF),
        pltpu.VMEM((NX, half, 128), BF),
        pltpu.VMEM((NY, half, 128), BF),
        pltpu.VMEM((NX - 1, half, 128), BF),
        pltpu.VMEM((NY - 1, half, 128), BF),
    ]


def on_device(
    hidden_in, token_ids, embed, norm1_gain, norm2_gain, w_qkv, rel_bias, w_proj, w_up, w_down, out_grad
):
    dma = pltpu.SemaphoreType.DMA
    operands = (
        hidden_in.reshape(CELLS, D),
        token_ids.reshape(8, 32),
        embed,
        norm1_gain.reshape(1, D),
        norm2_gain.reshape(1, D),
        w_qkv,
        rel_bias,
        w_proj,
        w_up,
        w_down,
        out_grad.reshape(CELLS, D),
    )
    chunk = NZ_LO // 2 * (MLP_UNIT + ATT_UNIT)
    grad_out, attention_grads, mlp_grads = pl.pallas_call(
        kernel,
        out_shape=(
            jax.ShapeDtypeStruct((CELLS, D), BF),
            jax.ShapeDtypeStruct((4, 128), F32),
            jax.ShapeDtypeStruct((8, 128), F32),
        ),
        in_specs=[pl.BlockSpec(memory_space=pltpu.HBM)] * len(operands),
        out_specs=[pl.BlockSpec(memory_space=pltpu.VMEM)] * 3,
        scratch_shapes=[pltpu.VMEM(operand.shape, operand.dtype) for operand in operands]
        + [
            pltpu.VMEM((32, D), BF),
            pltpu.VMEM((32, D), BF),
            pltpu.VMEM((128, D), BF),
            pltpu.VMEM((128, D), BF),
            pltpu.VMEM((32, D), BF),
            pltpu.VMEM((32, D), BF),
            pltpu.VMEM((3, 8, 32), jnp.int32),
            pltpu.VMEM((64, 512), F32),
            pltpu.VMEM((CELLS, 512), F32),
            pltpu.VMEM((4, 512, D), BF),
            pltpu.VMEM((4, 512, D), BF),
            pltpu.VMEM((CELLS, 3 * D), BF),
            pltpu.VMEM((CELLS, D), BF),
            pltpu.VMEM((CELLS, 3 * D), BF),
            pltpu.VMEM((CELLS, D), BF),
            pltpu.VMEM((32, D), BF),
            pltpu.VMEM((128, D), BF),
            pltpu.VMEM((32, D), BF),
        ]
        + reduce_scratch(MLP_UNIT)
        + reduce_scratch(ATT_UNIT)
        + [
            pltpu.VMEM((NY, chunk, 128), BF),
            pltpu.VMEM((NX, chunk, 128), BF),
            pltpu.VMEM((NY - 1, chunk, 128), BF),
            pltpu.VMEM((NX - 1, chunk, 128), BF),
            pltpu.VMEM((NZ_LO, NZ_HI, 16, 128), BF),
            pltpu.VMEM((NZ - 1, 16, 128), BF),
            pltpu.VMEM((2, 8, 128), F32),
            pltpu.VMEM((8, 128), F32),
        ]
        + [dma((len(operands),)), dma((9,)), dma((9,)), dma((3,)), dma((3,))]
        + [dma((7,))] * 6
        + [dma((NZ - 1,))] * 2,
        compiler_params=pltpu.CompilerParams(
            collective_id=0, has_side_effects=True, vmem_limit_bytes=62 * 1024 * 1024
        ),
        name="decoder_block_backward",
    )(*operands)
    return grad_out.reshape(1, 8, 32, D), attention_grads, mlp_grads


def solution(mesh):
    placed = (
        P("dp", "row", "col", None),
        P("dp", "row", "col"),
        P(),
        P(),
        P(),
        P(),
        P(),
        P(),
        P(),
        P(),
        P("dp", "row", "col", None),
    )
    return jax.shard_map(
        on_device,
        mesh=mesh,
        in_specs=placed,
        out_specs=(
            P("dp", "row", "col", None),
            P(("dp", "row", "col"), None),
            P(("dp", "row", "col"), None),
        ),
        check_vma=False,
    )
```

```python
import jax
import jax.numpy as jnp
from jax import lax
from jax.experimental import pallas as pl
from jax.experimental.pallas import tpu as pltpu
from jax.sharding import PartitionSpec as P

D = 256
FF = 1024
HEADS = 8
HEAD_DIM = 32
WIN = 8
PAIRS = 225
CELLS = 256
NORM_EPS = 1e-05
GELU_SCALE = 0.7978845608028654
GELU_CUBIC = 0.044715
SCALE = HEAD_DIM ** (-0.5)

NX, NY, NZ_LO, NZ_HI = 4, 4, 8, 2
NZ = NZ_LO * NZ_HI
ROW_DEVICES, COL_DEVICES = NZ_LO * NY, NZ_HI * 2
MLP_UNIT, ATT_UNIT = 16, 8

MESH = pl.DeviceIdType.MESH
BF = jnp.bfloat16
F32 = jnp.float32


def iota(shape, dim):
    return lax.broadcasted_iota(jnp.int32, shape, dim)


def one_hot(condition):
    return jnp.where(condition, 1.0, 0.0).astype(BF)


def dot(left, right):
    return jnp.dot(left, right, preferred_element_type=F32)


def dot_nt(left, right):
    return lax.dot_general(left, right, (((1,), (1,)), ((), ())), preferred_element_type=F32)


def dot_tn(left, right):
    return lax.dot_general(left, right, (((0,), (0,)), ((), ())), preferred_element_type=F32)


def mean_of(values):
    return jnp.mean(values, axis=-1, keepdims=True)


def layer_norm(values):
    center = values - mean_of(values)
    inv_std = lax.rsqrt(mean_of(center * center) + NORM_EPS)
    return center * inv_std, inv_std


def norm_back(upstream, normed, inv_std, gain):
    scaled = upstream * gain
    return inv_std * (scaled - mean_of(scaled) - normed * mean_of(scaled * normed))


def window_cell(token):
    return token & 7, ((token >> 6) << 3) + ((token >> 3) & 7)


def block_sum(values, ones_pair):
    high = values.astype(BF)
    low = (values - high.astype(F32)).astype(BF)
    parts = []
    for j in range(4):
        lanes = slice(128 * j, 128 * (j + 1))
        parts.append(dot(jnp.concatenate([high[:, lanes], low[:, lanes]], axis=1), ones_pair))
    return jnp.concatenate(parts, axis=1)


def load_rel_bias(rb):
    rb_high = rb.astype(BF)
    rb_rest = rb - rb_high.astype(F32)
    rb_mid = rb_rest.astype(BF)
    rb_low = (rb_rest - rb_mid.astype(F32)).astype(BF)
    parts = jnp.concatenate([rb_high, rb_mid, rb_low], axis=0)
    pair, lane = iota((PAIRS, 2048), 0), iota((PAIRS, 2048), 1)
    offset = lane & 15
    spread = dot(parts, one_hot((offset < 15) & (pair == 15 * (lane >> 7) + offset)))
    spread = spread[0:8] + spread[8:16] + spread[16:24]
    own = iota((8, 2048), 0) == ((iota((8, 2048), 1) >> 4) & 7)
    line = jnp.sum(jnp.where(own, spread, 0.0), axis=0, keepdims=True)
    return jnp.concatenate([line[:, 128 * u : 128 * u + 128] for u in range(16)], axis=0)


def kernel(
    hid_in, tok_in, emb_in, g1_in, g2_in, wqkv_in, rb_in, wproj_in, wup_in, wdown_in, og_in,
    out_ref, att_ref, mlp_ref,
    hid_ref, tok_ref, emb_ref, g1_ref, g2_ref, wqkv_ref, rb_ref, wproj_ref, wup_ref, wdown_ref, og_ref,
    stage_hid, stage_og, halo_hid, halo_og, edge_hid, edge_og, halo_tok,
    bias_s, probs_s, ke_s, ve_s, qkv_s, ctx_s, dqkv_s, back_main, back_rd, got_up, got_rd,
    mlp_f32, mlp_send, mlp_recv, mlp_x, mlp_y, mlp_rx, mlp_ry,
    att_f32, att_send, att_recv, att_x, att_y, att_rx, att_ry,
    x3, y3, rx3, ry3, z_send, z_recv, c_send, c_recv,
    in_sem, halo_ss, halo_rs, back_ss, back_rs, mlp_ss, mlp_rs, att_ss, att_rs, late_ss, late_rs, z_ss, z_rs, ring_sem,
):
    loads = [
        pltpu.make_async_copy(src, dst, in_sem.at[n])
        for n, (src, dst) in enumerate([
            (hid_in, hid_ref), (og_in, og_ref), (tok_in, tok_ref), (rb_in, rb_ref), (emb_in, emb_ref),
            (g1_in, g1_ref), (g2_in, g2_ref), (wqkv_in, wqkv_ref), (wproj_in, wproj_ref),
            (wup_in, wup_ref), (wdown_in, wdown_ref),
        ])
    ]
    for load in loads:
        load.start()

    x_at, row, col = lax.axis_index("dp"), lax.axis_index("row"), lax.axis_index("col")
    z_lo, y_at = row // NY, row % NY
    z_hi, core = col // 2, col % 2
    z_at = z_hi * NZ_LO + z_lo
    mate = 1 - core

    above = (row + ROW_DEVICES - 1) % ROW_DEVICES
    below = (row + 1) % ROW_DEVICES
    left = (col + COL_DEVICES - 1) % COL_DEVICES
    right = (col + 1) % COL_DEVICES

    def at_mate():
        return (x_at, row, z_hi * 2 + mate)

    def at_x(other):
        return (other, row, col)

    def at_y(other):
        return (x_at, z_lo * NY + other, col)

    def at_z(other):
        return (x_at, (other % NZ_LO) * NY + y_at, (other // NZ_LO) * 2 + core)

    barrier = pltpu.get_barrier_semaphore()
    near = [at_mate()]
    near += [at_x((x_at + d) % NX) for d in range(1, NX)]
    near += [at_y((y_at + d) % NY) for d in range(1, NY)]
    near += [at_z((z_at + 1) % NZ), at_z((z_at + NZ - 1) % NZ)]
    for partner in [(x_at, below, right), (x_at, below, col), (x_at, row, right)] + near:
        pl.semaphore_signal(barrier, inc=1, device_id=partner, device_id_type=MESH)

    def spread_ring(n):
        for other in ((z_at + 2**n) % NZ, (z_at + NZ - 2**n) % NZ):
            pl.semaphore_signal(ring_sem.at[n], inc=1, device_id=at_z(other), device_id_type=MESH)

    def hear_ring(n):
        pl.semaphore_wait(ring_sem.at[n], 2)

    def send(src, dst, send_sem, recv_sem, device):
        copy = pltpu.make_async_remote_copy(
            src_ref=src, dst_ref=dst, send_sem=send_sem, recv_sem=recv_sem,
            device_id=device, device_id_type=MESH,
        )
        copy.start()
        return copy

    r32, s256 = iota((32, CELLS), 0), iota((32, CELLS), 1)
    stage_row = jnp.where(r32 < 16, 4, 0) + ((r32 & 15) >> 2)
    pick = one_hot(s256 == stage_row * 32 + (r32 & 3))
    for n in range(3):
        loads[n].wait()
    stage_hid[...] = dot(pick, hid_ref[...]).astype(BF)
    stage_og[...] = dot(pick, og_ref[...]).astype(BF)

    pl.semaphore_wait(barrier, 3 + len(near))

    to_above, to_left, to_corner = (x_at, above, col), (x_at, row, left), (x_at, above, left)
    halo = []
    for n, (src, dst, device) in enumerate([
        (stage_hid.at[pl.ds(16, 16)], edge_hid.at[pl.ds(16, 16)], to_corner),
        (tok_ref, halo_tok.at[2], to_corner),
        (stage_hid.at[pl.ds(0, 16)], edge_hid.at[pl.ds(0, 16)], to_left),
        (tok_ref, halo_tok.at[1], to_left),
        (hid_ref.at[pl.ds(0, 128)], halo_hid, to_above),
        (tok_ref, halo_tok.at[0], to_above),
        (stage_og.at[pl.ds(16, 16)], edge_og.at[pl.ds(16, 16)], to_corner),
        (stage_og.at[pl.ds(0, 16)], edge_og.at[pl.ds(0, 16)], to_left),
        (og_ref.at[pl.ds(0, 128)], halo_og, to_above),
    ]):
        halo.append(send(src, dst, halo_ss.at[n], halo_rs.at[n], device))

    spread_ring(0)

    loads[3].wait()
    rb = load_rel_bias(rb_ref[...])
    wide_row, wide_lane = iota((128, 512), 0), iota((128, 512), 1)
    pair_sum = jnp.where(
        (wide_row >> 4) == (wide_lane >> 6), (wide_row & 15) + ((wide_lane >> 3) & 7), -1
    )
    rb_high = rb.astype(BF)
    rb_rest = rb - rb_high.astype(F32)
    rb_mid = rb_rest.astype(BF)
    rb_low = (rb_rest - rb_mid.astype(F32)).astype(BF)
    rb_parts = jnp.concatenate([rb_high, rb_mid, rb_low], axis=0)
    key_row = iota((8, 512), 1) & 7
    for qj in range(8):
        tall = dot(rb_parts, one_hot(pair_sum == qj + 7))
        tall = tall[0:16] + tall[16:32] + tall[32:48]
        rows = jnp.zeros((8, 512), F32)
        for ki in range(8):
            rows = jnp.where(key_row == ki, tall[7 - ki : 15 - ki], rows)
        bias_s[8 * qj : 8 * qj + 8, :] = rows

    t_row, t_col = window_cell(iota((CELLS, CELLS), 0))
    s_lane = iota((CELLS, CELLS), 1)
    pick_main = one_hot((t_col < 28) & (s_lane == 32 * t_row + t_col + 4))
    e_row, e_col = window_cell(iota((CELLS, 32), 0))
    pick_edge = one_hot((e_col >= 28) & (iota((CELLS, 32), 1) == 4 * e_row + e_col - 28))
    for load in loads[4:]:
        load.wait()

    for copy in halo[:6]:
        copy.wait_recv()
    tok = tok_ref[...]
    tok_below, tok_right, tok_corner = halo_tok[0], halo_tok[1], halo_tok[2]
    tok_main = jnp.concatenate(
        [tok[4 + i : 5 + i, :] for i in range(4)] + [tok_below[i : i + 1, :] for i in range(4)], axis=1
    )
    tok_edge = jnp.concatenate(
        [tok_right[4 + i : 5 + i, 0:4] for i in range(4)] + [tok_corner[i : i + 1, 0:4] for i in range(4)],
        axis=1,
    )
    tok_main = jnp.broadcast_to(tok_main.astype(F32), (128, CELLS)).astype(BF)
    tok_edge = jnp.broadcast_to(tok_edge.astype(F32), (128, 32)).astype(BF)
    ids = dot_nt(pick_main, tok_main) + dot_nt(pick_edge, tok_edge)
    ids = jnp.concatenate([ids, ids], axis=1)
    emb = emb_ref[...].astype(F32)
    token_part = jnp.where(
        ids < 1.5,
        jnp.where(ids < 0.5, emb[0:1], emb[1:2]),
        jnp.where(ids < 2.5, emb[2:3], emb[3:4]),
    )
    main_hid = jnp.concatenate([hid_ref[128:256, :], halo_hid[...]], axis=0)
    resid_in = dot(pick_main, main_hid) + dot(pick_edge, edge_hid[...]) + token_part
    normed_one, inv_one = layer_norm(resid_in)
    gain_one = g1_ref[...]
    normal_low = (normed_one * gain_one).astype(BF)

    qkv_s[...] = dot(normal_low, wqkv_ref[...]).astype(BF)

    head_mask = one_hot((iota((512, D), 0) >> 6) == (iota((512, D), 1) >> 5))
    ones_pair = one_hot(((iota((256, 128), 0) & 127) >> 6) == (iota((256, 128), 1) >> 6))
    for w in range(4):
        cells = slice(64 * w, 64 * w + 64)
        keys = jnp.concatenate([qkv_s[cells, D : 2 * D]] * HEADS, axis=0) * head_mask
        ke_s[w] = keys
        ve_s[w] = jnp.concatenate([qkv_s[cells, 2 * D :]] * HEADS, axis=0) * head_mask
        probs_s[cells, :] = jnp.exp(dot_nt(qkv_s[cells, :D], keys) * SCALE + bias_s[...])
    raised = probs_s[...]
    probs = raised / block_sum(raised, ones_pair)
    probs_s[...] = probs
    probs_low = probs.astype(BF)
    for w in range(4):
        cells = slice(64 * w, 64 * w + 64)
        ctx_s[cells, :] = dot(probs_low[cells], ve_s[w]).astype(BF)

    context = ctx_s[...]
    resid_mid = resid_in + dot(context, wproj_ref[...])
    normed_two, inv_two = layer_norm(resid_mid)
    gain_two = g2_ref[...]
    mlp_in = (normed_two * gain_two).astype(BF)

    for copy in halo[6:]:
        copy.wait_recv()
    main_og = jnp.concatenate([og_ref[128:256, :], halo_og[...]], axis=0)
    grad_f32 = dot(pick_main, main_og) + dot(pick_edge, edge_og[...])
    grad = grad_f32.astype(BF)

    grad_mid = jnp.zeros((CELLS, D), F32)
    for n in range(4):
        units = slice(256 * n, 256 * n + 256)
        pre = dot(mlp_in, wup_ref[:, units])
        grad_act = dot_nt(grad, wdown_ref[units, :])
        square = pre * pre
        tanh_part = jnp.tanh(GELU_SCALE * pre * (1.0 + GELU_CUBIC * square))
        half_plus = 0.5 * (1.0 + tanh_part)
        slope = half_plus + 0.5 * pre * (1.0 - tanh_part * tanh_part) * (
            GELU_SCALE * (1.0 + 3.0 * GELU_CUBIC * square)
        )
        act = (pre * half_plus).astype(BF)
        grad_pre = (grad_act * slope).astype(BF)
        grad_mid = grad_mid + dot_nt(grad_pre, wup_ref[:, units])
        up_grad = dot_tn(mlp_in, grad_pre)
        half, lane_tile = n // 2, 2 * (n % 2)
        mlp_f32[half, pl.ds(lane_tile, 256, stride=4), :] = up_grad[:, :128]
        mlp_f32[half, pl.ds(lane_tile + 1, 256, stride=4), :] = up_grad[:, 128:]
        down_grad = dot_tn(act, grad)
        mlp_f32[0, 1024 + 256 * n : 1280 + 256 * n, :] = down_grad[:, :128]
        mlp_f32[1, 1024 + 256 * n : 1280 + 256 * n, :] = down_grad[:, 128:]

    mlp = dict(
        unit=MLP_UNIT, f32=mlp_f32, send=mlp_send, recv=mlp_recv, x=mlp_x, y=mlp_y, rx=mlp_rx, ry=mlp_ry,
        ss=mlp_ss, rs=mlp_rs,
    )
    att = dict(
        unit=ATT_UNIT, f32=att_f32, send=att_send, recv=att_recv, x=att_x, y=att_y, rx=att_rx, ry=att_ry,
        ss=att_ss, rs=att_rs,
    )
    sends = []

    def start_mate(b):
        b["send"][...] = b["f32"][mate].astype(BF)
        b["p1"] = [send(b["send"], b["recv"], b["ss"].at[0], b["rs"].at[0], at_mate())]
        sends.extend(b["p1"])

    def start_xy(b):
        b["p1"][0].wait_recv()
        unit = b["unit"]
        part = NZ_LO // 2 * NY * unit
        quarter = part // NY
        for x in range(NX):
            first, second = slice(2 * part * x, 2 * part * x + part), slice(2 * part * x + part, 2 * part * (x + 1))
            total = b["f32"][core, first, :] + b["recv"][first, :].astype(F32)
            b["x"][x] = total.astype(BF)
            total = b["f32"][core, second, :] + b["recv"][second, :].astype(F32)
            total = total.reshape(NZ_LO // 2, NY, unit, 128)
            for y in range(NY):
                b["y"][y, quarter * x : quarter * (x + 1), :] = total[:, y].reshape(quarter, 128).astype(BF)
        b["p2"] = []
        for d in (2, 1, 3):
            other = (x_at + d) % NX
            b["p2"].append(
                send(b["x"].at[other], b["rx"].at[d - 1], b["ss"].at[d], b["rs"].at[d], at_x(other))
            )
            other = (y_at + d) % NY
            b["p2"].append(
                send(b["y"].at[other], b["ry"].at[d - 1], b["ss"].at[3 + d], b["rs"].at[3 + d], at_y(other))
            )
        sends.extend(b["p2"])

    start_mate(mlp)
    hear_ring(0)
    spread_ring(1)

    grad_res = grad_f32 + norm_back(grad_mid, normed_two, inv_two, gain_two)
    grad_res_low = grad_res.astype(BF)
    proj_grad = dot_tn(context, grad_res_low)
    att_f32[0, 768:, :] = proj_grad[:, :128]
    att_f32[1, 768:, :] = proj_grad[:, 128:]
    grad_context = dot_nt(grad_res_low, wproj_ref[...]).astype(BF)

    grad_probs = jnp.concatenate(
        [dot_nt(grad_context[64 * w : 64 * w + 64], ve_s[w]) for w in range(4)], axis=0
    )
    probs = probs_s[...]
    grad_scores = probs * (grad_probs - block_sum(probs * grad_probs, ones_pair))
    scores_low = grad_scores.astype(BF)
    probs_low = probs.astype(BF)

    head_of_lane = iota((64, D), 1) >> 5

    def own_heads(stacked):
        result = jnp.zeros((64, D), F32)
        for h in range(HEADS):
            result = jnp.where(head_of_lane == h, stacked[64 * h : 64 * h + 64], result)
        return result

    for w in range(4):
        cells = slice(64 * w, 64 * w + 64)
        dqkv_s[cells, :D] = (dot(scores_low[cells], ke_s[w]) * SCALE).astype(BF)
        dqkv_s[cells, D : 2 * D] = (own_heads(dot_tn(scores_low[cells], qkv_s[cells, :D])) * SCALE).astype(BF)
        dqkv_s[cells, 2 * D :] = own_heads(dot_tn(probs_low[cells], grad_context[cells])).astype(BF)

    for m in range(3):
        part_grad = dot_tn(normal_low, dqkv_s[:, D * m : D * (m + 1)])
        att_f32[0, pl.ds(m, 256, stride=3), :] = part_grad[:, :128]
        att_f32[1, pl.ds(m, 256, stride=3), :] = part_grad[:, 128:]

    start_mate(att)
    start_xy(mlp)

    grad_norm_in = dot_nt(dqkv_s[...], wqkv_ref[...])
    grad_in = (grad_res + norm_back(grad_norm_in, normed_one, inv_one, gain_one)).astype(BF)
    u_row, u_col = window_cell(iota((CELLS, CELLS), 1))
    place_main = one_hot((u_col < 28) & (iota((CELLS, CELLS), 0) == 32 * u_row + u_col + 4))
    v_row, v_col = window_cell(iota((32, CELLS), 1))
    place_edge = one_hot((v_col >= 28) & (iota((32, CELLS), 0) == 4 * v_row + v_col - 28))
    back_main[...] = dot(place_main, grad_in).astype(BF)
    back_rd[...] = dot(place_edge, grad_in).astype(BF)

    start_xy(att)
    hear_ring(1)
    spread_ring(2)

    to_below, to_right, to_last = (x_at, below, col), (x_at, row, right), (x_at, below, right)
    back = []
    for n, (src, dst, device) in enumerate([
        (back_rd.at[pl.ds(16, 16)], got_rd.at[pl.ds(16, 16)], to_last),
        (back_rd.at[pl.ds(0, 16)], got_rd.at[pl.ds(0, 16)], to_right),
        (back_main.at[pl.ds(128, 128)], got_up, to_below),
    ]):
        back.append(send(src, dst, back_ss.at[n], back_rs.at[n], device))

    first_parts, second_parts = [], []
    for b in (mlp, att):
        for copy in b["p2"]:
            copy.wait_recv()
        total = b["x"][x_at].astype(F32)
        for d in range(NX - 1):
            total = total + b["rx"][d].astype(F32)
        first_parts.append(total.reshape(NZ_LO // 2, NY, b["unit"], 128))
        total = b["y"][y_at].astype(F32)
        for d in range(NY - 1):
            total = total + b["ry"][d].astype(F32)
        second_parts.append(total.reshape(NX, NZ_LO // 2 * b["unit"], 128))
    for y in range(NY):
        x3[y, 0:64, :] = first_parts[0][:, y].reshape(64, 128).astype(BF)
        x3[y, 64:96, :] = first_parts[1][:, y].reshape(32, 128).astype(BF)
    for x in range(NX):
        y3[x, 0:64, :] = second_parts[0][x].astype(BF)
        y3[x, 64:96, :] = second_parts[1][x].astype(BF)
    swaps = []
    for d in (2, 1, 3):
        other = (y_at + d) % NY
        swaps.append(send(x3.at[other], rx3.at[d - 1], late_ss.at[d - 1], late_rs.at[d - 1], at_y(other)))
        other = (x_at + d) % NX
        swaps.append(send(y3.at[other], ry3.at[d - 1], late_ss.at[2 + d], late_rs.at[2 + d], at_x(other)))

    for copy in swaps:
        copy.wait_recv()
    hear_ring(2)
    for part, own, own_at, got in ((0, x3, y_at, rx3), (1, y3, x_at, ry3)):
        total = own[own_at].astype(F32)
        for d in range(NX - 1):
            total = total + got[d].astype(F32)
        for lo in range(NZ_LO // 2):
            for hi in range(NZ_HI):
                at_mlp, at_att = 16 * lo + 8 * hi, 64 + 8 * lo + 4 * hi
                piece = jnp.concatenate(
                    [total[at_mlp : at_mlp + 8], total[at_att : at_att + 4], jnp.zeros((4, 128), F32)], axis=0
                )
                z_send[part * (NZ_LO // 2) + lo, hi] = piece.astype(BF)
    ring = []
    for d in (8, 7, 9, 6, 10, 5, 11, 4, 12, 3, 13, 2, 14, 1, 15):
        other = (z_at + d) % NZ
        ring.append(
            send(
                z_send.at[other % NZ_LO, other // NZ_LO], z_recv.at[d - 1],
                z_ss.at[d - 1], z_rs.at[d - 1], at_z(other),
            )
        )

    for copy in back:
        copy.wait_recv()
    spread = one_hot(iota((128, 16), 0) == 32 * (iota((128, 16), 1) >> 2) + (iota((128, 16), 1) & 3))
    out_ref[0:128, :] = (got_up[...].astype(F32) + dot(spread, got_rd[16:32, :])).astype(BF)
    out_ref[128:256, :] = (back_main[0:128, :].astype(F32) + dot(spread, got_rd[0:16, :])).astype(BF)

    for copy in ring:
        copy.wait_recv()
    total = z_send[z_lo, z_hi].astype(F32)
    for d in range(NZ - 1):
        total = total + z_recv[d].astype(F32)
    for k in range(2):
        c_send[k] = jnp.concatenate(
            [total[4 * k : 4 * k + 4], total[8 + 2 * k : 10 + 2 * k], total[12:14]], axis=0
        )
    last = send(c_send.at[mate], c_recv, late_ss.at[6], late_rs.at[6], at_mate())
    last.wait_recv()
    own, got = c_send[core], c_recv[...]
    first, second = jnp.where(core == 0, own, got), jnp.where(core == 0, got, own)
    apart = jnp.concatenate([first[0:4], second[0:4]], axis=0)
    mixed = jnp.concatenate([part[i : i + 1] for i in range(4) for part in (first, second)], axis=0)
    mlp_ref[...] = jnp.where(x_at < 2, apart, mixed)
    att_ref[...] = jnp.concatenate([first[4:5], second[4:5], first[5:6], second[5:6]], axis=0)

    for copy in halo + back + sends + swaps + ring + [last]:
        copy.wait_send()


def reduce_scratch(unit):
    chip_rows = NZ_LO * NY * unit
    half = chip_rows // 2
    return [
        pltpu.VMEM((2, NX * chip_rows, 128), F32),
        pltpu.VMEM((NX * chip_rows, 128), BF),
        pltpu.VMEM((NX * chip_rows, 128), BF),
        pltpu.VMEM((NX, half, 128), BF),
        pltpu.VMEM((NY, half, 128), BF),
        pltpu.VMEM((NX - 1, half, 128), BF),
        pltpu.VMEM((NY - 1, half, 128), BF),
    ]


def on_device(
    hidden_in, token_ids, embed, norm1_gain, norm2_gain, w_qkv, rel_bias, w_proj, w_up, w_down, out_grad
):
    dma = pltpu.SemaphoreType.DMA
    operands = (
        hidden_in.reshape(CELLS, D),
        token_ids.reshape(8, 32),
        embed,
        norm1_gain.reshape(1, D),
        norm2_gain.reshape(1, D),
        w_qkv,
        rel_bias,
        w_proj,
        w_up,
        w_down,
        out_grad.reshape(CELLS, D),
    )
    chunk = NZ_LO // 2 * (MLP_UNIT + ATT_UNIT)
    grad_out, attention_grads, mlp_grads = pl.pallas_call(
        kernel,
        out_shape=(
            jax.ShapeDtypeStruct((CELLS, D), BF),
            jax.ShapeDtypeStruct((4, 128), F32),
            jax.ShapeDtypeStruct((8, 128), F32),
        ),
        in_specs=[pl.BlockSpec(memory_space=pltpu.HBM)] * len(operands),
        out_specs=[pl.BlockSpec(memory_space=pltpu.VMEM)] * 3,
        scratch_shapes=[pltpu.VMEM(operand.shape, operand.dtype) for operand in operands]
        + [
            pltpu.VMEM((32, D), BF),
            pltpu.VMEM((32, D), BF),
            pltpu.VMEM((128, D), BF),
            pltpu.VMEM((128, D), BF),
            pltpu.VMEM((32, D), BF),
            pltpu.VMEM((32, D), BF),
            pltpu.VMEM((3, 8, 32), jnp.int32),
            pltpu.VMEM((64, 512), F32),
            pltpu.VMEM((CELLS, 512), F32),
            pltpu.VMEM((4, 512, D), BF),
            pltpu.VMEM((4, 512, D), BF),
            pltpu.VMEM((CELLS, 3 * D), BF),
            pltpu.VMEM((CELLS, D), BF),
            pltpu.VMEM((CELLS, 3 * D), BF),
            pltpu.VMEM((CELLS, D), BF),
            pltpu.VMEM((32, D), BF),
            pltpu.VMEM((128, D), BF),
            pltpu.VMEM((32, D), BF),
        ]
        + reduce_scratch(MLP_UNIT)
        + reduce_scratch(ATT_UNIT)
        + [
            pltpu.VMEM((NY, chunk, 128), BF),
            pltpu.VMEM((NX, chunk, 128), BF),
            pltpu.VMEM((NY - 1, chunk, 128), BF),
            pltpu.VMEM((NX - 1, chunk, 128), BF),
            pltpu.VMEM((NZ_LO, NZ_HI, 16, 128), BF),
            pltpu.VMEM((NZ - 1, 16, 128), BF),
            pltpu.VMEM((2, 8, 128), F32),
            pltpu.VMEM((8, 128), F32),
        ]
        + [dma((len(operands),)), dma((9,)), dma((9,)), dma((3,)), dma((3,))]
        + [dma((7,))] * 6
        + [dma((NZ - 1,))] * 2
        + [pltpu.SemaphoreType.REGULAR((3,))],
        compiler_params=pltpu.CompilerParams(
            collective_id=0, has_side_effects=True, vmem_limit_bytes=62 * 1024 * 1024
        ),
        name="decoder_block_backward",
    )(*operands)
    return grad_out.reshape(1, 8, 32, D), attention_grads, mlp_grads


def solution(mesh):
    placed = (
        P("dp", "row", "col", None),
        P("dp", "row", "col"),
        P(),
        P(),
        P(),
        P(),
        P(),
        P(),
        P(),
        P(),
        P("dp", "row", "col", None),
    )
    return jax.shard_map(
        on_device,
        mesh=mesh,
        in_specs=placed,
        out_specs=(
            P("dp", "row", "col", None),
            P(("dp", "row", "col"), None),
            P(("dp", "row", "col"), None),
        ),
        check_vma=False,
    )
```

```python
import jax
import jax.numpy as jnp
from jax import lax
from jax.experimental import pallas as pl
from jax.experimental.pallas import tpu as pltpu
from jax.sharding import PartitionSpec as P

D = 256
FF = 1024
HEADS = 8
HEAD_DIM = 32
WIN = 8
PAIRS = 225
CELLS = 256
NORM_EPS = 1e-05
GELU_SCALE = 0.7978845608028654
GELU_CUBIC = 0.044715
SCALE = HEAD_DIM ** (-0.5)

NX, NY, NZ_LO, NZ_HI = 4, 4, 8, 2
NZ = NZ_LO * NZ_HI
ROW_DEVICES, COL_DEVICES = NZ_LO * NY, NZ_HI * 2
MLP_UNIT, ATT_UNIT = 16, 8

MESH = pl.DeviceIdType.MESH
BF = jnp.bfloat16
F32 = jnp.float32


def iota(shape, dim):
    return lax.broadcasted_iota(jnp.int32, shape, dim)


def one_hot(condition):
    return jnp.where(condition, 1.0, 0.0).astype(BF)


def dot(left, right):
    return jnp.dot(left, right, preferred_element_type=F32)


def dot_nt(left, right):
    return lax.dot_general(left, right, (((1,), (1,)), ((), ())), preferred_element_type=F32)


def dot_tn(left, right):
    return lax.dot_general(left, right, (((0,), (0,)), ((), ())), preferred_element_type=F32)


def mean_of(values):
    return jnp.mean(values, axis=-1, keepdims=True)


def layer_norm(values):
    center = values - mean_of(values)
    inv_std = lax.rsqrt(mean_of(center * center) + NORM_EPS)
    return center * inv_std, inv_std


def norm_back(upstream, normed, inv_std, gain):
    scaled = upstream * gain
    return inv_std * (scaled - mean_of(scaled) - normed * mean_of(scaled * normed))


def window_cell(token):
    return token & 7, ((token >> 6) << 3) + ((token >> 3) & 7)


def block_sum(values, ones_pair):
    high = values.astype(BF)
    low = (values - high.astype(F32)).astype(BF)
    parts = []
    for j in range(4):
        lanes = slice(128 * j, 128 * (j + 1))
        parts.append(dot(jnp.concatenate([high[:, lanes], low[:, lanes]], axis=1), ones_pair))
    return jnp.concatenate(parts, axis=1)


def load_rel_bias(rb):
    rb_high = rb.astype(BF)
    rb_rest = rb - rb_high.astype(F32)
    rb_mid = rb_rest.astype(BF)
    rb_low = (rb_rest - rb_mid.astype(F32)).astype(BF)
    parts = jnp.concatenate([rb_high, rb_mid, rb_low], axis=0)
    pair, lane = iota((PAIRS, 2048), 0), iota((PAIRS, 2048), 1)
    offset = lane & 15
    spread = dot(parts, one_hot((offset < 15) & (pair == 15 * (lane >> 7) + offset)))
    spread = spread[0:8] + spread[8:16] + spread[16:24]
    own = iota((8, 2048), 0) == ((iota((8, 2048), 1) >> 4) & 7)
    line = jnp.sum(jnp.where(own, spread, 0.0), axis=0, keepdims=True)
    return jnp.concatenate([line[:, 128 * u : 128 * u + 128] for u in range(16)], axis=0)


def kernel(
    hid_in, tok_in, emb_in, g1_in, g2_in, wqkv_in, rb_in, wproj_in, wup_in, wdown_in, og_in,
    out_ref, att_ref, mlp_ref,
    hid_ref, tok_ref, emb_ref, g1_ref, g2_ref, wqkv_ref, rb_ref, wproj_ref, wup_ref, wdown_ref, og_ref,
    stage_hid, stage_og, halo_hid, halo_og, edge_hid, edge_og, halo_tok,
    bias_s, probs_s, ke_s, ve_s, qkv_s, ctx_s, dqkv_s, back_main, back_rd, got_up, got_rd,
    mlp_f32, mlp_send, mlp_recv, mlp_x, mlp_y, mlp_rx, mlp_ry,
    att_f32, att_send, att_recv, att_x, att_y, att_rx, att_ry,
    x3, y3, rx3, ry3, z_send, z_recv, c_send, c_recv,
    in_sem, halo_ss, halo_rs, back_ss, back_rs, mlp_ss, mlp_rs, att_ss, att_rs, late_ss, late_rs, z_ss, z_rs, ring_sem, pass_ss, go_sem,
):
    loads = [
        pltpu.make_async_copy(src, dst, in_sem.at[n])
        for n, (src, dst) in enumerate([
            (hid_in, hid_ref), (og_in, og_ref), (tok_in, tok_ref), (rb_in, rb_ref), (emb_in, emb_ref),
            (g1_in, g1_ref), (g2_in, g2_ref), (wqkv_in, wqkv_ref), (wproj_in, wproj_ref),
            (wup_in, wup_ref), (wdown_in, wdown_ref),
        ])
    ]
    for load in loads:
        load.start()

    x_at, row, col = lax.axis_index("dp"), lax.axis_index("row"), lax.axis_index("col")
    z_lo, y_at = row // NY, row % NY
    z_hi, core = col // 2, col % 2
    z_at = z_hi * NZ_LO + z_lo
    mate = 1 - core

    above = (row + ROW_DEVICES - 1) % ROW_DEVICES
    below = (row + 1) % ROW_DEVICES
    left = (col + COL_DEVICES - 1) % COL_DEVICES
    right = (col + 1) % COL_DEVICES

    def at_mate():
        return (x_at, row, z_hi * 2 + mate)

    def at_x(other):
        return (other, row, col)

    def at_y(other):
        return (x_at, z_lo * NY + other, col)

    def at_z(other):
        return (x_at, (other % NZ_LO) * NY + y_at, (other // NZ_LO) * 2 + core)

    row_first = 1 - (row + ROW_DEVICES - 1) // ROW_DEVICES
    col_first = 1 - (col + COL_DEVICES - 1) // COL_DEVICES
    row_last, col_last = row == ROW_DEVICES - 1, col == COL_DEVICES - 1
    half_way = ROW_DEVICES // 2
    relay = (x_at, (row + half_way) % ROW_DEVICES, 0)
    is_relay = col == 0
    post = (x_at, half_way + col, 1)
    post_col = row - half_way
    is_post = jnp.logical_and(col == 1, jnp.logical_and(row >= half_way, row < half_way + COL_DEVICES))
    is_corner_post = jnp.logical_and(is_post, row % 2 == 1)
    corner_by_post = jnp.logical_and(row_last, core == 0)
    mail_corner = 1 - (1 - col_first) * (1 - row_first * core)
    far_left = (x_at, relay[1], COL_DEVICES - 1)
    far_corner = (x_at, (relay[1] + ROW_DEVICES - 1) % ROW_DEVICES, COL_DEVICES - 1)
    far_above = (x_at, ROW_DEVICES - 1, post_col)
    far_above_left = (x_at, ROW_DEVICES - 1, (post_col + COL_DEVICES - 1) % COL_DEVICES)

    barrier = pltpu.get_barrier_semaphore()

    def enter(*device):
        pl.semaphore_signal(barrier, inc=1, device_id=device, device_id_type=MESH)

    @pl.when(is_relay)
    def _():
        enter(*relay)
        enter(*relay)
        enter(*far_left)
        enter(*far_corner)

    @pl.when(is_post)
    def _():
        enter(x_at, 0, post_col)
        enter(*far_above)

    @pl.when(is_corner_post)
    def _():
        enter(x_at, 0, post_col)
        enter(*far_above_left)

    @pl.when(jnp.logical_not(row_last))
    def _():
        enter(x_at, below, col)

    @pl.when(jnp.logical_not(col_last))
    def _():
        enter(x_at, row, right)

    @pl.when(jnp.logical_not(jnp.logical_or(col_last, corner_by_post)))
    def _():
        enter(x_at, below, right)

    near = [at_mate()]
    near += [at_x((x_at + d) % NX) for d in range(1, NX)]
    near += [at_y((y_at + d) % NY) for d in range(1, NY)]
    near += [at_z((z_at + 1) % NZ), at_z((z_at + NZ - 1) % NZ)]
    for partner in near:
        enter(*partner)

    def spread_ring(n):
        for other in ((z_at + 2**n) % NZ, (z_at + NZ - 2**n) % NZ):
            pl.semaphore_signal(ring_sem.at[n], inc=1, device_id=at_z(other), device_id_type=MESH)

    def hear_ring(n):
        pl.semaphore_wait(ring_sem.at[n], 2)

    def send(src, dst, send_sem, recv_sem, device):
        copy = pltpu.make_async_remote_copy(
            src_ref=src, dst_ref=dst, send_sem=send_sem, recv_sem=recv_sem,
            device_id=device, device_id_type=MESH,
        )
        copy.start()
        return copy

    r32, s256 = iota((32, CELLS), 0), iota((32, CELLS), 1)
    stage_row = jnp.where(r32 < 16, 4, 0) + ((r32 & 15) >> 2)
    pick = one_hot(s256 == stage_row * 32 + (r32 & 3))
    for n in range(3):
        loads[n].wait()
    stage_hid[...] = dot(pick, hid_ref[...]).astype(BF)
    stage_og[...] = dot(pick, og_ref[...]).astype(BF)

    row_end, col_end = (row + 1) // ROW_DEVICES, (col + 1) // COL_DEVICES
    pl.semaphore_wait(barrier, 3 + len(near) + 2 * col_end + row_end + row_end * (1 - core))

    def go(*device):
        pl.semaphore_signal(go_sem, inc=1, device_id=device, device_id_type=MESH)

    @pl.when(col_last)
    def _():
        go(x_at, (row + half_way) % ROW_DEVICES, 0)
        go(x_at, (row + 1 + half_way) % ROW_DEVICES, 0)

    @pl.when(row_last)
    def _():
        go(*post)

    @pl.when(corner_by_post)
    def _():
        go(x_at, half_way + right, 1)

    def blend(flag, one, other):
        return tuple(flag * a + (1 - flag) * b for a, b in zip(one, other))

    to_above = blend(row_first, post, (x_at, above, col))
    to_left = blend(col_first, relay, (x_at, row, left))
    to_corner = blend(col_first, relay, blend(row_first * core, post, (x_at, above, left)))
    corner, edge = pl.ds(16, 16), pl.ds(0, 16)
    messages = [
        (stage_hid.at[corner], lambda k: edge_hid.at[k, corner], mail_corner, to_corner),
        (tok_ref, lambda k: halo_tok.at[k, 2], mail_corner, to_corner),
        (stage_hid.at[edge], lambda k: edge_hid.at[k, edge], col_first, to_left),
        (tok_ref, lambda k: halo_tok.at[k, 1], col_first, to_left),
        (hid_ref.at[pl.ds(0, 128)], lambda k: halo_hid.at[k], row_first, to_above),
        (tok_ref, lambda k: halo_tok.at[k, 0], row_first, to_above),
        (stage_og.at[corner], lambda k: edge_og.at[k, corner], mail_corner, to_corner),
        (stage_og.at[edge], lambda k: edge_og.at[k, edge], col_first, to_left),
        (og_ref.at[pl.ds(0, 128)], lambda k: halo_og.at[k], row_first, to_above),
    ]
    halo = [
        send(src, dst(mail), halo_ss.at[n], halo_rs.at[len(messages) * mail + n], device)
        for n, (src, dst, mail, device) in enumerate(messages)
    ]

    def passing(n, device):
        dst = messages[n][1]
        return pltpu.make_async_remote_copy(
            src_ref=dst(1), dst_ref=dst(0), send_sem=pass_ss.at[n], recv_sem=halo_rs.at[n],
            device_id=device, device_id_type=MESH,
        )

    def arrived(n, k):
        dst = messages[n][1]
        pltpu.make_async_remote_copy(
            src_ref=dst(k), dst_ref=dst(k), send_sem=pass_ss.at[n], recv_sem=halo_rs.at[len(messages) * k + n],
            device_id=at_mate(), device_id_type=MESH,
        ).wait_recv()

    passes = [
        (is_relay, 2, [(0, far_corner), (1, far_corner), (2, far_left), (3, far_left), (6, far_corner), (7, far_left)]),
        (is_post, 1 + row % 2, []),
        (is_corner_post, None, [(0, far_above_left), (1, far_above_left)]),
        (is_post, None, [(4, far_above), (5, far_above), (8, far_above)]),
        (is_corner_post, None, [(6, far_above_left)]),
    ]

    spread_ring(0)

    loads[3].wait()
    rb = load_rel_bias(rb_ref[...])
    wide_row, wide_lane = iota((128, 512), 0), iota((128, 512), 1)
    pair_sum = jnp.where(
        (wide_row >> 4) == (wide_lane >> 6), (wide_row & 15) + ((wide_lane >> 3) & 7), -1
    )
    rb_high = rb.astype(BF)
    rb_rest = rb - rb_high.astype(F32)
    rb_mid = rb_rest.astype(BF)
    rb_low = (rb_rest - rb_mid.astype(F32)).astype(BF)
    rb_parts = jnp.concatenate([rb_high, rb_mid, rb_low], axis=0)
    key_row = iota((8, 512), 1) & 7
    for qj in range(8):
        tall = dot(rb_parts, one_hot(pair_sum == qj + 7))
        tall = tall[0:16] + tall[16:32] + tall[32:48]
        rows = jnp.zeros((8, 512), F32)
        for ki in range(8):
            rows = jnp.where(key_row == ki, tall[7 - ki : 15 - ki], rows)
        bias_s[8 * qj : 8 * qj + 8, :] = rows

    t_row, t_col = window_cell(iota((CELLS, CELLS), 0))
    s_lane = iota((CELLS, CELLS), 1)
    pick_main = one_hot((t_col < 28) & (s_lane == 32 * t_row + t_col + 4))
    e_row, e_col = window_cell(iota((CELLS, 32), 0))
    pick_edge = one_hot((e_col >= 28) & (iota((CELLS, 32), 1) == 4 * e_row + e_col - 28))
    for load in loads[4:]:
        load.wait()

    for condition, signals, steps in passes:

        @pl.when(condition)
        def _():
            if signals is not None:
                pl.semaphore_wait(go_sem, signals)
            for n, device in steps:
                arrived(n, 1)
                passing(n, device).start()

    for n in range(6):
        arrived(n, 0)
    tok = tok_ref[...]
    tok_below, tok_right, tok_corner = halo_tok[0, 0], halo_tok[0, 1], halo_tok[0, 2]
    tok_main = jnp.concatenate(
        [tok[4 + i : 5 + i, :] for i in range(4)] + [tok_below[i : i + 1, :] for i in range(4)], axis=1
    )
    tok_edge = jnp.concatenate(
        [tok_right[4 + i : 5 + i, 0:4] for i in range(4)] + [tok_corner[i : i + 1, 0:4] for i in range(4)],
        axis=1,
    )
    tok_main = jnp.broadcast_to(tok_main.astype(F32), (128, CELLS)).astype(BF)
    tok_edge = jnp.broadcast_to(tok_edge.astype(F32), (128, 32)).astype(BF)
    ids = dot_nt(pick_main, tok_main) + dot_nt(pick_edge, tok_edge)
    ids = jnp.concatenate([ids, ids], axis=1)
    emb = emb_ref[...].astype(F32)
    token_part = jnp.where(
        ids < 1.5,
        jnp.where(ids < 0.5, emb[0:1], emb[1:2]),
        jnp.where(ids < 2.5, emb[2:3], emb[3:4]),
    )
    main_hid = jnp.concatenate([hid_ref[128:256, :], halo_hid[0]], axis=0)
    resid_in = dot(pick_main, main_hid) + dot(pick_edge, edge_hid[0]) + token_part
    normed_one, inv_one = layer_norm(resid_in)
    gain_one = g1_ref[...]
    normal_low = (normed_one * gain_one).astype(BF)

    qkv_s[...] = dot(normal_low, wqkv_ref[...]).astype(BF)

    head_mask = one_hot((iota((512, D), 0) >> 6) == (iota((512, D), 1) >> 5))
    ones_pair = one_hot(((iota((256, 128), 0) & 127) >> 6) == (iota((256, 128), 1) >> 6))
    for w in range(4):
        cells = slice(64 * w, 64 * w + 64)
        keys = jnp.concatenate([qkv_s[cells, D : 2 * D]] * HEADS, axis=0) * head_mask
        ke_s[w] = keys
        ve_s[w] = jnp.concatenate([qkv_s[cells, 2 * D :]] * HEADS, axis=0) * head_mask
        probs_s[cells, :] = jnp.exp(dot_nt(qkv_s[cells, :D], keys) * SCALE + bias_s[...])
    raised = probs_s[...]
    probs = raised / block_sum(raised, ones_pair)
    probs_s[...] = probs
    probs_low = probs.astype(BF)
    for w in range(4):
        cells = slice(64 * w, 64 * w + 64)
        ctx_s[cells, :] = dot(probs_low[cells], ve_s[w]).astype(BF)

    context = ctx_s[...]
    resid_mid = resid_in + dot(context, wproj_ref[...])
    normed_two, inv_two = layer_norm(resid_mid)
    gain_two = g2_ref[...]
    mlp_in = (normed_two * gain_two).astype(BF)

    for n in range(6, 9):
        arrived(n, 0)
    main_og = jnp.concatenate([og_ref[128:256, :], halo_og[0]], axis=0)
    grad_f32 = dot(pick_main, main_og) + dot(pick_edge, edge_og[0])
    grad = grad_f32.astype(BF)

    grad_mid = jnp.zeros((CELLS, D), F32)
    for n in range(4):
        units = slice(256 * n, 256 * n + 256)
        pre = dot(mlp_in, wup_ref[:, units])
        grad_act = dot_nt(grad, wdown_ref[units, :])
        square = pre * pre
        tanh_part = jnp.tanh(GELU_SCALE * pre * (1.0 + GELU_CUBIC * square))
        half_plus = 0.5 * (1.0 + tanh_part)
        slope = half_plus + 0.5 * pre * (1.0 - tanh_part * tanh_part) * (
            GELU_SCALE * (1.0 + 3.0 * GELU_CUBIC * square)
        )
        act = (pre * half_plus).astype(BF)
        grad_pre = (grad_act * slope).astype(BF)
        grad_mid = grad_mid + dot_nt(grad_pre, wup_ref[:, units])
        up_grad = dot_tn(mlp_in, grad_pre)
        half, lane_tile = n // 2, 2 * (n % 2)
        mlp_f32[half, pl.ds(lane_tile, 256, stride=4), :] = up_grad[:, :128]
        mlp_f32[half, pl.ds(lane_tile + 1, 256, stride=4), :] = up_grad[:, 128:]
        down_grad = dot_tn(act, grad)
        mlp_f32[0, 1024 + 256 * n : 1280 + 256 * n, :] = down_grad[:, :128]
        mlp_f32[1, 1024 + 256 * n : 1280 + 256 * n, :] = down_grad[:, 128:]

    mlp = dict(
        unit=MLP_UNIT, f32=mlp_f32, send=mlp_send, recv=mlp_recv, x=mlp_x, y=mlp_y, rx=mlp_rx, ry=mlp_ry,
        ss=mlp_ss, rs=mlp_rs,
    )
    att = dict(
        unit=ATT_UNIT, f32=att_f32, send=att_send, recv=att_recv, x=att_x, y=att_y, rx=att_rx, ry=att_ry,
        ss=att_ss, rs=att_rs,
    )
    sends = []

    def start_mate(b):
        b["send"][...] = b["f32"][mate].astype(BF)
        b["p1"] = [send(b["send"], b["recv"], b["ss"].at[0], b["rs"].at[0], at_mate())]
        sends.extend(b["p1"])

    def start_xy(b):
        b["p1"][0].wait_recv()
        unit = b["unit"]
        part = NZ_LO // 2 * NY * unit
        quarter = part // NY
        for x in range(NX):
            first, second = slice(2 * part * x, 2 * part * x + part), slice(2 * part * x + part, 2 * part * (x + 1))
            total = b["f32"][core, first, :] + b["recv"][first, :].astype(F32)
            b["x"][x] = total.astype(BF)
            total = b["f32"][core, second, :] + b["recv"][second, :].astype(F32)
            total = total.reshape(NZ_LO // 2, NY, unit, 128)
            for y in range(NY):
                b["y"][y, quarter * x : quarter * (x + 1), :] = total[:, y].reshape(quarter, 128).astype(BF)
        b["p2"] = []
        for d in (2, 1, 3):
            other = (x_at + d) % NX
            b["p2"].append(
                send(b["x"].at[other], b["rx"].at[d - 1], b["ss"].at[d], b["rs"].at[d], at_x(other))
            )
            other = (y_at + d) % NY
            b["p2"].append(
                send(b["y"].at[other], b["ry"].at[d - 1], b["ss"].at[3 + d], b["rs"].at[3 + d], at_y(other))
            )
        sends.extend(b["p2"])

    start_mate(mlp)
    hear_ring(0)
    spread_ring(1)

    grad_res = grad_f32 + norm_back(grad_mid, normed_two, inv_two, gain_two)
    grad_res_low = grad_res.astype(BF)
    proj_grad = dot_tn(context, grad_res_low)
    att_f32[0, 768:, :] = proj_grad[:, :128]
    att_f32[1, 768:, :] = proj_grad[:, 128:]
    grad_context = dot_nt(grad_res_low, wproj_ref[...]).astype(BF)

    grad_probs = jnp.concatenate(
        [dot_nt(grad_context[64 * w : 64 * w + 64], ve_s[w]) for w in range(4)], axis=0
    )
    probs = probs_s[...]
    grad_scores = probs * (grad_probs - block_sum(probs * grad_probs, ones_pair))
    scores_low = grad_scores.astype(BF)
    probs_low = probs.astype(BF)

    head_of_lane = iota((64, D), 1) >> 5

    def own_heads(stacked):
        result = jnp.zeros((64, D), F32)
        for h in range(HEADS):
            result = jnp.where(head_of_lane == h, stacked[64 * h : 64 * h + 64], result)
        return result

    for w in range(4):
        cells = slice(64 * w, 64 * w + 64)
        dqkv_s[cells, :D] = (dot(scores_low[cells], ke_s[w]) * SCALE).astype(BF)
        dqkv_s[cells, D : 2 * D] = (own_heads(dot_tn(scores_low[cells], qkv_s[cells, :D])) * SCALE).astype(BF)
        dqkv_s[cells, 2 * D :] = own_heads(dot_tn(probs_low[cells], grad_context[cells])).astype(BF)

    for m in range(3):
        part_grad = dot_tn(normal_low, dqkv_s[:, D * m : D * (m + 1)])
        att_f32[0, pl.ds(m, 256, stride=3), :] = part_grad[:, :128]
        att_f32[1, pl.ds(m, 256, stride=3), :] = part_grad[:, 128:]

    start_mate(att)
    start_xy(mlp)

    grad_norm_in = dot_nt(dqkv_s[...], wqkv_ref[...])
    grad_in = (grad_res + norm_back(grad_norm_in, normed_one, inv_one, gain_one)).astype(BF)
    u_row, u_col = window_cell(iota((CELLS, CELLS), 1))
    place_main = one_hot((u_col < 28) & (iota((CELLS, CELLS), 0) == 32 * u_row + u_col + 4))
    v_row, v_col = window_cell(iota((32, CELLS), 1))
    place_edge = one_hot((v_col >= 28) & (iota((32, CELLS), 0) == 4 * v_row + v_col - 28))
    back_main[...] = dot(place_main, grad_in).astype(BF)
    back_rd[...] = dot(place_edge, grad_in).astype(BF)

    start_xy(att)
    hear_ring(1)
    spread_ring(2)

    to_below, to_right, to_last = (x_at, below, col), (x_at, row, right), (x_at, below, right)
    back = []
    for n, (src, dst, device) in enumerate([
        (back_rd.at[pl.ds(16, 16)], got_rd.at[pl.ds(16, 16)], to_last),
        (back_rd.at[pl.ds(0, 16)], got_rd.at[pl.ds(0, 16)], to_right),
        (back_main.at[pl.ds(128, 128)], got_up, to_below),
    ]):
        back.append(send(src, dst, back_ss.at[n], back_rs.at[n], device))

    first_parts, second_parts = [], []
    for b in (mlp, att):
        for copy in b["p2"]:
            copy.wait_recv()
        total = b["x"][x_at].astype(F32)
        for d in range(NX - 1):
            total = total + b["rx"][d].astype(F32)
        first_parts.append(total.reshape(NZ_LO // 2, NY, b["unit"], 128))
        total = b["y"][y_at].astype(F32)
        for d in range(NY - 1):
            total = total + b["ry"][d].astype(F32)
        second_parts.append(total.reshape(NX, NZ_LO // 2 * b["unit"], 128))
    for y in range(NY):
        x3[y, 0:64, :] = first_parts[0][:, y].reshape(64, 128).astype(BF)
        x3[y, 64:96, :] = first_parts[1][:, y].reshape(32, 128).astype(BF)
    for x in range(NX):
        y3[x, 0:64, :] = second_parts[0][x].astype(BF)
        y3[x, 64:96, :] = second_parts[1][x].astype(BF)
    swaps = []
    for d in (2, 1, 3):
        other = (y_at + d) % NY
        swaps.append(send(x3.at[other], rx3.at[d - 1], late_ss.at[d - 1], late_rs.at[d - 1], at_y(other)))
        other = (x_at + d) % NX
        swaps.append(send(y3.at[other], ry3.at[d - 1], late_ss.at[2 + d], late_rs.at[2 + d], at_x(other)))

    for copy in swaps:
        copy.wait_recv()
    hear_ring(2)
    for part, own, own_at, got in ((0, x3, y_at, rx3), (1, y3, x_at, ry3)):
        total = own[own_at].astype(F32)
        for d in range(NX - 1):
            total = total + got[d].astype(F32)
        for lo in range(NZ_LO // 2):
            for hi in range(NZ_HI):
                at_mlp, at_att = 16 * lo + 8 * hi, 64 + 8 * lo + 4 * hi
                piece = jnp.concatenate(
                    [total[at_mlp : at_mlp + 8], total[at_att : at_att + 4], jnp.zeros((4, 128), F32)], axis=0
                )
                z_send[part * (NZ_LO // 2) + lo, hi] = piece.astype(BF)
    ring = []
    for d in (8, 7, 9, 6, 10, 5, 11, 4, 12, 3, 13, 2, 14, 1, 15):
        other = (z_at + d) % NZ
        ring.append(
            send(
                z_send.at[other % NZ_LO, other // NZ_LO], z_recv.at[d - 1],
                z_ss.at[d - 1], z_rs.at[d - 1], at_z(other),
            )
        )

    for copy in back:
        copy.wait_recv()
    spread = one_hot(iota((128, 16), 0) == 32 * (iota((128, 16), 1) >> 2) + (iota((128, 16), 1) & 3))
    out_ref[0:128, :] = (got_up[...].astype(F32) + dot(spread, got_rd[16:32, :])).astype(BF)
    out_ref[128:256, :] = (back_main[0:128, :].astype(F32) + dot(spread, got_rd[0:16, :])).astype(BF)

    for copy in ring:
        copy.wait_recv()
    total = z_send[z_lo, z_hi].astype(F32)
    for d in range(NZ - 1):
        total = total + z_recv[d].astype(F32)
    for k in range(2):
        c_send[k] = jnp.concatenate(
            [total[4 * k : 4 * k + 4], total[8 + 2 * k : 10 + 2 * k], total[12:14]], axis=0
        )
    last = send(c_send.at[mate], c_recv, late_ss.at[6], late_rs.at[6], at_mate())
    last.wait_recv()
    own, got = c_send[core], c_recv[...]
    first, second = jnp.where(core == 0, own, got), jnp.where(core == 0, got, own)
    apart = jnp.concatenate([first[0:4], second[0:4]], axis=0)
    mixed = jnp.concatenate([part[i : i + 1] for i in range(4) for part in (first, second)], axis=0)
    mlp_ref[...] = jnp.where(x_at < 2, apart, mixed)
    att_ref[...] = jnp.concatenate([first[4:5], second[4:5], first[5:6], second[5:6]], axis=0)

    for copy in halo + back + sends + swaps + ring + [last]:
        copy.wait_send()
    for condition, _, steps in passes:

        @pl.when(condition)
        def _():
            for n, device in steps:
                passing(n, device).wait_send()


def reduce_scratch(unit):
    chip_rows = NZ_LO * NY * unit
    half = chip_rows // 2
    return [
        pltpu.VMEM((2, NX * chip_rows, 128), F32),
        pltpu.VMEM((NX * chip_rows, 128), BF),
        pltpu.VMEM((NX * chip_rows, 128), BF),
        pltpu.VMEM((NX, half, 128), BF),
        pltpu.VMEM((NY, half, 128), BF),
        pltpu.VMEM((NX - 1, half, 128), BF),
        pltpu.VMEM((NY - 1, half, 128), BF),
    ]


def on_device(
    hidden_in, token_ids, embed, norm1_gain, norm2_gain, w_qkv, rel_bias, w_proj, w_up, w_down, out_grad
):
    dma = pltpu.SemaphoreType.DMA
    operands = (
        hidden_in.reshape(CELLS, D),
        token_ids.reshape(8, 32),
        embed,
        norm1_gain.reshape(1, D),
        norm2_gain.reshape(1, D),
        w_qkv,
        rel_bias,
        w_proj,
        w_up,
        w_down,
        out_grad.reshape(CELLS, D),
    )
    chunk = NZ_LO // 2 * (MLP_UNIT + ATT_UNIT)
    grad_out, attention_grads, mlp_grads = pl.pallas_call(
        kernel,
        out_shape=(
            jax.ShapeDtypeStruct((CELLS, D), BF),
            jax.ShapeDtypeStruct((4, 128), F32),
            jax.ShapeDtypeStruct((8, 128), F32),
        ),
        in_specs=[pl.BlockSpec(memory_space=pltpu.HBM)] * len(operands),
        out_specs=[pl.BlockSpec(memory_space=pltpu.VMEM)] * 3,
        scratch_shapes=[pltpu.VMEM(operand.shape, operand.dtype) for operand in operands]
        + [
            pltpu.VMEM((32, D), BF),
            pltpu.VMEM((32, D), BF),
            pltpu.VMEM((2, 128, D), BF),
            pltpu.VMEM((2, 128, D), BF),
            pltpu.VMEM((2, 32, D), BF),
            pltpu.VMEM((2, 32, D), BF),
            pltpu.VMEM((2, 3, 8, 32), jnp.int32),
            pltpu.VMEM((64, 512), F32),
            pltpu.VMEM((CELLS, 512), F32),
            pltpu.VMEM((4, 512, D), BF),
            pltpu.VMEM((4, 512, D), BF),
            pltpu.VMEM((CELLS, 3 * D), BF),
            pltpu.VMEM((CELLS, D), BF),
            pltpu.VMEM((CELLS, 3 * D), BF),
            pltpu.VMEM((CELLS, D), BF),
            pltpu.VMEM((32, D), BF),
            pltpu.VMEM((128, D), BF),
            pltpu.VMEM((32, D), BF),
        ]
        + reduce_scratch(MLP_UNIT)
        + reduce_scratch(ATT_UNIT)
        + [
            pltpu.VMEM((NY, chunk, 128), BF),
            pltpu.VMEM((NX, chunk, 128), BF),
            pltpu.VMEM((NY - 1, chunk, 128), BF),
            pltpu.VMEM((NX - 1, chunk, 128), BF),
            pltpu.VMEM((NZ_LO, NZ_HI, 16, 128), BF),
            pltpu.VMEM((NZ - 1, 16, 128), BF),
            pltpu.VMEM((2, 8, 128), F32),
            pltpu.VMEM((8, 128), F32),
        ]
        + [dma((len(operands),)), dma((9,)), dma((18,)), dma((3,)), dma((3,))]
        + [dma((7,))] * 6
        + [dma((NZ - 1,))] * 2
        + [pltpu.SemaphoreType.REGULAR((3,)), dma((9,)), pltpu.SemaphoreType.REGULAR],
        compiler_params=pltpu.CompilerParams(
            collective_id=0, has_side_effects=True, vmem_limit_bytes=62 * 1024 * 1024
        ),
        name="decoder_block_backward",
    )(*operands)
    return grad_out.reshape(1, 8, 32, D), attention_grads, mlp_grads


def solution(mesh):
    placed = (
        P("dp", "row", "col", None),
        P("dp", "row", "col"),
        P(),
        P(),
        P(),
        P(),
        P(),
        P(),
        P(),
        P(),
        P("dp", "row", "col", None),
    )
    return jax.shard_map(
        on_device,
        mesh=mesh,
        in_specs=placed,
        out_specs=(
            P("dp", "row", "col", None),
            P(("dp", "row", "col"), None),
            P(("dp", "row", "col"), None),
        ),
        check_vma=False,
    )
```

```python
import jax
import jax.numpy as jnp
from jax import lax
from jax.experimental import pallas as pl
from jax.experimental.pallas import tpu as pltpu
from jax.sharding import PartitionSpec as P

D = 256
FF = 1024
HEADS = 8
HEAD_DIM = 32
WIN = 8
PAIRS = 225
CELLS = 256
NORM_EPS = 1e-05
GELU_SCALE = 0.7978845608028654
GELU_CUBIC = 0.044715
SCALE = HEAD_DIM ** (-0.5)

NX, NY, NZ_LO, NZ_HI = 4, 4, 8, 2
NZ = NZ_LO * NZ_HI
ROW_DEVICES, COL_DEVICES = NZ_LO * NY, NZ_HI * 2
MLP_UNIT, ATT_UNIT = 16, 8

MESH = pl.DeviceIdType.MESH
BF = jnp.bfloat16
F32 = jnp.float32


def iota(shape, dim):
    return lax.broadcasted_iota(jnp.int32, shape, dim)


def one_hot(condition):
    return jnp.where(condition, 1.0, 0.0).astype(BF)


def dot(left, right):
    return jnp.dot(left, right, preferred_element_type=F32)


def dot_nt(left, right):
    return lax.dot_general(left, right, (((1,), (1,)), ((), ())), preferred_element_type=F32)


def dot_tn(left, right):
    return lax.dot_general(left, right, (((0,), (0,)), ((), ())), preferred_element_type=F32)


def mean_of(values):
    return jnp.mean(values, axis=-1, keepdims=True)


def layer_norm(values):
    center = values - mean_of(values)
    inv_std = lax.rsqrt(mean_of(center * center) + NORM_EPS)
    return center * inv_std, inv_std


def norm_back(upstream, normed, inv_std, gain):
    scaled = upstream * gain
    return inv_std * (scaled - mean_of(scaled) - normed * mean_of(scaled * normed))


def window_cell(token):
    return token & 7, ((token >> 6) << 3) + ((token >> 3) & 7)


def block_sum(values, ones_pair):
    high = values.astype(BF)
    low = (values - high.astype(F32)).astype(BF)
    parts = []
    for j in range(4):
        lanes = slice(128 * j, 128 * (j + 1))
        parts.append(dot(jnp.concatenate([high[:, lanes], low[:, lanes]], axis=1), ones_pair))
    return jnp.concatenate(parts, axis=1)


def load_rel_bias(rb):
    rb_high = rb.astype(BF)
    rb_rest = rb - rb_high.astype(F32)
    rb_mid = rb_rest.astype(BF)
    rb_low = (rb_rest - rb_mid.astype(F32)).astype(BF)
    parts = jnp.concatenate([rb_high, rb_mid, rb_low], axis=0)
    pair, lane = iota((PAIRS, 2048), 0), iota((PAIRS, 2048), 1)
    offset = lane & 15
    spread = dot(parts, one_hot((offset < 15) & (pair == 15 * (lane >> 7) + offset)))
    spread = spread[0:8] + spread[8:16] + spread[16:24]
    own = iota((8, 2048), 0) == ((iota((8, 2048), 1) >> 4) & 7)
    line = jnp.sum(jnp.where(own, spread, 0.0), axis=0, keepdims=True)
    return jnp.concatenate([line[:, 128 * u : 128 * u + 128] for u in range(16)], axis=0)


def kernel(
    hid_in, tok_in, emb_in, g1_in, g2_in, wqkv_in, rb_in, wproj_in, wup_in, wdown_in, og_in,
    out_ref, att_ref, mlp_ref,
    hid_ref, tok_ref, emb_ref, g1_ref, g2_ref, wqkv_ref, rb_ref, wproj_ref, wup_ref, wdown_ref, og_ref,
    stage_hid, stage_og, halo_hid, halo_og, edge_hid, edge_og, halo_tok,
    bias_s, probs_s, ke_s, ve_s, qkv_s, ctx_s, dqkv_s, back_main, back_rd, got_up, got_rd,
    mlp_f32, mlp_send, mlp_recv, mlp_x, mlp_y, mlp_rx, mlp_ry,
    att_f32, att_send, att_recv, att_x, att_y, att_rx, att_ry,
    x3, y3, rx3, ry3, z_send, z_recv, c_send, c_recv,
    in_sem, halo_ss, halo_rs, back_ss, back_rs, mlp_ss, mlp_rs, att_ss, att_rs, late_ss, late_rs, z_ss, z_rs, ring_sem, pass_ss, go_sem,
):
    x_at, row, col = lax.axis_index("dp"), lax.axis_index("row"), lax.axis_index("col")
    z_lo, y_at = row // NY, row % NY
    z_hi, core = col // 2, col % 2
    z_at = z_hi * NZ_LO + z_lo
    mate = 1 - core

    above = (row + ROW_DEVICES - 1) % ROW_DEVICES
    below = (row + 1) % ROW_DEVICES
    left = (col + COL_DEVICES - 1) % COL_DEVICES
    right = (col + 1) % COL_DEVICES

    def at_mate():
        return (x_at, row, z_hi * 2 + mate)

    def at_x(other):
        return (other, row, col)

    def at_y(other):
        return (x_at, z_lo * NY + other, col)

    def at_z(other):
        return (x_at, (other % NZ_LO) * NY + y_at, (other // NZ_LO) * 2 + core)

    row_first = (1 - (row + ROW_DEVICES - 1) // ROW_DEVICES) * (1 - z_hi)
    col_first = 1 - (col + COL_DEVICES - 1) // COL_DEVICES
    row_last, col_last = row == ROW_DEVICES - 1, col == COL_DEVICES - 1
    row_by_post = jnp.logical_and(row_last, z_hi == 0)
    half_way = ROW_DEVICES // 2
    relay = (x_at, (row + half_way) % ROW_DEVICES, 0)
    is_relay = col == 0
    post = (x_at, half_way + col, 1)
    post_col = row - half_way
    is_post = jnp.logical_and(col == 1, jnp.logical_or(row == half_way, row == half_way + 1))
    is_corner_post = jnp.logical_and(is_post, row % 2 == 1)
    corner_by_post = jnp.logical_and(row_last, col == 0)
    mail_corner = 1 - (1 - col_first) * (1 - row_first * core)
    far_left = (x_at, relay[1], COL_DEVICES - 1)
    far_corner = (x_at, (relay[1] + ROW_DEVICES - 1) % ROW_DEVICES, COL_DEVICES - 1)
    far_above = (x_at, ROW_DEVICES - 1, post_col)
    far_above_left = (x_at, ROW_DEVICES - 1, (post_col + COL_DEVICES - 1) % COL_DEVICES)

    barrier = pltpu.get_barrier_semaphore()

    def enter(*device):
        pl.semaphore_signal(barrier, inc=1, device_id=device, device_id_type=MESH)

    @pl.when(is_relay)
    def _():
        enter(*relay)
        enter(*relay)
        enter(*far_left)
        enter(*far_corner)

    @pl.when(is_post)
    def _():
        enter(x_at, 0, post_col)
        enter(*far_above)

    @pl.when(is_corner_post)
    def _():
        enter(x_at, 0, post_col)
        enter(*far_above_left)

    @pl.when(jnp.logical_not(row_by_post))
    def _():
        enter(x_at, below, col)

    @pl.when(jnp.logical_not(col_last))
    def _():
        enter(x_at, row, right)

    @pl.when(jnp.logical_not(jnp.logical_or(col_last, corner_by_post)))
    def _():
        enter(x_at, below, right)

    near = [at_mate()]
    near += [at_x((x_at + d) % NX) for d in range(1, NX)]
    near += [at_y((y_at + d) % NY) for d in range(1, NY)]
    near += [at_z((z_at + 1) % NZ), at_z((z_at + NZ - 1) % NZ)]
    for partner in near:
        enter(*partner)

    loads = [
        pltpu.make_async_copy(src, dst, in_sem.at[n])
        for n, (src, dst) in enumerate([
            (hid_in, hid_ref), (og_in, og_ref), (tok_in, tok_ref), (rb_in, rb_ref), (emb_in, emb_ref),
            (g1_in, g1_ref), (g2_in, g2_ref), (wqkv_in, wqkv_ref), (wproj_in, wproj_ref),
            (wup_in, wup_ref), (wdown_in, wdown_ref),
        ])
    ]
    for load in loads:
        load.start()

    def spread_ring(n):
        for other in ((z_at + 2**n) % NZ, (z_at + NZ - 2**n) % NZ):
            pl.semaphore_signal(ring_sem.at[n], inc=1, device_id=at_z(other), device_id_type=MESH)

    def hear_ring(n):
        pl.semaphore_wait(ring_sem.at[n], 2)

    def send(src, dst, send_sem, recv_sem, device):
        copy = pltpu.make_async_remote_copy(
            src_ref=src, dst_ref=dst, send_sem=send_sem, recv_sem=recv_sem,
            device_id=device, device_id_type=MESH,
        )
        copy.start()
        return copy

    r32, s256 = iota((32, CELLS), 0), iota((32, CELLS), 1)
    stage_row = jnp.where(r32 < 16, 4, 0) + ((r32 & 15) >> 2)
    pick = one_hot(s256 == stage_row * 32 + (r32 & 3))
    for n in range(3):
        loads[n].wait()
    stage_hid[...] = dot(pick, hid_ref[...]).astype(BF)
    stage_og[...] = dot(pick, og_ref[...]).astype(BF)

    row_end, col_end = (row + 1) // ROW_DEVICES * (1 - z_hi), (col + 1) // COL_DEVICES
    pl.semaphore_wait(barrier, 3 + len(near) + 2 * col_end + row_end + row_end * (1 - core))

    def go(*device):
        pl.semaphore_signal(go_sem, inc=1, device_id=device, device_id_type=MESH)

    @pl.when(col_last)
    def _():
        go(x_at, (row + half_way) % ROW_DEVICES, 0)
        go(x_at, (row + 1 + half_way) % ROW_DEVICES, 0)

    @pl.when(row_by_post)
    def _():
        go(*post)

    @pl.when(corner_by_post)
    def _():
        go(x_at, half_way + right, 1)

    def blend(flag, one, other):
        return tuple(flag * a + (1 - flag) * b for a, b in zip(one, other))

    to_above = blend(row_first, post, (x_at, above, col))
    to_left = blend(col_first, relay, (x_at, row, left))
    to_corner = blend(col_first, relay, blend(row_first * core, post, (x_at, above, left)))
    corner, edge = pl.ds(16, 16), pl.ds(0, 16)
    messages = [
        (stage_hid.at[corner], lambda k: edge_hid.at[k, corner], mail_corner, to_corner),
        (tok_ref, lambda k: halo_tok.at[k, 2], mail_corner, to_corner),
        (stage_hid.at[edge], lambda k: edge_hid.at[k, edge], col_first, to_left),
        (tok_ref, lambda k: halo_tok.at[k, 1], col_first, to_left),
        (hid_ref.at[pl.ds(0, 128)], lambda k: halo_hid.at[k], row_first, to_above),
        (tok_ref, lambda k: halo_tok.at[k, 0], row_first, to_above),
        (stage_og.at[corner], lambda k: edge_og.at[k, corner], mail_corner, to_corner),
        (stage_og.at[edge], lambda k: edge_og.at[k, edge], col_first, to_left),
        (og_ref.at[pl.ds(0, 128)], lambda k: halo_og.at[k], row_first, to_above),
    ]
    halo = [
        send(src, dst(mail), halo_ss.at[n], halo_rs.at[len(messages) * mail + n], device)
        for n, (src, dst, mail, device) in enumerate(messages)
    ]

    def passing(n, device):
        dst = messages[n][1]
        return pltpu.make_async_remote_copy(
            src_ref=dst(1), dst_ref=dst(0), send_sem=pass_ss.at[n], recv_sem=halo_rs.at[n],
            device_id=device, device_id_type=MESH,
        )

    def arrived(n, k):
        dst = messages[n][1]
        pltpu.make_async_remote_copy(
            src_ref=dst(k), dst_ref=dst(k), send_sem=pass_ss.at[n], recv_sem=halo_rs.at[len(messages) * k + n],
            device_id=at_mate(), device_id_type=MESH,
        ).wait_recv()

    passes = [
        (is_relay, 2, [(0, far_corner), (1, far_corner), (2, far_left), (3, far_left), (6, far_corner), (7, far_left)]),
        (is_post, 1 + row % 2, []),
        (is_corner_post, None, [(0, far_above_left), (1, far_above_left)]),
        (is_post, None, [(4, far_above), (5, far_above), (8, far_above)]),
        (is_corner_post, None, [(6, far_above_left)]),
    ]

    spread_ring(0)

    loads[3].wait()
    rb = load_rel_bias(rb_ref[...])
    wide_row, wide_lane = iota((128, 512), 0), iota((128, 512), 1)
    pair_sum = jnp.where(
        (wide_row >> 4) == (wide_lane >> 6), (wide_row & 15) + ((wide_lane >> 3) & 7), -1
    )
    rb_high = rb.astype(BF)
    rb_rest = rb - rb_high.astype(F32)
    rb_mid = rb_rest.astype(BF)
    rb_low = (rb_rest - rb_mid.astype(F32)).astype(BF)
    rb_parts = jnp.concatenate([rb_high, rb_mid, rb_low], axis=0)
    key_row = iota((8, 512), 1) & 7
    for qj in range(8):
        tall = dot(rb_parts, one_hot(pair_sum == qj + 7))
        tall = tall[0:16] + tall[16:32] + tall[32:48]
        rows = jnp.zeros((8, 512), F32)
        for ki in range(8):
            rows = jnp.where(key_row == ki, tall[7 - ki : 15 - ki], rows)
        bias_s[8 * qj : 8 * qj + 8, :] = rows

    t_row, t_col = window_cell(iota((CELLS, CELLS), 0))
    s_lane = iota((CELLS, CELLS), 1)
    pick_main = one_hot((t_col < 28) & (s_lane == 32 * t_row + t_col + 4))
    e_row, e_col = window_cell(iota((CELLS, 32), 0))
    pick_edge = one_hot((e_col >= 28) & (iota((CELLS, 32), 1) == 4 * e_row + e_col - 28))
    for load in loads[4:]:
        load.wait()

    for condition, signals, steps in passes:

        @pl.when(condition)
        def _():
            if signals is not None:
                pl.semaphore_wait(go_sem, signals)
            for n, device in steps:
                arrived(n, 1)
                passing(n, device).start()

    for n in range(6):
        arrived(n, 0)
    tok = tok_ref[...]
    tok_below, tok_right, tok_corner = halo_tok[0, 0], halo_tok[0, 1], halo_tok[0, 2]
    tok_main = jnp.concatenate(
        [tok[4 + i : 5 + i, :] for i in range(4)] + [tok_below[i : i + 1, :] for i in range(4)], axis=1
    )
    tok_edge = jnp.concatenate(
        [tok_right[4 + i : 5 + i, 0:4] for i in range(4)] + [tok_corner[i : i + 1, 0:4] for i in range(4)],
        axis=1,
    )
    tok_main = jnp.broadcast_to(tok_main.astype(F32), (128, CELLS)).astype(BF)
    tok_edge = jnp.broadcast_to(tok_edge.astype(F32), (128, 32)).astype(BF)
    ids = dot_nt(pick_main, tok_main) + dot_nt(pick_edge, tok_edge)
    ids = jnp.concatenate([ids, ids], axis=1)
    emb = emb_ref[...].astype(F32)
    token_part = jnp.where(
        ids < 1.5,
        jnp.where(ids < 0.5, emb[0:1], emb[1:2]),
        jnp.where(ids < 2.5, emb[2:3], emb[3:4]),
    )
    main_hid = jnp.concatenate([hid_ref[128:256, :], halo_hid[0]], axis=0)
    resid_in = dot(pick_main, main_hid) + dot(pick_edge, edge_hid[0]) + token_part
    normed_one, inv_one = layer_norm(resid_in)
    gain_one = g1_ref[...]
    normal_low = (normed_one * gain_one).astype(BF)

    qkv_s[...] = dot(normal_low, wqkv_ref[...]).astype(BF)

    head_mask = one_hot((iota((512, D), 0) >> 6) == (iota((512, D), 1) >> 5))
    ones_pair = one_hot(((iota((256, 128), 0) & 127) >> 6) == (iota((256, 128), 1) >> 6))
    for w in range(4):
        cells = slice(64 * w, 64 * w + 64)
        keys = jnp.concatenate([qkv_s[cells, D : 2 * D]] * HEADS, axis=0) * head_mask
        ke_s[w] = keys
        ve_s[w] = jnp.concatenate([qkv_s[cells, 2 * D :]] * HEADS, axis=0) * head_mask
        probs_s[cells, :] = jnp.exp(dot_nt(qkv_s[cells, :D], keys) * SCALE + bias_s[...])
    raised = probs_s[...]
    probs = raised / block_sum(raised, ones_pair)
    probs_s[...] = probs
    probs_low = probs.astype(BF)
    for w in range(4):
        cells = slice(64 * w, 64 * w + 64)
        ctx_s[cells, :] = dot(probs_low[cells], ve_s[w]).astype(BF)

    context = ctx_s[...]
    resid_mid = resid_in + dot(context, wproj_ref[...])
    normed_two, inv_two = layer_norm(resid_mid)
    gain_two = g2_ref[...]
    mlp_in = (normed_two * gain_two).astype(BF)

    for n in range(6, 9):
        arrived(n, 0)
    main_og = jnp.concatenate([og_ref[128:256, :], halo_og[0]], axis=0)
    grad_f32 = dot(pick_main, main_og) + dot(pick_edge, edge_og[0])
    grad = grad_f32.astype(BF)

    grad_mid = jnp.zeros((CELLS, D), F32)
    for n in range(4):
        units = slice(256 * n, 256 * n + 256)
        pre = dot(mlp_in, wup_ref[:, units])
        grad_act = dot_nt(grad, wdown_ref[units, :])
        square = pre * pre
        tanh_part = jnp.tanh(GELU_SCALE * pre * (1.0 + GELU_CUBIC * square))
        half_plus = 0.5 * (1.0 + tanh_part)
        slope = half_plus + 0.5 * pre * (1.0 - tanh_part * tanh_part) * (
            GELU_SCALE * (1.0 + 3.0 * GELU_CUBIC * square)
        )
        act = (pre * half_plus).astype(BF)
        grad_pre = (grad_act * slope).astype(BF)
        grad_mid = grad_mid + dot_nt(grad_pre, wup_ref[:, units])
        up_grad = dot_tn(mlp_in, grad_pre)
        half, lane_tile = n // 2, 2 * (n % 2)
        mlp_f32[half, pl.ds(lane_tile, 256, stride=4), :] = up_grad[:, :128]
        mlp_f32[half, pl.ds(lane_tile + 1, 256, stride=4), :] = up_grad[:, 128:]
        down_grad = dot_tn(act, grad)
        mlp_f32[0, 1024 + 256 * n : 1280 + 256 * n, :] = down_grad[:, :128]
        mlp_f32[1, 1024 + 256 * n : 1280 + 256 * n, :] = down_grad[:, 128:]

    mlp = dict(
        unit=MLP_UNIT, f32=mlp_f32, send=mlp_send, recv=mlp_recv, x=mlp_x, y=mlp_y, rx=mlp_rx, ry=mlp_ry,
        ss=mlp_ss, rs=mlp_rs,
    )
    att = dict(
        unit=ATT_UNIT, f32=att_f32, send=att_send, recv=att_recv, x=att_x, y=att_y, rx=att_rx, ry=att_ry,
        ss=att_ss, rs=att_rs,
    )
    sends = []

    def start_mate(b):
        b["send"][...] = b["f32"][mate].astype(BF)
        b["p1"] = [send(b["send"], b["recv"], b["ss"].at[0], b["rs"].at[0], at_mate())]
        sends.extend(b["p1"])

    def start_xy(b):
        b["p1"][0].wait_recv()
        unit = b["unit"]
        part = NZ_LO // 2 * NY * unit
        quarter = part // NY
        for x in range(NX):
            first, second = slice(2 * part * x, 2 * part * x + part), slice(2 * part * x + part, 2 * part * (x + 1))
            total = b["f32"][core, first, :] + b["recv"][first, :].astype(F32)
            b["x"][x] = total.astype(BF)
            total = b["f32"][core, second, :] + b["recv"][second, :].astype(F32)
            total = total.reshape(NZ_LO // 2, NY, unit, 128)
            for y in range(NY):
                b["y"][y, quarter * x : quarter * (x + 1), :] = total[:, y].reshape(quarter, 128).astype(BF)
        b["p2"] = []
        for d in (2, 1, 3):
            other = (x_at + d) % NX
            b["p2"].append(
                send(b["x"].at[other], b["rx"].at[d - 1], b["ss"].at[d], b["rs"].at[d], at_x(other))
            )
            other = (y_at + d) % NY
            b["p2"].append(
                send(b["y"].at[other], b["ry"].at[d - 1], b["ss"].at[3 + d], b["rs"].at[3 + d], at_y(other))
            )
        sends.extend(b["p2"])

    start_mate(mlp)
    hear_ring(0)
    spread_ring(1)

    grad_res = grad_f32 + norm_back(grad_mid, normed_two, inv_two, gain_two)
    grad_res_low = grad_res.astype(BF)
    proj_grad = dot_tn(context, grad_res_low)
    att_f32[0, 768:, :] = proj_grad[:, :128]
    att_f32[1, 768:, :] = proj_grad[:, 128:]
    grad_context = dot_nt(grad_res_low, wproj_ref[...]).astype(BF)

    grad_probs = jnp.concatenate(
        [dot_nt(grad_context[64 * w : 64 * w + 64], ve_s[w]) for w in range(4)], axis=0
    )
    probs = probs_s[...]
    grad_scores = probs * (grad_probs - block_sum(probs * grad_probs, ones_pair))
    scores_low = grad_scores.astype(BF)
    probs_low = probs.astype(BF)

    head_of_lane = iota((64, D), 1) >> 5

    def own_heads(stacked):
        result = jnp.zeros((64, D), F32)
        for h in range(HEADS):
            result = jnp.where(head_of_lane == h, stacked[64 * h : 64 * h + 64], result)
        return result

    for w in range(4):
        cells = slice(64 * w, 64 * w + 64)
        dqkv_s[cells, :D] = (dot(scores_low[cells], ke_s[w]) * SCALE).astype(BF)
        dqkv_s[cells, D : 2 * D] = (own_heads(dot_tn(scores_low[cells], qkv_s[cells, :D])) * SCALE).astype(BF)
        dqkv_s[cells, 2 * D :] = own_heads(dot_tn(probs_low[cells], grad_context[cells])).astype(BF)

    for m in range(3):
        part_grad = dot_tn(normal_low, dqkv_s[:, D * m : D * (m + 1)])
        att_f32[0, pl.ds(m, 256, stride=3), :] = part_grad[:, :128]
        att_f32[1, pl.ds(m, 256, stride=3), :] = part_grad[:, 128:]

    start_mate(att)
    start_xy(mlp)

    grad_norm_in = dot_nt(dqkv_s[...], wqkv_ref[...])
    grad_in = (grad_res + norm_back(grad_norm_in, normed_one, inv_one, gain_one)).astype(BF)
    u_row, u_col = window_cell(iota((CELLS, CELLS), 1))
    place_main = one_hot((u_col < 28) & (iota((CELLS, CELLS), 0) == 32 * u_row + u_col + 4))
    v_row, v_col = window_cell(iota((32, CELLS), 1))
    place_edge = one_hot((v_col >= 28) & (iota((32, CELLS), 0) == 4 * v_row + v_col - 28))
    back_main[...] = dot(place_main, grad_in).astype(BF)
    back_rd[...] = dot(place_edge, grad_in).astype(BF)

    start_xy(att)
    hear_ring(1)
    spread_ring(2)

    to_below, to_right, to_last = (x_at, below, col), (x_at, row, right), (x_at, below, right)
    back = [
        pltpu.make_async_remote_copy(
            src_ref=src, dst_ref=dst, send_sem=back_ss.at[n], recv_sem=back_rs.at[n],
            device_id=device, device_id_type=MESH,
        )
        for n, (src, dst, device) in enumerate([
            (back_rd.at[pl.ds(16, 16)], got_rd.at[pl.ds(16, 16)], to_last),
            (back_rd.at[pl.ds(0, 16)], got_rd.at[pl.ds(0, 16)], to_right),
            (back_main.at[pl.ds(128, 128)], got_up, to_below),
        ])
    ]
    back[0].start()
    back[1].start()
    pl.when(row_last)(back[2].start)

    first_parts, second_parts = [], []
    for b in (mlp, att):
        for copy in b["p2"]:
            copy.wait_recv()
        total = b["x"][x_at].astype(F32)
        for d in range(NX - 1):
            total = total + b["rx"][d].astype(F32)
        first_parts.append(total.reshape(NZ_LO // 2, NY, b["unit"], 128))
        total = b["y"][y_at].astype(F32)
        for d in range(NY - 1):
            total = total + b["ry"][d].astype(F32)
        second_parts.append(total.reshape(NX, NZ_LO // 2 * b["unit"], 128))
    for y in range(NY):
        x3[y, 0:64, :] = first_parts[0][:, y].reshape(64, 128).astype(BF)
        x3[y, 64:96, :] = first_parts[1][:, y].reshape(32, 128).astype(BF)
    for x in range(NX):
        y3[x, 0:64, :] = second_parts[0][x].astype(BF)
        y3[x, 64:96, :] = second_parts[1][x].astype(BF)
    swaps = []
    for d in (2, 1, 3):
        other = (y_at + d) % NY
        swaps.append(send(x3.at[other], rx3.at[d - 1], late_ss.at[d - 1], late_rs.at[d - 1], at_y(other)))
        other = (x_at + d) % NX
        swaps.append(send(y3.at[other], ry3.at[d - 1], late_ss.at[2 + d], late_rs.at[2 + d], at_x(other)))

    pl.when(jnp.logical_not(row_last))(back[2].start)

    for copy in swaps:
        copy.wait_recv()
    hear_ring(2)
    for part, own, own_at, got in ((0, x3, y_at, rx3), (1, y3, x_at, ry3)):
        total = own[own_at].astype(F32)
        for d in range(NX - 1):
            total = total + got[d].astype(F32)
        for lo in range(NZ_LO // 2):
            for hi in range(NZ_HI):
                at_mlp, at_att = 16 * lo + 8 * hi, 64 + 8 * lo + 4 * hi
                piece = jnp.concatenate(
                    [total[at_mlp : at_mlp + 8], total[at_att : at_att + 4], jnp.zeros((4, 128), F32)], axis=0
                )
                z_send[part * (NZ_LO // 2) + lo, hi] = piece.astype(BF)
    ring = []
    for d in (8, 7, 9, 6, 10, 5, 11, 4, 12, 3, 13, 2, 14, 1, 15):
        other = (z_at + d) % NZ
        ring.append(
            send(
                z_send.at[other % NZ_LO, other // NZ_LO], z_recv.at[d - 1],
                z_ss.at[d - 1], z_rs.at[d - 1], at_z(other),
            )
        )

    for copy in back:
        copy.wait_recv()
    spread = one_hot(iota((128, 16), 0) == 32 * (iota((128, 16), 1) >> 2) + (iota((128, 16), 1) & 3))
    out_ref[0:128, :] = (got_up[...].astype(F32) + dot(spread, got_rd[16:32, :])).astype(BF)
    out_ref[128:256, :] = (back_main[0:128, :].astype(F32) + dot(spread, got_rd[0:16, :])).astype(BF)

    for copy in ring:
        copy.wait_recv()
    total = z_send[z_lo, z_hi].astype(F32)
    for d in range(NZ - 1):
        total = total + z_recv[d].astype(F32)
    for k in range(2):
        c_send[k] = jnp.concatenate(
            [total[4 * k : 4 * k + 4], total[8 + 2 * k : 10 + 2 * k], total[12:14]], axis=0
        )
    last = send(c_send.at[mate], c_recv, late_ss.at[6], late_rs.at[6], at_mate())
    last.wait_recv()
    own, got = c_send[core], c_recv[...]
    first, second = jnp.where(core == 0, own, got), jnp.where(core == 0, got, own)
    apart = jnp.concatenate([first[0:4], second[0:4]], axis=0)
    mixed = jnp.concatenate([part[i : i + 1] for i in range(4) for part in (first, second)], axis=0)
    mlp_ref[...] = jnp.where(x_at < 2, apart, mixed)
    att_ref[...] = jnp.concatenate([first[4:5], second[4:5], first[5:6], second[5:6]], axis=0)

    for copy in halo + back + sends + swaps + ring + [last]:
        copy.wait_send()
    for condition, _, steps in passes:

        @pl.when(condition)
        def _():
            for n, device in steps:
                passing(n, device).wait_send()


def reduce_scratch(unit):
    chip_rows = NZ_LO * NY * unit
    half = chip_rows // 2
    return [
        pltpu.VMEM((2, NX * chip_rows, 128), F32),
        pltpu.VMEM((NX * chip_rows, 128), BF),
        pltpu.VMEM((NX * chip_rows, 128), BF),
        pltpu.VMEM((NX, half, 128), BF),
        pltpu.VMEM((NY, half, 128), BF),
        pltpu.VMEM((NX - 1, half, 128), BF),
        pltpu.VMEM((NY - 1, half, 128), BF),
    ]


def finish_kernel(grad_in, att_in, mlp_in, grad_out, att_out, mlp_out, grad_s, att_s, mlp_s, in_sem, out_sem):
    steps = ((grad_in, grad_s, grad_out), (att_in, att_s, att_out), (mlp_in, mlp_s, mlp_out))
    loads = [pltpu.make_async_copy(src, held, in_sem.at[n]) for n, (src, held, _) in enumerate(steps)]
    stores = [pltpu.make_async_copy(held, dst, out_sem.at[n]) for n, (_, held, dst) in enumerate(steps)]
    for load in loads:
        load.start()
    for load, store in zip(loads, stores):
        load.wait()
        store.start()
    for store in stores:
        store.wait()


def on_device(
    hidden_in, token_ids, embed, norm1_gain, norm2_gain, w_qkv, rel_bias, w_proj, w_up, w_down, out_grad
):
    dma = pltpu.SemaphoreType.DMA
    operands = (
        hidden_in.reshape(CELLS, D),
        token_ids.reshape(8, 32),
        embed,
        norm1_gain.reshape(1, D),
        norm2_gain.reshape(1, D),
        w_qkv,
        rel_bias,
        w_proj,
        w_up,
        w_down,
        out_grad.reshape(CELLS, D),
    )
    chunk = NZ_LO // 2 * (MLP_UNIT + ATT_UNIT)
    grad_out, attention_grads, mlp_grads = pl.pallas_call(
        kernel,
        out_shape=(
            jax.ShapeDtypeStruct((CELLS, D), BF),
            jax.ShapeDtypeStruct((4, 128), F32),
            jax.ShapeDtypeStruct((8, 128), F32),
        ),
        in_specs=[pl.BlockSpec(memory_space=pltpu.HBM)] * len(operands),
        out_specs=[pl.BlockSpec(memory_space=pltpu.VMEM)] * 3,
        scratch_shapes=[pltpu.VMEM(operand.shape, operand.dtype) for operand in operands]
        + [
            pltpu.VMEM((32, D), BF),
            pltpu.VMEM((32, D), BF),
            pltpu.VMEM((2, 128, D), BF),
            pltpu.VMEM((2, 128, D), BF),
            pltpu.VMEM((2, 32, D), BF),
            pltpu.VMEM((2, 32, D), BF),
            pltpu.VMEM((2, 3, 8, 32), jnp.int32),
            pltpu.VMEM((64, 512), F32),
            pltpu.VMEM((CELLS, 512), F32),
            pltpu.VMEM((4, 512, D), BF),
            pltpu.VMEM((4, 512, D), BF),
            pltpu.VMEM((CELLS, 3 * D), BF),
            pltpu.VMEM((CELLS, D), BF),
            pltpu.VMEM((CELLS, 3 * D), BF),
            pltpu.VMEM((CELLS, D), BF),
            pltpu.VMEM((32, D), BF),
            pltpu.VMEM((128, D), BF),
            pltpu.VMEM((32, D), BF),
        ]
        + reduce_scratch(MLP_UNIT)
        + reduce_scratch(ATT_UNIT)
        + [
            pltpu.VMEM((NY, chunk, 128), BF),
            pltpu.VMEM((NX, chunk, 128), BF),
            pltpu.VMEM((NY - 1, chunk, 128), BF),
            pltpu.VMEM((NX - 1, chunk, 128), BF),
            pltpu.VMEM((NZ_LO, NZ_HI, 16, 128), BF),
            pltpu.VMEM((NZ - 1, 16, 128), BF),
            pltpu.VMEM((2, 8, 128), F32),
            pltpu.VMEM((8, 128), F32),
        ]
        + [dma((len(operands),)), dma((9,)), dma((18,)), dma((3,)), dma((3,))]
        + [dma((7,))] * 6
        + [dma((NZ - 1,))] * 2
        + [pltpu.SemaphoreType.REGULAR((3,)), dma((9,)), pltpu.SemaphoreType.REGULAR],
        compiler_params=pltpu.CompilerParams(
            collective_id=0, has_side_effects=True, vmem_limit_bytes=62 * 1024 * 1024
        ),
        name="decoder_block_backward",
    )(*operands)
    results = (grad_out, attention_grads, mlp_grads)
    grad_out, attention_grads, mlp_grads = pl.pallas_call(
        finish_kernel,
        out_shape=tuple(jax.ShapeDtypeStruct(result.shape, result.dtype) for result in results),
        in_specs=[pl.BlockSpec(memory_space=pltpu.HBM)] * 3,
        out_specs=[pl.BlockSpec(memory_space=pltpu.HBM)] * 3,
        scratch_shapes=[pltpu.VMEM(result.shape, result.dtype) for result in results] + [dma((3,)), dma((3,))],
        compiler_params=pltpu.CompilerParams(vmem_limit_bytes=62 * 1024 * 1024),
        name="hand_over_results",
    )(*results)
    return grad_out.reshape(1, 8, 32, D), attention_grads, mlp_grads


def solution(mesh):
    placed = (
        P("dp", "row", "col", None),
        P("dp", "row", "col"),
        P(),
        P(),
        P(),
        P(),
        P(),
        P(),
        P(),
        P(),
        P("dp", "row", "col", None),
    )
    return jax.shard_map(
        on_device,
        mesh=mesh,
        in_specs=placed,
        out_specs=(
            P("dp", "row", "col", None),
            P(("dp", "row", "col"), None),
            P(("dp", "row", "col"), None),
        ),
        check_vma=False,
    )
```

```python
import jax
import jax.numpy as jnp
from jax import lax
from jax.experimental import pallas as pl
from jax.experimental.pallas import tpu as pltpu
from jax.sharding import PartitionSpec as P

D = 256
FF = 1024
HEADS = 8
HEAD_DIM = 32
WIN = 8
PAIRS = 225
CELLS = 256
NORM_EPS = 1e-05
GELU_SCALE = 0.7978845608028654
GELU_CUBIC = 0.044715
SCALE = HEAD_DIM ** (-0.5)

NX, NY, NZ_LO, NZ_HI = 4, 4, 8, 2
NZ = NZ_LO * NZ_HI
ROW_DEVICES, COL_DEVICES = NZ_LO * NY, NZ_HI * 2
MLP_UNIT, ATT_UNIT = 16, 8

MESH = pl.DeviceIdType.MESH
BF = jnp.bfloat16
F32 = jnp.float32


def iota(shape, dim):
    return lax.broadcasted_iota(jnp.int32, shape, dim)


def one_hot(condition):
    return jnp.where(condition, 1.0, 0.0).astype(BF)


def dot(left, right):
    return jnp.dot(left, right, preferred_element_type=F32)


def dot_nt(left, right):
    return lax.dot_general(left, right, (((1,), (1,)), ((), ())), preferred_element_type=F32)


def dot_tn(left, right):
    return lax.dot_general(left, right, (((0,), (0,)), ((), ())), preferred_element_type=F32)


def mean_of(values):
    return jnp.mean(values, axis=-1, keepdims=True)


def layer_norm(values):
    center = values - mean_of(values)
    inv_std = lax.rsqrt(mean_of(center * center) + NORM_EPS)
    return center * inv_std, inv_std


def norm_back(upstream, normed, inv_std, gain):
    scaled = upstream * gain
    return inv_std * (scaled - mean_of(scaled) - normed * mean_of(scaled * normed))


def window_cell(token):
    return token & 7, ((token >> 6) << 3) + ((token >> 3) & 7)


def block_sum(values, ones_pair):
    high = values.astype(BF)
    low = (values - high.astype(F32)).astype(BF)
    parts = []
    for j in range(4):
        lanes = slice(128 * j, 128 * (j + 1))
        parts.append(dot(jnp.concatenate([high[:, lanes], low[:, lanes]], axis=1), ones_pair))
    return jnp.concatenate(parts, axis=1)


def load_rel_bias(rb):
    rb_high = rb.astype(BF)
    rb_rest = rb - rb_high.astype(F32)
    rb_mid = rb_rest.astype(BF)
    rb_low = (rb_rest - rb_mid.astype(F32)).astype(BF)
    parts = jnp.concatenate([rb_high, rb_mid, rb_low], axis=0)
    pair, lane = iota((PAIRS, 2048), 0), iota((PAIRS, 2048), 1)
    offset = lane & 15
    spread = dot(parts, one_hot((offset < 15) & (pair == 15 * (lane >> 7) + offset)))
    spread = spread[0:8] + spread[8:16] + spread[16:24]
    own = iota((8, 2048), 0) == ((iota((8, 2048), 1) >> 4) & 7)
    line = jnp.sum(jnp.where(own, spread, 0.0), axis=0, keepdims=True)
    return jnp.concatenate([line[:, 128 * u : 128 * u + 128] for u in range(16)], axis=0)


def kernel(
    hid_in, tok_in, emb_in, g1_in, g2_in, wqkv_in, rb_in, wproj_in, wup_in, wdown_in, og_in,
    out_ref, att_ref, mlp_ref,
    hid_ref, tok_ref, emb_ref, g1_ref, g2_ref, wqkv_ref, rb_ref, wproj_ref, wup_ref, wdown_ref, og_ref,
    stage_hid, stage_og, halo_hid, halo_og, edge_hid, edge_og, halo_tok,
    bias_s, probs_s, ke_s, ve_s, qkv_s, ctx_s, dqkv_s, back_main, back_rd, got_up, got_rd,
    mlp_f32, mlp_send, mlp_recv, mlp_x, mlp_y, mlp_rx, mlp_ry,
    att_f32, att_send, att_recv, att_x, att_y, att_rx, att_ry,
    x3, y3, rx3, ry3, z_send, z_recv, c_send, c_recv,
    in_sem, halo_ss, halo_rs, back_ss, back_rs, mlp_ss, mlp_rs, att_ss, att_rs, late_ss, late_rs, z_ss, z_rs, ring_sem, pass_ss, go_sem,
):
    x_at, row, col = lax.axis_index("dp"), lax.axis_index("row"), lax.axis_index("col")
    z_lo, y_at = row // NY, row % NY
    z_hi, core = col // 2, col % 2
    z_at = z_hi * NZ_LO + z_lo
    mate = 1 - core

    above = (row + ROW_DEVICES - 1) % ROW_DEVICES
    below = (row + 1) % ROW_DEVICES
    left = (col + COL_DEVICES - 1) % COL_DEVICES
    right = (col + 1) % COL_DEVICES

    def at_mate():
        return (x_at, row, z_hi * 2 + mate)

    def at_x(other):
        return (other, row, col)

    def at_y(other):
        return (x_at, z_lo * NY + other, col)

    def at_z(other):
        return (x_at, (other % NZ_LO) * NY + y_at, (other // NZ_LO) * 2 + core)

    row_first = (1 - (row + ROW_DEVICES - 1) // ROW_DEVICES) * (1 - z_hi)
    col_first = 1 - (col + COL_DEVICES - 1) // COL_DEVICES
    row_last, col_last = row == ROW_DEVICES - 1, col == COL_DEVICES - 1
    row_by_post = jnp.logical_and(row_last, z_hi == 0)
    half_way = ROW_DEVICES // 2
    relay = (x_at, (row + half_way) % ROW_DEVICES, 0)
    is_relay = col == 0
    post = (x_at, half_way + col, 1)
    post_col = row - half_way
    is_post = jnp.logical_and(col == 1, jnp.logical_or(row == half_way, row == half_way + 1))
    is_corner_post = jnp.logical_and(is_post, row % 2 == 1)
    corner_by_post = jnp.logical_and(row_last, col == 0)
    mail_corner = 1 - (1 - col_first) * (1 - row_first * core)
    far_left = (x_at, relay[1], COL_DEVICES - 1)
    far_corner = (x_at, (relay[1] + ROW_DEVICES - 1) % ROW_DEVICES, COL_DEVICES - 1)
    far_above = (x_at, ROW_DEVICES - 1, post_col)
    far_above_left = (x_at, ROW_DEVICES - 1, (post_col + COL_DEVICES - 1) % COL_DEVICES)

    barrier = pltpu.get_barrier_semaphore()

    def enter(*device):
        pl.semaphore_signal(barrier, inc=1, device_id=device, device_id_type=MESH)

    @pl.when(is_relay)
    def _():
        enter(*relay)
        enter(*relay)
        enter(*far_left)
        enter(*far_corner)

    @pl.when(is_post)
    def _():
        enter(x_at, 0, post_col)
        enter(*far_above)

    @pl.when(is_corner_post)
    def _():
        enter(x_at, 0, post_col)
        enter(*far_above_left)

    @pl.when(jnp.logical_not(row_by_post))
    def _():
        enter(x_at, below, col)

    @pl.when(jnp.logical_not(col_last))
    def _():
        enter(x_at, row, right)

    @pl.when(jnp.logical_not(jnp.logical_or(col_last, corner_by_post)))
    def _():
        enter(x_at, below, right)

    near = [at_mate()]
    near += [at_x((x_at + d) % NX) for d in range(1, NX)]
    near += [at_y((y_at + d) % NY) for d in range(1, NY)]
    near += [at_z((z_at + 1) % NZ), at_z((z_at + NZ - 1) % NZ)]
    for partner in near:
        enter(*partner)

    loads = [
        pltpu.make_async_copy(src, dst, in_sem.at[n])
        for n, (src, dst) in enumerate([
            (hid_in, hid_ref), (og_in, og_ref), (tok_in, tok_ref), (rb_in, rb_ref), (emb_in, emb_ref),
            (g1_in, g1_ref), (g2_in, g2_ref), (wqkv_in, wqkv_ref), (wproj_in, wproj_ref),
            (wup_in, wup_ref), (wdown_in, wdown_ref),
        ])
    ]
    for load in loads:
        load.start()

    def spread_ring(n):
        for other in ((z_at + 2**n) % NZ, (z_at + NZ - 2**n) % NZ):
            pl.semaphore_signal(ring_sem.at[n], inc=1, device_id=at_z(other), device_id_type=MESH)

    def hear_ring(n):
        pl.semaphore_wait(ring_sem.at[n], 2)

    def send(src, dst, send_sem, recv_sem, device):
        copy = pltpu.make_async_remote_copy(
            src_ref=src, dst_ref=dst, send_sem=send_sem, recv_sem=recv_sem,
            device_id=device, device_id_type=MESH,
        )
        copy.start()
        return copy

    r32, s256 = iota((32, CELLS), 0), iota((32, CELLS), 1)
    stage_row = jnp.where(r32 < 16, 4, 0) + ((r32 & 15) >> 2)
    pick = one_hot(s256 == stage_row * 32 + (r32 & 3))
    for n in range(3):
        loads[n].wait()
    stage_hid[...] = dot(pick, hid_ref[...]).astype(BF)
    stage_og[...] = dot(pick, og_ref[...]).astype(BF)

    row_end, col_end = (row + 1) // ROW_DEVICES * (1 - z_hi), (col + 1) // COL_DEVICES
    pl.semaphore_wait(barrier, 3 + len(near) + 2 * col_end + row_end + row_end * (1 - core))

    def go(*device):
        pl.semaphore_signal(go_sem, inc=1, device_id=device, device_id_type=MESH)

    @pl.when(col_last)
    def _():
        go(x_at, (row + half_way) % ROW_DEVICES, 0)
        go(x_at, (row + 1 + half_way) % ROW_DEVICES, 0)

    @pl.when(row_by_post)
    def _():
        go(*post)

    @pl.when(corner_by_post)
    def _():
        go(x_at, half_way + right, 1)

    def blend(flag, one, other):
        return tuple(flag * a + (1 - flag) * b for a, b in zip(one, other))

    to_above = blend(row_first, post, (x_at, above, col))
    to_left = blend(col_first, relay, (x_at, row, left))
    to_corner = blend(col_first, relay, blend(row_first * core, post, (x_at, above, left)))
    corner, edge = pl.ds(16, 16), pl.ds(0, 16)
    messages = [
        (stage_hid.at[corner], lambda k: edge_hid.at[k, corner], mail_corner, to_corner),
        (tok_ref, lambda k: halo_tok.at[k, 2], mail_corner, to_corner),
        (stage_hid.at[edge], lambda k: edge_hid.at[k, edge], col_first, to_left),
        (tok_ref, lambda k: halo_tok.at[k, 1], col_first, to_left),
        (hid_ref.at[pl.ds(0, 128)], lambda k: halo_hid.at[k], row_first, to_above),
        (tok_ref, lambda k: halo_tok.at[k, 0], row_first, to_above),
        (stage_og.at[corner], lambda k: edge_og.at[k, corner], mail_corner, to_corner),
        (stage_og.at[edge], lambda k: edge_og.at[k, edge], col_first, to_left),
        (og_ref.at[pl.ds(0, 128)], lambda k: halo_og.at[k], row_first, to_above),
    ]
    halo = [
        send(src, dst(mail), halo_ss.at[n], halo_rs.at[len(messages) * mail + n], device)
        for n, (src, dst, mail, device) in enumerate(messages)
    ]

    def passing(n, device):
        dst = messages[n][1]
        return pltpu.make_async_remote_copy(
            src_ref=dst(1), dst_ref=dst(0), send_sem=pass_ss.at[n], recv_sem=halo_rs.at[n],
            device_id=device, device_id_type=MESH,
        )

    def arrived(n, k):
        dst = messages[n][1]
        pltpu.make_async_remote_copy(
            src_ref=dst(k), dst_ref=dst(k), send_sem=pass_ss.at[n], recv_sem=halo_rs.at[len(messages) * k + n],
            device_id=at_mate(), device_id_type=MESH,
        ).wait_recv()

    passes = [
        (is_relay, 2, [(0, far_corner), (1, far_corner), (2, far_left), (3, far_left), (6, far_corner), (7, far_left)]),
        (is_post, 1 + row % 2, []),
        (is_corner_post, None, [(0, far_above_left), (1, far_above_left)]),
        (is_post, None, [(4, far_above), (5, far_above), (8, far_above)]),
        (is_corner_post, None, [(6, far_above_left)]),
    ]

    spread_ring(0)

    loads[3].wait()
    rb = load_rel_bias(rb_ref[...])
    wide_row, wide_lane = iota((128, 512), 0), iota((128, 512), 1)
    pair_sum = jnp.where(
        (wide_row >> 4) == (wide_lane >> 6), (wide_row & 15) + ((wide_lane >> 3) & 7), -1
    )
    rb_high = rb.astype(BF)
    rb_rest = rb - rb_high.astype(F32)
    rb_mid = rb_rest.astype(BF)
    rb_low = (rb_rest - rb_mid.astype(F32)).astype(BF)
    rb_parts = jnp.concatenate([rb_high, rb_mid, rb_low], axis=0)
    key_row = iota((8, 512), 1) & 7
    for qj in range(8):
        tall = dot(rb_parts, one_hot(pair_sum == qj + 7))
        tall = tall[0:16] + tall[16:32] + tall[32:48]
        rows = jnp.zeros((8, 512), F32)
        for ki in range(8):
            rows = jnp.where(key_row == ki, tall[7 - ki : 15 - ki], rows)
        bias_s[8 * qj : 8 * qj + 8, :] = rows

    t_row, t_col = window_cell(iota((CELLS, CELLS), 0))
    s_lane = iota((CELLS, CELLS), 1)
    pick_main = one_hot((t_col < 28) & (s_lane == 32 * t_row + t_col + 4))
    e_row, e_col = window_cell(iota((CELLS, 32), 0))
    pick_edge = one_hot((e_col >= 28) & (iota((CELLS, 32), 1) == 4 * e_row + e_col - 28))
    for load in loads[4:]:
        load.wait()

    for condition, signals, steps in passes:

        @pl.when(condition)
        def _():
            if signals is not None:
                pl.semaphore_wait(go_sem, signals)
            for n, device in steps:
                arrived(n, 1)
                passing(n, device).start()

    for n in range(6):
        arrived(n, 0)
    tok = tok_ref[...]
    tok_below, tok_right, tok_corner = halo_tok[0, 0], halo_tok[0, 1], halo_tok[0, 2]
    tok_main = jnp.concatenate(
        [tok[4 + i : 5 + i, :] for i in range(4)] + [tok_below[i : i + 1, :] for i in range(4)], axis=1
    )
    tok_edge = jnp.concatenate(
        [tok_right[4 + i : 5 + i, 0:4] for i in range(4)] + [tok_corner[i : i + 1, 0:4] for i in range(4)],
        axis=1,
    )
    tok_main = jnp.broadcast_to(tok_main.astype(F32), (128, CELLS)).astype(BF)
    tok_edge = jnp.broadcast_to(tok_edge.astype(F32), (128, 32)).astype(BF)
    ids = dot_nt(pick_main, tok_main) + dot_nt(pick_edge, tok_edge)
    ids = jnp.concatenate([ids, ids], axis=1)
    emb = emb_ref[...].astype(F32)
    token_part = jnp.where(
        ids < 1.5,
        jnp.where(ids < 0.5, emb[0:1], emb[1:2]),
        jnp.where(ids < 2.5, emb[2:3], emb[3:4]),
    )
    main_hid = jnp.concatenate([hid_ref[128:256, :], halo_hid[0]], axis=0)
    resid_in = dot(pick_main, main_hid) + dot(pick_edge, edge_hid[0]) + token_part
    normed_one, inv_one = layer_norm(resid_in)
    gain_one = g1_ref[...]
    normal_low = (normed_one * gain_one).astype(BF)

    qkv_s[...] = dot(normal_low, wqkv_ref[...]).astype(BF)

    head_mask = one_hot((iota((512, D), 0) >> 6) == (iota((512, D), 1) >> 5))
    ones_pair = one_hot(((iota((256, 128), 0) & 127) >> 6) == (iota((256, 128), 1) >> 6))
    for w in range(4):
        cells = slice(64 * w, 64 * w + 64)
        keys = jnp.concatenate([qkv_s[cells, D : 2 * D]] * HEADS, axis=0) * head_mask
        ke_s[w] = keys
        ve_s[w] = jnp.concatenate([qkv_s[cells, 2 * D :]] * HEADS, axis=0) * head_mask
        probs_s[cells, :] = jnp.exp(dot_nt(qkv_s[cells, :D], keys) * SCALE + bias_s[...])
    raised = probs_s[...]
    probs = raised / block_sum(raised, ones_pair)
    probs_s[...] = probs
    probs_low = probs.astype(BF)
    for w in range(4):
        cells = slice(64 * w, 64 * w + 64)
        ctx_s[cells, :] = dot(probs_low[cells], ve_s[w]).astype(BF)

    context = ctx_s[...]
    resid_mid = resid_in + dot(context, wproj_ref[...])
    normed_two, inv_two = layer_norm(resid_mid)
    gain_two = g2_ref[...]
    mlp_in = (normed_two * gain_two).astype(BF)

    for n in range(6, 9):
        arrived(n, 0)
    main_og = jnp.concatenate([og_ref[128:256, :], halo_og[0]], axis=0)
    grad_f32 = dot(pick_main, main_og) + dot(pick_edge, edge_og[0])
    grad = grad_f32.astype(BF)

    grad_mid = jnp.zeros((CELLS, D), F32)
    for n in range(4):
        units = slice(256 * n, 256 * n + 256)
        pre = dot(mlp_in, wup_ref[:, units])
        grad_act = dot_nt(grad, wdown_ref[units, :])
        square = pre * pre
        tanh_part = jnp.tanh(GELU_SCALE * pre * (1.0 + GELU_CUBIC * square))
        half_plus = 0.5 * (1.0 + tanh_part)
        slope = half_plus + 0.5 * pre * (1.0 - tanh_part * tanh_part) * (
            GELU_SCALE * (1.0 + 3.0 * GELU_CUBIC * square)
        )
        act = (pre * half_plus).astype(BF)
        grad_pre = (grad_act * slope).astype(BF)
        grad_mid = grad_mid + dot_nt(grad_pre, wup_ref[:, units])
        up_grad = dot_tn(mlp_in, grad_pre)
        half, lane_tile = n // 2, 2 * (n % 2)
        mlp_f32[half, pl.ds(lane_tile, 256, stride=4), :] = up_grad[:, :128]
        mlp_f32[half, pl.ds(lane_tile + 1, 256, stride=4), :] = up_grad[:, 128:]
        down_grad = dot_tn(act, grad)
        mlp_f32[0, 1024 + 256 * n : 1280 + 256 * n, :] = down_grad[:, :128]
        mlp_f32[1, 1024 + 256 * n : 1280 + 256 * n, :] = down_grad[:, 128:]

    mlp = dict(
        unit=MLP_UNIT, f32=mlp_f32, send=mlp_send, recv=mlp_recv, x=mlp_x, y=mlp_y, rx=mlp_rx, ry=mlp_ry,
        ss=mlp_ss, rs=mlp_rs,
    )
    att = dict(
        unit=ATT_UNIT, f32=att_f32, send=att_send, recv=att_recv, x=att_x, y=att_y, rx=att_rx, ry=att_ry,
        ss=att_ss, rs=att_rs,
    )
    sends = []

    def start_mate(b):
        b["send"][...] = b["f32"][mate].astype(BF)
        b["p1"] = [send(b["send"], b["recv"], b["ss"].at[0], b["rs"].at[0], at_mate())]
        sends.extend(b["p1"])

    def start_xy(b):
        b["p1"][0].wait_recv()
        unit = b["unit"]
        part = NZ_LO // 2 * NY * unit
        quarter = part // NY
        for x in range(NX):
            first, second = slice(2 * part * x, 2 * part * x + part), slice(2 * part * x + part, 2 * part * (x + 1))
            total = b["f32"][core, first, :] + b["recv"][first, :].astype(F32)
            b["x"][x] = total.astype(BF)
            total = b["f32"][core, second, :] + b["recv"][second, :].astype(F32)
            total = total.reshape(NZ_LO // 2, NY, unit, 128)
            for y in range(NY):
                b["y"][y, quarter * x : quarter * (x + 1), :] = total[:, y].reshape(quarter, 128).astype(BF)
        b["p2"] = []
        for d in (2, 1, 3):
            other = (x_at + d) % NX
            b["p2"].append(
                send(b["x"].at[other], b["rx"].at[d - 1], b["ss"].at[d], b["rs"].at[d], at_x(other))
            )
            other = (y_at + d) % NY
            b["p2"].append(
                send(b["y"].at[other], b["ry"].at[d - 1], b["ss"].at[3 + d], b["rs"].at[3 + d], at_y(other))
            )
        sends.extend(b["p2"])

    start_mate(mlp)
    hear_ring(0)
    spread_ring(1)

    grad_res = grad_f32 + norm_back(grad_mid, normed_two, inv_two, gain_two)
    grad_res_low = grad_res.astype(BF)
    proj_grad = dot_tn(context, grad_res_low)
    att_f32[0, 768:, :] = proj_grad[:, :128]
    att_f32[1, 768:, :] = proj_grad[:, 128:]
    grad_context = dot_nt(grad_res_low, wproj_ref[...]).astype(BF)

    grad_probs = jnp.concatenate(
        [dot_nt(grad_context[64 * w : 64 * w + 64], ve_s[w]) for w in range(4)], axis=0
    )
    probs = probs_s[...]
    grad_scores = probs * (grad_probs - block_sum(probs * grad_probs, ones_pair))
    scores_low = grad_scores.astype(BF)
    probs_low = probs.astype(BF)

    head_of_lane = iota((64, D), 1) >> 5

    def own_heads(stacked):
        result = jnp.zeros((64, D), F32)
        for h in range(HEADS):
            result = jnp.where(head_of_lane == h, stacked[64 * h : 64 * h + 64], result)
        return result

    for w in range(4):
        cells = slice(64 * w, 64 * w + 64)
        dqkv_s[cells, :D] = (dot(scores_low[cells], ke_s[w]) * SCALE).astype(BF)
        dqkv_s[cells, D : 2 * D] = (own_heads(dot_tn(scores_low[cells], qkv_s[cells, :D])) * SCALE).astype(BF)
        dqkv_s[cells, 2 * D :] = own_heads(dot_tn(probs_low[cells], grad_context[cells])).astype(BF)

    start_xy(mlp)
    for m in range(3):
        part_grad = dot_tn(normal_low, dqkv_s[:, D * m : D * (m + 1)])
        att_f32[0, pl.ds(m, 256, stride=3), :] = part_grad[:, :128]
        att_f32[1, pl.ds(m, 256, stride=3), :] = part_grad[:, 128:]

    start_mate(att)

    grad_norm_in = dot_nt(dqkv_s[...], wqkv_ref[...])
    grad_in = (grad_res + norm_back(grad_norm_in, normed_one, inv_one, gain_one)).astype(BF)
    u_row, u_col = window_cell(iota((CELLS, CELLS), 1))
    place_main = one_hot((u_col < 28) & (iota((CELLS, CELLS), 0) == 32 * u_row + u_col + 4))
    v_row, v_col = window_cell(iota((32, CELLS), 1))
    place_edge = one_hot((v_col >= 28) & (iota((32, CELLS), 0) == 4 * v_row + v_col - 28))
    back_main[...] = dot(place_main, grad_in).astype(BF)
    back_rd[...] = dot(place_edge, grad_in).astype(BF)

    start_xy(att)
    hear_ring(1)
    spread_ring(2)

    to_below, to_right, to_last = (x_at, below, col), (x_at, row, right), (x_at, below, right)
    back = [
        pltpu.make_async_remote_copy(
            src_ref=src, dst_ref=dst, send_sem=back_ss.at[n], recv_sem=back_rs.at[n],
            device_id=device, device_id_type=MESH,
        )
        for n, (src, dst, device) in enumerate([
            (back_rd.at[pl.ds(16, 16)], got_rd.at[pl.ds(16, 16)], to_last),
            (back_rd.at[pl.ds(0, 16)], got_rd.at[pl.ds(0, 16)], to_right),
            (back_main.at[pl.ds(128, 128)], got_up, to_below),
        ])
    ]
    back[0].start()
    back[1].start()
    back[2].start()

    first_parts, second_parts = [], []
    for b in (mlp, att):
        for copy in b["p2"]:
            copy.wait_recv()
        total = b["x"][x_at].astype(F32)
        for d in range(NX - 1):
            total = total + b["rx"][d].astype(F32)
        first_parts.append(total.reshape(NZ_LO // 2, NY, b["unit"], 128))
        total = b["y"][y_at].astype(F32)
        for d in range(NY - 1):
            total = total + b["ry"][d].astype(F32)
        second_parts.append(total.reshape(NX, NZ_LO // 2 * b["unit"], 128))
    for y in range(NY):
        x3[y, 0:64, :] = first_parts[0][:, y].reshape(64, 128).astype(BF)
        x3[y, 64:96, :] = first_parts[1][:, y].reshape(32, 128).astype(BF)
    for x in range(NX):
        y3[x, 0:64, :] = second_parts[0][x].astype(BF)
        y3[x, 64:96, :] = second_parts[1][x].astype(BF)
    swaps = []
    for d in (2, 1, 3):
        other = (y_at + d) % NY
        swaps.append(send(x3.at[other], rx3.at[d - 1], late_ss.at[d - 1], late_rs.at[d - 1], at_y(other)))
        other = (x_at + d) % NX
        swaps.append(send(y3.at[other], ry3.at[d - 1], late_ss.at[2 + d], late_rs.at[2 + d], at_x(other)))


    for copy in swaps:
        copy.wait_recv()
    hear_ring(2)
    for part, own, own_at, got in ((0, x3, y_at, rx3), (1, y3, x_at, ry3)):
        total = own[own_at].astype(F32)
        for d in range(NX - 1):
            total = total + got[d].astype(F32)
        for lo in range(NZ_LO // 2):
            for hi in range(NZ_HI):
                at_mlp, at_att = 16 * lo + 8 * hi, 64 + 8 * lo + 4 * hi
                piece = jnp.concatenate(
                    [total[at_mlp : at_mlp + 8], total[at_att : at_att + 4], jnp.zeros((4, 128), F32)], axis=0
                )
                z_send[part * (NZ_LO // 2) + lo, hi] = piece.astype(BF)
    ring = []
    for d in (8, 7, 9, 6, 10, 5, 11, 4, 12, 3, 13, 2, 14, 1, 15):
        other = (z_at + d) % NZ
        ring.append(
            send(
                z_send.at[other % NZ_LO, other // NZ_LO], z_recv.at[d - 1],
                z_ss.at[d - 1], z_rs.at[d - 1], at_z(other),
            )
        )

    for copy in back:
        copy.wait_recv()
    spread = one_hot(iota((128, 16), 0) == 32 * (iota((128, 16), 1) >> 2) + (iota((128, 16), 1) & 3))
    out_ref[0:128, :] = (got_up[...].astype(F32) + dot(spread, got_rd[16:32, :])).astype(BF)
    out_ref[128:256, :] = (back_main[0:128, :].astype(F32) + dot(spread, got_rd[0:16, :])).astype(BF)

    for copy in ring:
        copy.wait_recv()
    total = z_send[z_lo, z_hi].astype(F32)
    for d in range(NZ - 1):
        total = total + z_recv[d].astype(F32)
    for k in range(2):
        c_send[k] = jnp.concatenate(
            [total[4 * k : 4 * k + 4], total[8 + 2 * k : 10 + 2 * k], total[12:14]], axis=0
        )
    last = send(c_send.at[mate], c_recv, late_ss.at[6], late_rs.at[6], at_mate())
    last.wait_recv()
    own, got = c_send[core], c_recv[...]
    first, second = jnp.where(core == 0, own, got), jnp.where(core == 0, got, own)
    apart = jnp.concatenate([first[0:4], second[0:4]], axis=0)
    mixed = jnp.concatenate([part[i : i + 1] for i in range(4) for part in (first, second)], axis=0)
    mlp_ref[...] = jnp.where(x_at < 2, apart, mixed)
    att_ref[...] = jnp.concatenate([first[4:5], second[4:5], first[5:6], second[5:6]], axis=0)

    for copy in halo + back + sends + swaps + ring + [last]:
        copy.wait_send()
    for condition, _, steps in passes:

        @pl.when(condition)
        def _():
            for n, device in steps:
                passing(n, device).wait_send()


def reduce_scratch(unit):
    chip_rows = NZ_LO * NY * unit
    half = chip_rows // 2
    return [
        pltpu.VMEM((2, NX * chip_rows, 128), F32),
        pltpu.VMEM((NX * chip_rows, 128), BF),
        pltpu.VMEM((NX * chip_rows, 128), BF),
        pltpu.VMEM((NX, half, 128), BF),
        pltpu.VMEM((NY, half, 128), BF),
        pltpu.VMEM((NX - 1, half, 128), BF),
        pltpu.VMEM((NY - 1, half, 128), BF),
    ]


def finish_kernel(grad_in, att_in, mlp_in, grad_out, att_out, mlp_out, grad_s, att_s, mlp_s, in_sem, out_sem):
    steps = ((grad_in, grad_s, grad_out), (att_in, att_s, att_out), (mlp_in, mlp_s, mlp_out))
    loads = [pltpu.make_async_copy(src, held, in_sem.at[n]) for n, (src, held, _) in enumerate(steps)]
    stores = [pltpu.make_async_copy(held, dst, out_sem.at[n]) for n, (_, held, dst) in enumerate(steps)]
    for load in loads:
        load.start()
    for load, store in zip(loads, stores):
        load.wait()
        store.start()
    for store in stores:
        store.wait()


def on_device(
    hidden_in, token_ids, embed, norm1_gain, norm2_gain, w_qkv, rel_bias, w_proj, w_up, w_down, out_grad
):
    dma = pltpu.SemaphoreType.DMA
    operands = (
        hidden_in.reshape(CELLS, D),
        token_ids.reshape(8, 32),
        embed,
        norm1_gain.reshape(1, D),
        norm2_gain.reshape(1, D),
        w_qkv,
        rel_bias,
        w_proj,
        w_up,
        w_down,
        out_grad.reshape(CELLS, D),
    )
    chunk = NZ_LO // 2 * (MLP_UNIT + ATT_UNIT)
    grad_out, attention_grads, mlp_grads = pl.pallas_call(
        kernel,
        out_shape=(
            jax.ShapeDtypeStruct((CELLS, D), BF),
            jax.ShapeDtypeStruct((4, 128), F32),
            jax.ShapeDtypeStruct((8, 128), F32),
        ),
        in_specs=[pl.BlockSpec(memory_space=pltpu.HBM)] * len(operands),
        out_specs=[pl.BlockSpec(memory_space=pltpu.VMEM)] * 3,
        scratch_shapes=[pltpu.VMEM(operand.shape, operand.dtype) for operand in operands]
        + [
            pltpu.VMEM((32, D), BF),
            pltpu.VMEM((32, D), BF),
            pltpu.VMEM((2, 128, D), BF),
            pltpu.VMEM((2, 128, D), BF),
            pltpu.VMEM((2, 32, D), BF),
            pltpu.VMEM((2, 32, D), BF),
            pltpu.VMEM((2, 3, 8, 32), jnp.int32),
            pltpu.VMEM((64, 512), F32),
            pltpu.VMEM((CELLS, 512), F32),
            pltpu.VMEM((4, 512, D), BF),
            pltpu.VMEM((4, 512, D), BF),
            pltpu.VMEM((CELLS, 3 * D), BF),
            pltpu.VMEM((CELLS, D), BF),
            pltpu.VMEM((CELLS, 3 * D), BF),
            pltpu.VMEM((CELLS, D), BF),
            pltpu.VMEM((32, D), BF),
            pltpu.VMEM((128, D), BF),
            pltpu.VMEM((32, D), BF),
        ]
        + reduce_scratch(MLP_UNIT)
        + reduce_scratch(ATT_UNIT)
        + [
            pltpu.VMEM((NY, chunk, 128), BF),
            pltpu.VMEM((NX, chunk, 128), BF),
            pltpu.VMEM((NY - 1, chunk, 128), BF),
            pltpu.VMEM((NX - 1, chunk, 128), BF),
            pltpu.VMEM((NZ_LO, NZ_HI, 16, 128), BF),
            pltpu.VMEM((NZ - 1, 16, 128), BF),
            pltpu.VMEM((2, 8, 128), F32),
            pltpu.VMEM((8, 128), F32),
        ]
        + [dma((len(operands),)), dma((9,)), dma((18,)), dma((3,)), dma((3,))]
        + [dma((7,))] * 6
        + [dma((NZ - 1,))] * 2
        + [pltpu.SemaphoreType.REGULAR((3,)), dma((9,)), pltpu.SemaphoreType.REGULAR],
        compiler_params=pltpu.CompilerParams(
            collective_id=0, has_side_effects=True, vmem_limit_bytes=62 * 1024 * 1024
        ),
        name="decoder_block_backward",
    )(*operands)
    results = (grad_out, attention_grads, mlp_grads)
    grad_out, attention_grads, mlp_grads = pl.pallas_call(
        finish_kernel,
        out_shape=tuple(jax.ShapeDtypeStruct(result.shape, result.dtype) for result in results),
        in_specs=[pl.BlockSpec(memory_space=pltpu.HBM)] * 3,
        out_specs=[pl.BlockSpec(memory_space=pltpu.HBM)] * 3,
        scratch_shapes=[pltpu.VMEM(result.shape, result.dtype) for result in results] + [dma((3,)), dma((3,))],
        compiler_params=pltpu.CompilerParams(vmem_limit_bytes=62 * 1024 * 1024),
        name="hand_over_results",
    )(*results)
    return grad_out.reshape(1, 8, 32, D), attention_grads, mlp_grads


def solution(mesh):
    placed = (
        P("dp", "row", "col", None),
        P("dp", "row", "col"),
        P(),
        P(),
        P(),
        P(),
        P(),
        P(),
        P(),
        P(),
        P("dp", "row", "col", None),
    )
    return jax.shard_map(
        on_device,
        mesh=mesh,
        in_specs=placed,
        out_specs=(
            P("dp", "row", "col", None),
            P(("dp", "row", "col"), None),
            P(("dp", "row", "col"), None),
        ),
        check_vma=False,
    )
```

```python
import jax
import jax.numpy as jnp
from jax import lax
from jax.experimental import pallas as pl
from jax.experimental.pallas import tpu as pltpu
from jax.sharding import PartitionSpec as P

D = 256
FF = 1024
HEADS = 8
HEAD_DIM = 32
WIN = 8
PAIRS = 225
CELLS = 256
NORM_EPS = 1e-05
GELU_SCALE = 0.7978845608028654
GELU_CUBIC = 0.044715
SCALE = HEAD_DIM ** (-0.5)

NX, NY, NZ_LO, NZ_HI = 4, 4, 8, 2
NZ = NZ_LO * NZ_HI
ROW_DEVICES, COL_DEVICES = NZ_LO * NY, NZ_HI * 2
MLP_UNIT, ATT_UNIT = 16, 8

MESH = pl.DeviceIdType.MESH
BF = jnp.bfloat16
F32 = jnp.float32


def iota(shape, dim):
    return lax.broadcasted_iota(jnp.int32, shape, dim)


def one_hot(condition):
    return jnp.where(condition, 1.0, 0.0).astype(BF)


def dot(left, right):
    return jnp.dot(left, right, preferred_element_type=F32)


def dot_nt(left, right):
    return lax.dot_general(left, right, (((1,), (1,)), ((), ())), preferred_element_type=F32)


def dot_tn(left, right):
    return lax.dot_general(left, right, (((0,), (0,)), ((), ())), preferred_element_type=F32)


def mean_of(values):
    return jnp.mean(values, axis=-1, keepdims=True)


def layer_norm(values):
    center = values - mean_of(values)
    inv_std = lax.rsqrt(mean_of(center * center) + NORM_EPS)
    return center * inv_std, inv_std


def norm_back(upstream, normed, inv_std, gain):
    scaled = upstream * gain
    return inv_std * (scaled - mean_of(scaled) - normed * mean_of(scaled * normed))


def window_cell(token):
    return token & 7, ((token >> 6) << 3) + ((token >> 3) & 7)


def block_sum(values, ones_pair):
    high = values.astype(BF)
    low = (values - high.astype(F32)).astype(BF)
    parts = []
    for j in range(4):
        lanes = slice(128 * j, 128 * (j + 1))
        parts.append(dot(jnp.concatenate([high[:, lanes], low[:, lanes]], axis=1), ones_pair))
    return jnp.concatenate(parts, axis=1)


def load_rel_bias(rb):
    rb_high = rb.astype(BF)
    rb_rest = rb - rb_high.astype(F32)
    rb_mid = rb_rest.astype(BF)
    rb_low = (rb_rest - rb_mid.astype(F32)).astype(BF)
    parts = jnp.concatenate([rb_high, rb_mid, rb_low], axis=0)
    pair, lane = iota((PAIRS, 2048), 0), iota((PAIRS, 2048), 1)
    offset = lane & 15
    spread = dot(parts, one_hot((offset < 15) & (pair == 15 * (lane >> 7) + offset)))
    spread = spread[0:8] + spread[8:16] + spread[16:24]
    own = iota((8, 2048), 0) == ((iota((8, 2048), 1) >> 4) & 7)
    line = jnp.sum(jnp.where(own, spread, 0.0), axis=0, keepdims=True)
    return jnp.concatenate([line[:, 128 * u : 128 * u + 128] for u in range(16)], axis=0)


def kernel(
    hid_in, tok_in, emb_in, g1_in, g2_in, wqkv_in, rb_in, wproj_in, wup_in, wdown_in, og_in,
    out_ref, att_ref, mlp_ref,
    hid_ref, tok_ref, emb_ref, g1_ref, g2_ref, wqkv_ref, rb_ref, wproj_ref, wup_ref, wdown_ref, og_ref,
    stage_hid, stage_og, halo_hid, halo_og, edge_hid, edge_og, halo_tok,
    bias_s, probs_s, ke_s, ve_s, qkv_s, ctx_s, dqkv_s, back_main, back_rd, got_up, got_rd,
    mlp_f32, mlp_send, mlp_recv, mlp_x, mlp_y, mlp_rx, mlp_ry,
    att_f32, att_send, att_recv, att_x, att_y, att_rx, att_ry,
    x3, y3, rx3, ry3, z_send, z_recv, c_send, c_recv,
    in_sem, halo_ss, halo_rs, back_ss, back_rs, mlp_ss, mlp_rs, att_ss, att_rs, late_ss, late_rs, z_ss, z_rs, ring_sem, pass_ss, go_sem,
    out_s, out_sem,
):
    x_at, row, col = lax.axis_index("dp"), lax.axis_index("row"), lax.axis_index("col")
    z_lo, y_at = row // NY, row % NY
    z_hi, core = col // 2, col % 2
    z_at = z_hi * NZ_LO + z_lo
    mate = 1 - core

    above = (row + ROW_DEVICES - 1) % ROW_DEVICES
    below = (row + 1) % ROW_DEVICES
    left = (col + COL_DEVICES - 1) % COL_DEVICES
    right = (col + 1) % COL_DEVICES

    def at_mate():
        return (x_at, row, z_hi * 2 + mate)

    def at_x(other):
        return (other, row, col)

    def at_y(other):
        return (x_at, z_lo * NY + other, col)

    def at_z(other):
        return (x_at, (other % NZ_LO) * NY + y_at, (other // NZ_LO) * 2 + core)

    row_first = (1 - (row + ROW_DEVICES - 1) // ROW_DEVICES) * (1 - z_hi)
    col_first = 1 - (col + COL_DEVICES - 1) // COL_DEVICES
    row_last, col_last = row == ROW_DEVICES - 1, col == COL_DEVICES - 1
    row_by_post = jnp.logical_and(row_last, z_hi == 0)
    half_way = ROW_DEVICES // 2
    relay = (x_at, (row + half_way) % ROW_DEVICES, 0)
    is_relay = col == 0
    post = (x_at, half_way + col, 1)
    post_col = row - half_way
    is_post = jnp.logical_and(col == 1, jnp.logical_or(row == half_way, row == half_way + 1))
    is_corner_post = jnp.logical_and(is_post, row % 2 == 1)
    corner_by_post = jnp.logical_and(row_last, col == 0)
    mail_corner = 1 - (1 - col_first) * (1 - row_first * core)
    far_left = (x_at, relay[1], COL_DEVICES - 1)
    far_corner = (x_at, (relay[1] + ROW_DEVICES - 1) % ROW_DEVICES, COL_DEVICES - 1)
    far_above = (x_at, ROW_DEVICES - 1, post_col)
    far_above_left = (x_at, ROW_DEVICES - 1, (post_col + COL_DEVICES - 1) % COL_DEVICES)

    barrier = pltpu.get_barrier_semaphore()

    def enter(*device):
        pl.semaphore_signal(barrier, inc=1, device_id=device, device_id_type=MESH)

    @pl.when(is_relay)
    def _():
        enter(*relay)
        enter(*relay)
        enter(*far_left)
        enter(*far_corner)

    @pl.when(is_post)
    def _():
        enter(x_at, 0, post_col)
        enter(*far_above)

    @pl.when(is_corner_post)
    def _():
        enter(x_at, 0, post_col)
        enter(*far_above_left)

    @pl.when(jnp.logical_not(row_by_post))
    def _():
        enter(x_at, below, col)

    @pl.when(jnp.logical_not(col_last))
    def _():
        enter(x_at, row, right)

    @pl.when(jnp.logical_not(jnp.logical_or(col_last, corner_by_post)))
    def _():
        enter(x_at, below, right)

    near = [at_mate()]
    near += [at_x((x_at + d) % NX) for d in (1, NX - 1)]
    near += [at_y((y_at + d) % NY) for d in (1, NY - 1)]
    near += [at_z((z_at + 1) % NZ), at_z((z_at + NZ - 1) % NZ)]
    for partner in near:
        enter(*partner)

    loads = [
        pltpu.make_async_copy(src, dst, in_sem.at[n])
        for n, (src, dst) in enumerate([
            (hid_in, hid_ref), (og_in, og_ref), (tok_in, tok_ref), (rb_in, rb_ref), (emb_in, emb_ref),
            (g1_in, g1_ref), (g2_in, g2_ref), (wqkv_in, wqkv_ref), (wproj_in, wproj_ref),
            (wup_in, wup_ref), (wdown_in, wdown_ref),
        ])
    ]
    for load in loads:
        load.start()

    def spread_ring(n):
        for other in ((z_at + 2**n) % NZ, (z_at + NZ - 2**n) % NZ):
            pl.semaphore_signal(ring_sem.at[n], inc=1, device_id=at_z(other), device_id_type=MESH)

    def spread_plane():
        for other in near[1:5]:
            pl.semaphore_signal(ring_sem.at[3], inc=1, device_id=other, device_id_type=MESH)

    def hear_plane():
        pl.semaphore_wait(ring_sem.at[3], 4)

    def hear_ring(n):
        pl.semaphore_wait(ring_sem.at[n], 2)

    def send(src, dst, send_sem, recv_sem, device):
        copy = pltpu.make_async_remote_copy(
            src_ref=src, dst_ref=dst, send_sem=send_sem, recv_sem=recv_sem,
            device_id=device, device_id_type=MESH,
        )
        copy.start()
        return copy

    r32, s256 = iota((32, CELLS), 0), iota((32, CELLS), 1)
    stage_row = jnp.where(r32 < 16, 4, 0) + ((r32 & 15) >> 2)
    pick = one_hot(s256 == stage_row * 32 + (r32 & 3))
    for n in range(3):
        loads[n].wait()
    stage_hid[...] = dot(pick, hid_ref[...]).astype(BF)
    stage_og[...] = dot(pick, og_ref[...]).astype(BF)

    row_end, col_end = (row + 1) // ROW_DEVICES * (1 - z_hi), (col + 1) // COL_DEVICES
    pl.semaphore_wait(barrier, 3 + len(near) + 2 * col_end + row_end + row_end * (1 - core))

    def go(*device):
        pl.semaphore_signal(go_sem, inc=1, device_id=device, device_id_type=MESH)

    @pl.when(col_last)
    def _():
        go(x_at, (row + half_way) % ROW_DEVICES, 0)
        go(x_at, (row + 1 + half_way) % ROW_DEVICES, 0)

    @pl.when(row_by_post)
    def _():
        go(*post)

    @pl.when(corner_by_post)
    def _():
        go(x_at, half_way + right, 1)

    def blend(flag, one, other):
        return tuple(flag * a + (1 - flag) * b for a, b in zip(one, other))

    to_above = blend(row_first, post, (x_at, above, col))
    to_left = blend(col_first, relay, (x_at, row, left))
    to_corner = blend(col_first, relay, blend(row_first * core, post, (x_at, above, left)))
    corner, edge = pl.ds(16, 16), pl.ds(0, 16)
    messages = [
        (stage_hid.at[corner], lambda k: edge_hid.at[k, corner], mail_corner, to_corner),
        (tok_ref, lambda k: halo_tok.at[k, 2], mail_corner, to_corner),
        (stage_hid.at[edge], lambda k: edge_hid.at[k, edge], col_first, to_left),
        (tok_ref, lambda k: halo_tok.at[k, 1], col_first, to_left),
        (hid_ref.at[pl.ds(0, 128)], lambda k: halo_hid.at[k], row_first, to_above),
        (tok_ref, lambda k: halo_tok.at[k, 0], row_first, to_above),
        (stage_og.at[corner], lambda k: edge_og.at[k, corner], mail_corner, to_corner),
        (stage_og.at[edge], lambda k: edge_og.at[k, edge], col_first, to_left),
        (og_ref.at[pl.ds(0, 128)], lambda k: halo_og.at[k], row_first, to_above),
    ]
    halo = [
        send(src, dst(mail), halo_ss.at[n], halo_rs.at[len(messages) * mail + n], device)
        for n, (src, dst, mail, device) in enumerate(messages)
    ]

    def passing(n, device):
        dst = messages[n][1]
        return pltpu.make_async_remote_copy(
            src_ref=dst(1), dst_ref=dst(0), send_sem=pass_ss.at[n], recv_sem=halo_rs.at[n],
            device_id=device, device_id_type=MESH,
        )

    def arrived(n, k):
        dst = messages[n][1]
        pltpu.make_async_remote_copy(
            src_ref=dst(k), dst_ref=dst(k), send_sem=pass_ss.at[n], recv_sem=halo_rs.at[len(messages) * k + n],
            device_id=at_mate(), device_id_type=MESH,
        ).wait_recv()

    passes = [
        (is_relay, 2, [(0, far_corner), (1, far_corner), (2, far_left), (3, far_left), (6, far_corner), (7, far_left)]),
        (is_post, 1 + row % 2, []),
        (is_corner_post, None, [(0, far_above_left), (1, far_above_left)]),
        (is_post, None, [(4, far_above), (5, far_above), (8, far_above)]),
        (is_corner_post, None, [(6, far_above_left)]),
    ]

    spread_ring(0)
    spread_plane()

    loads[3].wait()
    rb = load_rel_bias(rb_ref[...])
    wide_row, wide_lane = iota((128, 512), 0), iota((128, 512), 1)
    pair_sum = jnp.where(
        (wide_row >> 4) == (wide_lane >> 6), (wide_row & 15) + ((wide_lane >> 3) & 7), -1
    )
    rb_high = rb.astype(BF)
    rb_rest = rb - rb_high.astype(F32)
    rb_mid = rb_rest.astype(BF)
    rb_low = (rb_rest - rb_mid.astype(F32)).astype(BF)
    rb_parts = jnp.concatenate([rb_high, rb_mid, rb_low], axis=0)
    key_row = iota((8, 512), 1) & 7
    for qj in range(8):
        tall = dot(rb_parts, one_hot(pair_sum == qj + 7))
        tall = tall[0:16] + tall[16:32] + tall[32:48]
        rows = jnp.zeros((8, 512), F32)
        for ki in range(8):
            rows = jnp.where(key_row == ki, tall[7 - ki : 15 - ki], rows)
        bias_s[8 * qj : 8 * qj + 8, :] = rows

    t_row, t_col = window_cell(iota((CELLS, CELLS), 0))
    s_lane = iota((CELLS, CELLS), 1)
    pick_main = one_hot((t_col < 28) & (s_lane == 32 * t_row + t_col + 4))
    e_row, e_col = window_cell(iota((CELLS, 32), 0))
    pick_edge = one_hot((e_col >= 28) & (iota((CELLS, 32), 1) == 4 * e_row + e_col - 28))
    for load in loads[4:]:
        load.wait()

    for condition, signals, steps in passes:

        @pl.when(condition)
        def _():
            if signals is not None:
                pl.semaphore_wait(go_sem, signals)
            for n, device in steps:
                arrived(n, 1)
                passing(n, device).start()

    for n in range(6):
        arrived(n, 0)
    tok = tok_ref[...]
    tok_below, tok_right, tok_corner = halo_tok[0, 0], halo_tok[0, 1], halo_tok[0, 2]
    tok_main = jnp.concatenate(
        [tok[4 + i : 5 + i, :] for i in range(4)] + [tok_below[i : i + 1, :] for i in range(4)], axis=1
    )
    tok_edge = jnp.concatenate(
        [tok_right[4 + i : 5 + i, 0:4] for i in range(4)] + [tok_corner[i : i + 1, 0:4] for i in range(4)],
        axis=1,
    )
    tok_main = jnp.broadcast_to(tok_main.astype(F32), (128, CELLS)).astype(BF)
    tok_edge = jnp.broadcast_to(tok_edge.astype(F32), (128, 32)).astype(BF)
    ids = dot_nt(pick_main, tok_main) + dot_nt(pick_edge, tok_edge)
    ids = jnp.concatenate([ids, ids], axis=1)
    emb = emb_ref[...].astype(F32)
    token_part = jnp.where(
        ids < 1.5,
        jnp.where(ids < 0.5, emb[0:1], emb[1:2]),
        jnp.where(ids < 2.5, emb[2:3], emb[3:4]),
    )
    main_hid = jnp.concatenate([hid_ref[128:256, :], halo_hid[0]], axis=0)
    resid_in = dot(pick_main, main_hid) + dot(pick_edge, edge_hid[0]) + token_part
    normed_one, inv_one = layer_norm(resid_in)
    gain_one = g1_ref[...]
    normal_low = (normed_one * gain_one).astype(BF)

    qkv_s[...] = dot(normal_low, wqkv_ref[...]).astype(BF)

    head_mask = one_hot((iota((512, D), 0) >> 6) == (iota((512, D), 1) >> 5))
    ones_pair = one_hot(((iota((256, 128), 0) & 127) >> 6) == (iota((256, 128), 1) >> 6))
    for w in range(4):
        cells = slice(64 * w, 64 * w + 64)
        keys = jnp.concatenate([qkv_s[cells, D : 2 * D]] * HEADS, axis=0) * head_mask
        ke_s[w] = keys
        ve_s[w] = jnp.concatenate([qkv_s[cells, 2 * D :]] * HEADS, axis=0) * head_mask
        probs_s[cells, :] = jnp.exp(dot_nt(qkv_s[cells, :D], keys) * SCALE + bias_s[...])
    raised = probs_s[...]
    probs = raised / block_sum(raised, ones_pair)
    probs_s[...] = probs
    probs_low = probs.astype(BF)
    for w in range(4):
        cells = slice(64 * w, 64 * w + 64)
        ctx_s[cells, :] = dot(probs_low[cells], ve_s[w]).astype(BF)

    context = ctx_s[...]
    resid_mid = resid_in + dot(context, wproj_ref[...])
    normed_two, inv_two = layer_norm(resid_mid)
    gain_two = g2_ref[...]
    mlp_in = (normed_two * gain_two).astype(BF)

    for n in range(6, 9):
        arrived(n, 0)
    main_og = jnp.concatenate([og_ref[128:256, :], halo_og[0]], axis=0)
    grad_f32 = dot(pick_main, main_og) + dot(pick_edge, edge_og[0])
    grad = grad_f32.astype(BF)

    grad_mid = jnp.zeros((CELLS, D), F32)
    for n in range(4):
        units = slice(256 * n, 256 * n + 256)
        pre = dot(mlp_in, wup_ref[:, units])
        grad_act = dot_nt(grad, wdown_ref[units, :])
        square = pre * pre
        tanh_part = jnp.tanh(GELU_SCALE * pre * (1.0 + GELU_CUBIC * square))
        half_plus = 0.5 * (1.0 + tanh_part)
        slope = half_plus + 0.5 * pre * (1.0 - tanh_part * tanh_part) * (
            GELU_SCALE * (1.0 + 3.0 * GELU_CUBIC * square)
        )
        act = (pre * half_plus).astype(BF)
        grad_pre = (grad_act * slope).astype(BF)
        grad_mid = grad_mid + dot_nt(grad_pre, wup_ref[:, units])
        up_grad = dot_tn(mlp_in, grad_pre)
        half, lane_tile = n // 2, 2 * (n % 2)
        mlp_f32[half, pl.ds(lane_tile, 256, stride=4), :] = up_grad[:, :128]
        mlp_f32[half, pl.ds(lane_tile + 1, 256, stride=4), :] = up_grad[:, 128:]
        down_grad = dot_tn(act, grad)
        mlp_f32[0, 1024 + 256 * n : 1280 + 256 * n, :] = down_grad[:, :128]
        mlp_f32[1, 1024 + 256 * n : 1280 + 256 * n, :] = down_grad[:, 128:]

    mlp = dict(
        unit=MLP_UNIT, f32=mlp_f32, send=mlp_send, recv=mlp_recv, x=mlp_x, y=mlp_y, rx=mlp_rx, ry=mlp_ry,
        ss=mlp_ss, rs=mlp_rs,
    )
    att = dict(
        unit=ATT_UNIT, f32=att_f32, send=att_send, recv=att_recv, x=att_x, y=att_y, rx=att_rx, ry=att_ry,
        ss=att_ss, rs=att_rs,
    )
    sends = []

    def start_mate(b):
        b["send"][...] = b["f32"][mate].astype(BF)
        b["p1"] = [send(b["send"], b["recv"], b["ss"].at[0], b["rs"].at[0], at_mate())]
        sends.extend(b["p1"])

    def start_xy(b):
        b["p1"][0].wait_recv()
        unit = b["unit"]
        part = NZ_LO // 2 * NY * unit
        quarter = part // NY
        for x in range(NX):
            first, second = slice(2 * part * x, 2 * part * x + part), slice(2 * part * x + part, 2 * part * (x + 1))
            total = b["f32"][core, first, :] + b["recv"][first, :].astype(F32)
            b["x"][x] = total.astype(BF)
            total = b["f32"][core, second, :] + b["recv"][second, :].astype(F32)
            total = total.reshape(NZ_LO // 2, NY, unit, 128)
            for y in range(NY):
                b["y"][y, quarter * x : quarter * (x + 1), :] = total[:, y].reshape(quarter, 128).astype(BF)
        b["p2"] = []
        for d in (2, 1, 3):
            other = (x_at + d) % NX
            b["p2"].append(
                send(b["x"].at[other], b["rx"].at[d - 1], b["ss"].at[d], b["rs"].at[d], at_x(other))
            )
            other = (y_at + d) % NY
            b["p2"].append(
                send(b["y"].at[other], b["ry"].at[d - 1], b["ss"].at[3 + d], b["rs"].at[3 + d], at_y(other))
            )
        sends.extend(b["p2"])

    start_mate(mlp)
    hear_ring(0)
    spread_ring(1)

    grad_res = grad_f32 + norm_back(grad_mid, normed_two, inv_two, gain_two)
    grad_res_low = grad_res.astype(BF)
    proj_grad = dot_tn(context, grad_res_low)
    att_f32[0, 768:, :] = proj_grad[:, :128]
    att_f32[1, 768:, :] = proj_grad[:, 128:]
    grad_context = dot_nt(grad_res_low, wproj_ref[...]).astype(BF)

    grad_probs = jnp.concatenate(
        [dot_nt(grad_context[64 * w : 64 * w + 64], ve_s[w]) for w in range(4)], axis=0
    )
    probs = probs_s[...]
    grad_scores = probs * (grad_probs - block_sum(probs * grad_probs, ones_pair))
    scores_low = grad_scores.astype(BF)
    probs_low = probs.astype(BF)

    head_of_lane = iota((64, D), 1) >> 5

    def own_heads(stacked):
        result = jnp.zeros((64, D), F32)
        for h in range(HEADS):
            result = jnp.where(head_of_lane == h, stacked[64 * h : 64 * h + 64], result)
        return result

    for w in range(4):
        cells = slice(64 * w, 64 * w + 64)
        dqkv_s[cells, :D] = (dot(scores_low[cells], ke_s[w]) * SCALE).astype(BF)
        dqkv_s[cells, D : 2 * D] = (own_heads(dot_tn(scores_low[cells], qkv_s[cells, :D])) * SCALE).astype(BF)
        dqkv_s[cells, 2 * D :] = own_heads(dot_tn(probs_low[cells], grad_context[cells])).astype(BF)

    hear_plane()
    start_xy(mlp)
    for m in range(3):
        part_grad = dot_tn(normal_low, dqkv_s[:, D * m : D * (m + 1)])
        att_f32[0, pl.ds(m, 256, stride=3), :] = part_grad[:, :128]
        att_f32[1, pl.ds(m, 256, stride=3), :] = part_grad[:, 128:]

    start_mate(att)

    grad_norm_in = dot_nt(dqkv_s[...], wqkv_ref[...])
    grad_in = (grad_res + norm_back(grad_norm_in, normed_one, inv_one, gain_one)).astype(BF)
    u_row, u_col = window_cell(iota((CELLS, CELLS), 1))
    place_main = one_hot((u_col < 28) & (iota((CELLS, CELLS), 0) == 32 * u_row + u_col + 4))
    v_row, v_col = window_cell(iota((32, CELLS), 1))
    place_edge = one_hot((v_col >= 28) & (iota((32, CELLS), 0) == 4 * v_row + v_col - 28))
    back_main[...] = dot(place_main, grad_in).astype(BF)
    back_rd[...] = dot(place_edge, grad_in).astype(BF)

    start_xy(att)
    hear_ring(1)
    spread_ring(2)

    to_below, to_right, to_last = (x_at, below, col), (x_at, row, right), (x_at, below, right)
    back = [
        pltpu.make_async_remote_copy(
            src_ref=src, dst_ref=dst, send_sem=back_ss.at[n], recv_sem=back_rs.at[n],
            device_id=device, device_id_type=MESH,
        )
        for n, (src, dst, device) in enumerate([
            (back_rd.at[pl.ds(16, 16)], got_rd.at[pl.ds(16, 16)], to_last),
            (back_rd.at[pl.ds(0, 16)], got_rd.at[pl.ds(0, 16)], to_right),
            (back_main.at[pl.ds(128, 128)], got_up, to_below),
        ])
    ]
    back[0].start()
    back[1].start()
    back[2].start()

    first_parts, second_parts = [], []
    for b in (mlp, att):
        for copy in b["p2"]:
            copy.wait_recv()
        total = b["x"][x_at].astype(F32)
        for d in range(NX - 1):
            total = total + b["rx"][d].astype(F32)
        first_parts.append(total.reshape(NZ_LO // 2, NY, b["unit"], 128))
        total = b["y"][y_at].astype(F32)
        for d in range(NY - 1):
            total = total + b["ry"][d].astype(F32)
        second_parts.append(total.reshape(NX, NZ_LO // 2 * b["unit"], 128))
    for y in range(NY):
        x3[y, 0:64, :] = first_parts[0][:, y].reshape(64, 128).astype(BF)
        x3[y, 64:96, :] = first_parts[1][:, y].reshape(32, 128).astype(BF)
    for x in range(NX):
        y3[x, 0:64, :] = second_parts[0][x].astype(BF)
        y3[x, 64:96, :] = second_parts[1][x].astype(BF)
    swaps = []
    for d in (2, 1, 3):
        other = (y_at + d) % NY
        swaps.append(send(x3.at[other], rx3.at[d - 1], late_ss.at[d - 1], late_rs.at[d - 1], at_y(other)))
        other = (x_at + d) % NX
        swaps.append(send(y3.at[other], ry3.at[d - 1], late_ss.at[2 + d], late_rs.at[2 + d], at_x(other)))


    for copy in swaps:
        copy.wait_recv()
    hear_ring(2)
    for part, own, own_at, got in ((0, x3, y_at, rx3), (1, y3, x_at, ry3)):
        total = own[own_at].astype(F32)
        for d in range(NX - 1):
            total = total + got[d].astype(F32)
        for lo in range(NZ_LO // 2):
            for hi in range(NZ_HI):
                at_mlp, at_att = 16 * lo + 8 * hi, 64 + 8 * lo + 4 * hi
                piece = jnp.concatenate(
                    [total[at_mlp : at_mlp + 8], total[at_att : at_att + 4], jnp.zeros((4, 128), F32)], axis=0
                )
                z_send[part * (NZ_LO // 2) + lo, hi] = piece.astype(BF)
    ring = []
    for d in (8, 7, 9, 6, 10, 5, 11, 4, 12, 3, 13, 2, 14, 1, 15):
        other = (z_at + d) % NZ
        ring.append(
            send(
                z_send.at[other % NZ_LO, other // NZ_LO], z_recv.at[d - 1],
                z_ss.at[d - 1], z_rs.at[d - 1], at_z(other),
            )
        )

    for copy in back:
        copy.wait_recv()
    spread = one_hot(iota((128, 16), 0) == 32 * (iota((128, 16), 1) >> 2) + (iota((128, 16), 1) & 3))
    out_s[0:128, :] = (got_up[...].astype(F32) + dot(spread, got_rd[16:32, :])).astype(BF)
    out_s[128:256, :] = (back_main[0:128, :].astype(F32) + dot(spread, got_rd[0:16, :])).astype(BF)
    out_copy = pltpu.make_async_copy(out_s, out_ref, out_sem)
    out_copy.start()

    for copy in ring:
        copy.wait_recv()
    total = z_send[z_lo, z_hi].astype(F32)
    for d in range(NZ - 1):
        total = total + z_recv[d].astype(F32)
    for k in range(2):
        c_send[k] = jnp.concatenate(
            [total[4 * k : 4 * k + 4], total[8 + 2 * k : 10 + 2 * k], total[12:14]], axis=0
        )
    last = send(c_send.at[mate], c_recv, late_ss.at[6], late_rs.at[6], at_mate())
    last.wait_recv()
    own, got = c_send[core], c_recv[...]
    first, second = jnp.where(core == 0, own, got), jnp.where(core == 0, got, own)
    apart = jnp.concatenate([first[0:4], second[0:4]], axis=0)
    mixed = jnp.concatenate([part[i : i + 1] for i in range(4) for part in (first, second)], axis=0)
    mlp_ref[...] = jnp.where(x_at < 2, apart, mixed)
    att_ref[...] = jnp.concatenate([first[4:5], second[4:5], first[5:6], second[5:6]], axis=0)

    out_copy.wait()
    for copy in halo + back + sends + swaps + ring + [last]:
        copy.wait_send()
    for condition, _, steps in passes:

        @pl.when(condition)
        def _():
            for n, device in steps:
                passing(n, device).wait_send()


def reduce_scratch(unit):
    chip_rows = NZ_LO * NY * unit
    half = chip_rows // 2
    return [
        pltpu.VMEM((2, NX * chip_rows, 128), F32),
        pltpu.VMEM((NX * chip_rows, 128), BF),
        pltpu.VMEM((NX * chip_rows, 128), BF),
        pltpu.VMEM((NX, half, 128), BF),
        pltpu.VMEM((NY, half, 128), BF),
        pltpu.VMEM((NX - 1, half, 128), BF),
        pltpu.VMEM((NY - 1, half, 128), BF),
    ]


def finish_kernel(grad_in, att_in, mlp_in, grad_out, att_out, mlp_out, grad_s, att_s, mlp_s, in_sem, out_sem):
    steps = ((grad_in, grad_s, grad_out), (att_in, att_s, att_out), (mlp_in, mlp_s, mlp_out))
    loads = [pltpu.make_async_copy(src, held, in_sem.at[n]) for n, (src, held, _) in enumerate(steps)]
    stores = [pltpu.make_async_copy(held, dst, out_sem.at[n]) for n, (_, held, dst) in enumerate(steps)]
    for load in loads:
        load.start()
    for load, store in zip(loads, stores):
        load.wait()
        store.start()
    for store in stores:
        store.wait()


def on_device(
    hidden_in, token_ids, embed, norm1_gain, norm2_gain, w_qkv, rel_bias, w_proj, w_up, w_down, out_grad
):
    dma = pltpu.SemaphoreType.DMA
    operands = (
        hidden_in.reshape(CELLS, D),
        token_ids.reshape(8, 32),
        embed,
        norm1_gain.reshape(1, D),
        norm2_gain.reshape(1, D),
        w_qkv,
        rel_bias,
        w_proj,
        w_up,
        w_down,
        out_grad.reshape(CELLS, D),
    )
    chunk = NZ_LO // 2 * (MLP_UNIT + ATT_UNIT)
    grad_out, attention_grads, mlp_grads = pl.pallas_call(
        kernel,
        out_shape=(
            jax.ShapeDtypeStruct((CELLS, D), BF),
            jax.ShapeDtypeStruct((4, 128), F32),
            jax.ShapeDtypeStruct((8, 128), F32),
        ),
        in_specs=[pl.BlockSpec(memory_space=pltpu.HBM)] * len(operands),
        out_specs=[pl.BlockSpec(memory_space=pltpu.HBM)] + [pl.BlockSpec(memory_space=pltpu.VMEM)] * 2,
        scratch_shapes=[pltpu.VMEM(operand.shape, operand.dtype) for operand in operands]
        + [
            pltpu.VMEM((32, D), BF),
            pltpu.VMEM((32, D), BF),
            pltpu.VMEM((2, 128, D), BF),
            pltpu.VMEM((2, 128, D), BF),
            pltpu.VMEM((2, 32, D), BF),
            pltpu.VMEM((2, 32, D), BF),
            pltpu.VMEM((2, 3, 8, 32), jnp.int32),
            pltpu.VMEM((64, 512), F32),
            pltpu.VMEM((CELLS, 512), F32),
            pltpu.VMEM((4, 512, D), BF),
            pltpu.VMEM((4, 512, D), BF),
            pltpu.VMEM((CELLS, 3 * D), BF),
            pltpu.VMEM((CELLS, D), BF),
            pltpu.VMEM((CELLS, 3 * D), BF),
            pltpu.VMEM((CELLS, D), BF),
            pltpu.VMEM((32, D), BF),
            pltpu.VMEM((128, D), BF),
            pltpu.VMEM((32, D), BF),
        ]
        + reduce_scratch(MLP_UNIT)
        + reduce_scratch(ATT_UNIT)
        + [
            pltpu.VMEM((NY, chunk, 128), BF),
            pltpu.VMEM((NX, chunk, 128), BF),
            pltpu.VMEM((NY - 1, chunk, 128), BF),
            pltpu.VMEM((NX - 1, chunk, 128), BF),
            pltpu.VMEM((NZ_LO, NZ_HI, 16, 128), BF),
            pltpu.VMEM((NZ - 1, 16, 128), BF),
            pltpu.VMEM((2, 8, 128), F32),
            pltpu.VMEM((8, 128), F32),
        ]
        + [dma((len(operands),)), dma((9,)), dma((18,)), dma((3,)), dma((3,))]
        + [dma((7,))] * 6
        + [dma((NZ - 1,))] * 2
        + [pltpu.SemaphoreType.REGULAR((4,)), dma((9,)), pltpu.SemaphoreType.REGULAR]
        + [pltpu.VMEM((CELLS, D), BF), dma],
        compiler_params=pltpu.CompilerParams(
            collective_id=0, has_side_effects=True, vmem_limit_bytes=62 * 1024 * 1024
        ),
        name="decoder_block_backward",
    )(*operands)
    results = (grad_out, attention_grads, mlp_grads)
    grad_out, attention_grads, mlp_grads = pl.pallas_call(
        finish_kernel,
        out_shape=tuple(jax.ShapeDtypeStruct(result.shape, result.dtype) for result in results),
        in_specs=[pl.BlockSpec(memory_space=pltpu.HBM)] * 3,
        out_specs=[pl.BlockSpec(memory_space=pltpu.HBM)] * 3,
        scratch_shapes=[pltpu.VMEM(result.shape, result.dtype) for result in results] + [dma((3,)), dma((3,))],
        compiler_params=pltpu.CompilerParams(vmem_limit_bytes=62 * 1024 * 1024),
        name="hand_over_results",
    )(*results)
    return grad_out.reshape(1, 8, 32, D), attention_grads, mlp_grads


def solution(mesh):
    placed = (
        P("dp", "row", "col", None),
        P("dp", "row", "col"),
        P(),
        P(),
        P(),
        P(),
        P(),
        P(),
        P(),
        P(),
        P("dp", "row", "col", None),
    )
    return jax.shard_map(
        on_device,
        mesh=mesh,
        in_specs=placed,
        out_specs=(
            P("dp", "row", "col", None),
            P(("dp", "row", "col"), None),
            P(("dp", "row", "col"), None),
        ),
        check_vma=False,
    )
```
